128 devices in a mesh: dp: 32 (over z_lo, x, y), expert: 4 (over z_hi, core).
Axes of the slice: x: 4, y: 4, z: 4 (z_hi: 2, z_lo: 2; z = z_hi * 2 + z_lo), core: 2. Of those that a mesh axis runs over, the one named last changes fastest.
Arguments:
- tokens: bfloat16 [16384, 4096], P(('dp', 'expert')), may hold values from -24 to 24
- cotangent: bfloat16 [16384, 4096], P(('dp', 'expert')), may hold values from -0.59765625 to 0.59765625
- routes: int32 [16384, 8], P(('dp', 'expert')), may hold values from 0 to 127, as said below
- route_gates: float32 [16384, 8], P(('dp', 'expert')), may hold values from 0.05 to 0.4
- gate_up: bfloat16 [4, 4096, 1536], P('expert'), may hold values from -0.09375 to 0.09375
- down_proj: bfloat16 [4, 768, 4096], P('expert'), may hold values from -0.21875 to 0.21875
Outputs:
- token_grad: bfloat16 [16384, 4096], P(('dp', 'expert'))
- gate_up_grad: bfloat16 [4, 4096, 1536], P('expert', 'dp')
- down_grad: bfloat16 [4, 768, 4096], P('expert', 'dp')
The draws below stay inside these ranges and needn't reach their ends.
Inputs may be any that keep to these rules, and one draw needn't show every extreme that they name: A row of routes names 8 different ids. In the tokens of one device (aligned blocks of 128 rows) each expert e < 4 is named by at most 48 rows. In every draw some expert is named by exactly 48 rows in every block of one data group of 4 blocks.
All inputs are finite; a program needn't handle non-finite values.
Results may differ from the reference program's by a relative error of at most 0.006.
Values may be sent and summed in bfloat16 or wider, within the bound.
No kernel may reach another device: no remote copies, remote signals or barrier semaphores. Data moves between devices by JAX's collectives and lax.ppermute only.
A program may use at most 192 MiB of HBM per device.

```python
from functools import partial
import jax
import jax.numpy as jnp
from jax import lax

D = 4096
E_ALL = 128
TOP = 8
FF = 768
TOK_DEV = 128
CAP = 48
EXPERTS = 4
TOKENS = 16384
N_DP = 32
N_EXPERT = 4


def draw_routes(key, part):
    key = jax.random.fold_in(key, 7)
    subkeys = jax.random.split(key, 6)
    blocks = N_DP * N_EXPERT
    levels = jax.random.randint(subkeys[0], (1, EXPERTS), 1, 5)
    lowest = CAP * levels // 8
    highest = CAP * levels // 4 + 1
    counts = jax.random.randint(subkeys[1], (blocks, EXPERTS), lowest, highest)
    counts = jnp.minimum(counts, CAP)
    busy_group = jax.random.randint(subkeys[2], (), 0, N_DP)
    busy_expert = jax.random.randint(subkeys[3], (), 0, EXPERTS)
    in_group = jnp.arange(blocks) // N_EXPERT == busy_group
    chosen = in_group[:, None] & (jnp.arange(EXPERTS) == busy_expert)[None, :]
    counts = jnp.where(chosen, CAP, counts)
    scores = jax.random.randint(subkeys[4], (blocks, EXPERTS, TOK_DEV), 0, 2 ** 16) * TOK_DEV + jnp.arange(TOK_DEV, dtype=jnp.int32)
    ranking = jnp.argsort(jnp.argsort(scores, axis=2), axis=2)
    member = ranking < counts[:, :, None]
    window_ids = jnp.arange(EXPERTS, dtype=jnp.int32)[None, :, None]
    inside = jnp.where(member, 2 ** 29 + window_ids, -1 - window_ids)
    inside = jnp.transpose(inside, (0, 2, 1))
    outside = jax.random.randint(subkeys[5], (blocks, TOK_DEV, E_ALL - EXPERTS), 0, 2 ** 20) * E_ALL + jnp.arange(E_ALL - EXPERTS, dtype=jnp.int32)
    joined = jnp.concatenate([inside, outside], axis=2)
    top_scores, picked = lax.top_k(joined, TOP)
    return picked.astype(jnp.int32).reshape(blocks * TOK_DEV, TOP)


def spiked(array, own_key, source, target, shards_of, factor):
    owner, partner = [(jnp.arange(array.shape[axis_at]) // (array.shape[axis_at] // shards_of)).reshape([-1 if axis == axis_at else 1 for axis in range(array.ndim)]) for axis_at in (source, target)]
    chosen = jax.random.permutation(own_key, shards_of)[partner]
    strong = (owner == chosen) | (owner == (partner + shards_of // 2) % shards_of)
    return jnp.where(strong, factor * array, array)


def steps_of(key, shape, shards, low, top_value):
    factor_of = 1.0
    for axis_at, shards_of in shards:
        draws = jax.random.uniform(jax.random.fold_in(jax.random.fold_in(key, 6), axis_at), (shards_of,), jnp.float32, low / len(shards), top_value / len(shards))
        factor_of = factor_of * jnp.repeat(jnp.exp(draws), shape[axis_at] // shards_of).reshape((-1,) + (1,) * (len(shape) - 1 - axis_at))
    return factor_of


def centred(key, dims, spread, most, cuts=(), kind=jnp.bfloat16):
    factor_of = steps_of(key, dims, cuts, -0.22, 0.18) if cuts else 1.0
    values = jax.random.normal(key, dims, jnp.float32) * spread * factor_of
    return jnp.minimum(jnp.maximum(values, -most), most).astype(kind)


def heavy_noise(stream_key, shape, scale, bound, cuts, heavy, kind=jnp.bfloat16):
    entries = scale * jax.random.normal(stream_key, shape, jnp.float32)
    if cuts:
        entries = entries * steps_of(stream_key, shape, cuts, -0.22, 0.18)
    return jnp.clip(spiked(entries, jax.random.fold_in(stream_key, 3), *heavy), -bound, bound).astype(kind)


def setup_inputs(seed: int = 0) -> dict:
    seeds = jax.random.split(jax.random.key(seed), 7)
    return {
        "tokens": heavy_noise(seeds[0], (TOKENS, D), 1.0, 24.0, ((0, 128),), (0, 1, 128, 5.5)),
        "cotangent": centred(seeds[1], (TOKENS, D), 0.1, 0.59765625, ((0, 128),)),
        "routes": draw_routes(jax.random.fold_in(seeds[6], 71), 0),
        "route_gates": jnp.clip(0.05 + 0.35 * jax.random.uniform(seeds[3], (TOKENS, TOP), jnp.float32) ** steps_of(seeds[3], (TOKENS, TOP), ((0, 128),), -0.2, 0.2), 0.05, 0.4),
        "gate_up": centred(seeds[4], (EXPERTS, D, 2 * FF), D ** -0.5, 0.09375, ((0, 4),)),
        "down_proj": centred(seeds[5], (EXPERTS, FF, D), FF ** -0.5, 0.21875, ((0, 4),)),
    }


def route_tables(route_rows, gate_rows, experts, capacity):
    matches = route_rows[:, :, None] == jnp.arange(experts, dtype=jnp.int32)[None, None, :]
    member = jnp.any(matches, axis=1)
    weight = jnp.sum(jnp.where(matches, gate_rows[:, :, None], jnp.float32(0.0)), axis=1).astype(jnp.float32)
    position = jnp.cumsum(member.astype(jnp.int32), axis=0) - 1
    select = member[:, :, None] & (position[:, :, None] == jnp.arange(capacity, dtype=jnp.int32)[None, None, :])
    return select, weight


def expert_math(expert_rows, scaled, gate_up, down_proj):
    inner = down_proj.shape[0]
    activation = jnp.dot(expert_rows, gate_up, preferred_element_type=jnp.float32)
    gate_part = activation[:, :inner]
    up_part = activation[:, inner:]
    gate_sig = jax.nn.sigmoid(gate_part)
    silu_val = gate_part * gate_sig
    hidden = (silu_val * up_part).astype(jnp.bfloat16)
    grad_hidden = lax.dot_general(scaled, down_proj, (((1,), (1,)), ((), ())), preferred_element_type=jnp.float32)
    grad_gate = grad_hidden * up_part * (gate_sig * (1.0 + gate_part * (1.0 - gate_sig)))
    grad_upper = grad_hidden * silu_val
    grad_act = jnp.concatenate([grad_gate, grad_upper], axis=1).astype(jnp.bfloat16)
    token_back = lax.dot_general(grad_act, gate_up, (((1,), (1,)), ((), ())), preferred_element_type=jnp.float32).astype(jnp.bfloat16)
    return hidden, grad_act, token_back


def reference(tokens, cotangent, routes, route_gates, gate_up, down_proj):
    group_rows = TOK_DEV * N_EXPERT
    tables = jax.vmap(partial(route_tables, experts=EXPERTS, capacity=CAP))
    maximal_precision = lax.Precision.HIGHEST

    def one_group(totals, group_id):
        offset = (group_id * group_rows).astype(jnp.int32)
        block_input_rows = lax.dynamic_slice_in_dim(tokens, offset, group_rows, 0).reshape(N_EXPERT, TOK_DEV, D)
        block_output_gradient = lax.dynamic_slice_in_dim(cotangent, offset, group_rows, 0).reshape(N_EXPERT, TOK_DEV, D)
        block_routes = lax.dynamic_slice_in_dim(routes, offset, group_rows, 0).reshape(N_EXPERT, TOK_DEV, TOP)
        block_gates = lax.dynamic_slice_in_dim(route_gates, offset, group_rows, 0).reshape(N_EXPERT, TOK_DEV, TOP)
        select, weight = tables(block_routes, block_gates)
        choosing_mask = select.astype(jnp.float32).reshape(N_EXPERT, TOK_DEV, EXPERTS * CAP)
        position_gate = jnp.sum(jnp.where(select, weight[:, :, :, None], jnp.float32(0.0)), axis=1).reshape(N_EXPERT, EXPERTS * CAP, 1)
        position_rows = jnp.einsum("vmi,vma->via", choosing_mask, block_input_rows.astype(jnp.float32), precision=maximal_precision).astype(jnp.bfloat16)
        position_gradient = (jnp.einsum("vmi,vma->via", choosing_mask, block_output_gradient.astype(jnp.float32), precision=maximal_precision) * position_gate).astype(jnp.bfloat16)
        expert_rows = position_rows.reshape(N_EXPERT, EXPERTS, CAP, D).transpose(1, 0, 2, 3).reshape(EXPERTS, N_EXPERT * CAP, D)
        expert_grad = position_gradient.reshape(N_EXPERT, EXPERTS, CAP, D).transpose(1, 0, 2, 3).reshape(EXPERTS, N_EXPERT * CAP, D)
        hidden, grad_act, token_back = jax.vmap(expert_math)(expert_rows, expert_grad, gate_up, down_proj)
        upper_part = jnp.einsum("erd,erf->edf", expert_rows.astype(jnp.float32), grad_act.astype(jnp.float32), precision=maximal_precision)
        lower_part = jnp.einsum("erf,erd->efd", hidden.astype(jnp.float32), expert_grad.astype(jnp.float32), precision=maximal_precision)
        reverse_block_list = token_back.reshape(EXPERTS, N_EXPERT, CAP, D).transpose(1, 0, 2, 3).reshape(N_EXPERT, EXPERTS * CAP, D)
        cluster_gradient = jnp.einsum("zyc,zcg->zyg", choosing_mask, reverse_block_list.astype(jnp.float32), precision=maximal_precision).astype(jnp.bfloat16)
        return (totals[0] + upper_part, totals[1] + lower_part), cluster_gradient.reshape(group_rows, D)

    start_totals = (jnp.zeros((EXPERTS, D, 2 * FF), jnp.float32), jnp.zeros((EXPERTS, FF, D), jnp.float32))
    sums, grads = lax.scan(one_group, start_totals, jnp.arange(N_DP, dtype=jnp.int32))
    return grads.reshape(TOKENS, D), sums[0].astype(jnp.bfloat16), sums[1].astype(jnp.bfloat16)
```

```python
import jax
import jax.numpy as jnp
from jax import lax
from jax.sharding import Mesh, PartitionSpec as P

CAP = 48
BF = jnp.bfloat16
F32 = jnp.float32
AXES = ("w", "x", "y", "v", "c")


def swap_expert(a, k):
    return lax.ppermute(a, ("v", "c"), [(i, i ^ k) for i in range(4)])


def shift(a, axis, j):
    if j == 0:
        return a
    return lax.ppermute(a, axis, [(i, (i + j) % 4) for i in range(4)])


def swap_w(a):
    return lax.ppermute(a, "w", [(0, 1), (1, 0)])


def rows_dot(a, b):
    return lax.dot_general(a, b, (((0,), (0,)), ((), ())), preferred_element_type=F32)


def shards(tokens, cotangent, routes, gates, gate_up, down_proj):
    gate_up, down_proj = gate_up[0], down_proj[0]
    w, x, y = lax.axis_index("w"), lax.axis_index("x"), lax.axis_index("y")
    me = lax.axis_index(("v", "c"))
    toks, width = tokens.shape
    inner = down_proj.shape[0]
    experts = jnp.bitwise_xor(me, jnp.arange(4, dtype=jnp.int32))
    matches = routes[:, :, None] == experts[None, None, :]
    member = jnp.any(matches, axis=1)
    weight = jnp.sum(jnp.where(matches, gates[:, :, None], F32(0.0)), axis=1)
    position = jnp.cumsum(member.astype(jnp.int32), axis=0) - 1
    select = member[:, :, None] & (
        position[:, :, None] == jnp.arange(CAP, dtype=jnp.int32)[None, None, :]
    )
    mask = select.astype(BF).reshape(toks, 4 * CAP)
    slot_gate = jnp.sum(jnp.where(select, weight[:, :, None], F32(0.0)), axis=0).reshape(4 * CAP, 1)
    send_x = rows_dot(mask, tokens).astype(BF).reshape(4, CAP, width)
    send_g = (rows_dot(mask, cotangent) * slot_gate).astype(BF).reshape(4, CAP, width)
    X = jnp.concatenate([send_x[0]] + [swap_expert(send_x[k], k) for k in (1, 2, 3)], axis=0)
    G = jnp.concatenate([send_g[0]] + [swap_expert(send_g[k], k) for k in (1, 2, 3)], axis=0)
    rows = X.shape[0]

    X5 = X.reshape(rows, 2, 4, 4, 128)
    xa = [
        shift(lax.dynamic_index_in_dim(X5, (x + j) % 4, 2, False).reshape(rows, width // 4), "x", j)
        for j in range(4)
    ]
    xb = [
        shift(lax.dynamic_index_in_dim(X5, (y + j) % 4, 3, False).reshape(rows, width // 4), "y", j)
        for j in range(4)
    ]

    act = jnp.dot(X, gate_up, preferred_element_type=F32)
    gpart, upart = act[:, :inner], act[:, inner:]
    sig = jax.nn.sigmoid(gpart)
    silu = gpart * sig
    hidden = (silu * upart).astype(BF)

    ga = [
        shift(lax.dynamic_slice_in_dim(G, ((y + j) % 4) * (width // 4), width // 4, 1), "y", j)
        for j in range(4)
    ]
    ha = [shift(hidden, "y", j) for j in range(4)]

    dh = lax.dot_general(G, down_proj, (((1,), (1,)), ((), ())), preferred_element_type=F32)
    dact_g = (dh * upart * (sig * (1.0 + gpart * (1.0 - sig)))).astype(BF)
    dact_u = (dh * silu).astype(BF)

    da = [shift(dact_g, "x", j) for j in range(4)]
    db = [shift(dact_u, "y", j) for j in range(4)]

    back = lax.dot_general(
        jnp.concatenate([dact_g, dact_u], axis=1),
        gate_up,
        (((1,), (1,)), ((), ())),
        preferred_element_type=F32,
    ).astype(BF).reshape(4, CAP, width)
    arrived = jnp.concatenate([back[0]] + [swap_expert(back[k], k) for k in (1, 2, 3)], axis=0)
    token_grad = jnp.dot(mask, arrived, preferred_element_type=F32).astype(BF)

    def gate_half(xs, ds, other, name):
        xs4 = jnp.concatenate(xs, axis=0).reshape(4 * rows, 2, 4, 128)
        ds4 = jnp.concatenate(ds, axis=0)
        total = None
        for j in (1, 2, 3, 0):
            part = lax.dynamic_index_in_dim(xs4, (other + j) % 4, 2, False).reshape(4 * rows, 256)
            got = rows_dot(part, ds4)
            if j:
                got = shift(got.astype(BF), name, j).astype(F32)
            total = got if total is None else total + got
        total = total.reshape(2, 128, inner)
        theirs = swap_w(lax.dynamic_index_in_dim(total, 1 - w, 0, False).astype(BF))
        return (lax.dynamic_index_in_dim(total, w, 0, False) + theirs.astype(F32)).astype(BF)

    pd = rows_dot(jnp.concatenate(ha, axis=0), jnp.concatenate(ga, axis=0))
    pd = pd.reshape(2, 4, 96, width // 4)
    total = None
    for j in (1, 2, 3, 0):
        got = lax.dynamic_index_in_dim(pd, (x + j) % 4, 1, False)
        if j:
            got = shift(got.astype(BF), "x", j).astype(F32)
        total = got if total is None else total + got

    gate_grad = gate_half(xa, da, y, "y")
    up_grad = gate_half(xb, db, x, "x")
    theirs = swap_w(lax.dynamic_index_in_dim(total, 1 - w, 0, False).astype(BF))
    down = (lax.dynamic_index_in_dim(total, w, 0, False) + theirs.astype(F32)).astype(BF)
    down = down.reshape(4, 24, width // 4)
    cols = [
        shift(lax.dynamic_index_in_dim(down, (y + j) % 4, 0, False), "y", j) for j in range(4)
    ]
    turned = jnp.concatenate(cols[::-1] + cols[::-1], axis=1)
    down_grad = lax.dynamic_slice_in_dim(turned, (3 - y) * (width // 4), width, 1)
    return token_grad, jnp.concatenate([gate_grad, up_grad], axis=1)[None], down_grad[None]


def solution(mesh):
    fine = Mesh(mesh.devices.reshape(2, 4, 4, 2, 2), AXES)
    rows, expert, dp = P(AXES, None), ("v", "c"), ("w", "x", "y")
    in_specs = (rows, rows, rows, rows, P(expert, None, None), P(expert, None, None))
    out_specs = (rows, P(expert, dp, None), P(expert, dp, None))
    return jax.shard_map(
        shards, mesh=fine, in_specs=in_specs, out_specs=out_specs, check_vma=False
    )
```

```python
import functools

import jax
import jax.numpy as jnp
from jax import lax
from jax.experimental import pallas as pl
from jax.experimental.pallas import tpu as pltpu
from jax.sharding import Mesh, PartitionSpec as P

CAP = 48
BF = jnp.bfloat16
F32 = jnp.float32
AXES = ("w", "x", "y", "v", "c")
VMEM = pl.BlockSpec(memory_space=pltpu.VMEM)
SMEM = pl.BlockSpec(memory_space=pltpu.SMEM)
LIMIT = 48 * 1024 * 1024


def swap_expert(a, k):
    return lax.ppermute(a, ("v", "c"), [(i, i ^ k) for i in range(4)])


def shift(a, axis, j):
    if j == 0:
        return a
    return lax.ppermute(a, axis, [(i, (i + j) % 4) for i in range(4)])


def swap_w(a):
    return lax.ppermute(a, "w", [(0, 1), (1, 0)])


def rows_dot(a, b):
    return lax.dot_general(a, b, (((0,), (0,)), ((), ())), preferred_element_type=F32)


def wide_dot(a, b):
    return lax.dot_general(a, b, (((1,), (1,)), ((), ())), preferred_element_type=F32)


def shape(rows, cols, dtype=BF):
    return jax.ShapeDtypeStruct((rows, cols), dtype)


def call(body, outs, ins, scratch=(), flops=0, moved=0, scalars=1):
    return pl.pallas_call(
        body,
        out_shape=outs,
        in_specs=[SMEM] * scalars + [VMEM] * (ins - scalars),
        out_specs=[VMEM] * len(outs),
        scratch_shapes=list(scratch),
        compiler_params=pltpu.CompilerParams(vmem_limit_bytes=LIMIT),
        cost_estimate=pl.CostEstimate(flops=flops, bytes_accessed=moved, transcendentals=0),
    )


def aligned(i, size):
    return pl.ds(pl.multiple_of(i * size, size), size)


def pack_x(at, x0, x1, x2, x3, *outs):
    x, y = at[1], at[2]
    whole, alongx, alongy = outs[0], outs[1:5], outs[5:9]
    for k, piece in enumerate((x0, x1, x2, x3)):
        rows = pl.ds(k * CAP, CAP)
        whole[rows, :] = piece[...]
        for j in range(4):
            for b in range(2):
                tx = b * 4 + lax.rem(x + j, 4)
                alongx[j][rows, b * 512 : b * 512 + 512] = piece[:, aligned(tx, 512)]
            for b in range(8):
                ty = b * 4 + lax.rem(y + j, 4)
                alongy[j][rows, b * 128 : b * 128 + 128] = piece[:, aligned(ty, 128)]


def pack_g(at, g0, g1, g2, g3, hidden, *outs):
    for j in range(4):
        cols = aligned(lax.rem(at[2] + j, 4), 1024)
        for k, piece in enumerate((g0, g1, g2, g3)):
            outs[j][k * CAP : k * CAP + CAP, :1024] = piece[:, cols]
        outs[j][:, 1024:] = hidden[...]


def act_step(x, wg, wu, hidden, slope, silu):
    gpart = jnp.dot(x[...], wg[...], preferred_element_type=F32)
    upart = jnp.dot(x[...], wu[...], preferred_element_type=F32)
    sig = jax.nn.sigmoid(gpart)
    soft = gpart * sig
    hidden[...] = (soft * upart).astype(BF)
    slope[...] = upart * (sig * (1.0 + gpart * (1.0 - sig)))
    silu[...] = soft


def act_call(X, gate_up, inner):
    rows, width = X.shape
    step = 256
    n = inner // step
    out = pl.BlockSpec((rows, step), lambda i: (0, i))
    return pl.pallas_call(
        act_step,
        grid=(n,),
        in_specs=[
            pl.BlockSpec((rows, width), lambda i: (0, 0)),
            pl.BlockSpec((width, step), lambda i: (0, i)),
            pl.BlockSpec((width, step), lambda i: (0, i + n)),
        ],
        out_specs=[out, out, out],
        out_shape=[shape(rows, inner), shape(rows, inner, F32), shape(rows, inner, F32)],
        compiler_params=pltpu.CompilerParams(vmem_limit_bytes=LIMIT),
        cost_estimate=pl.CostEstimate(
            flops=4 * rows * width * inner, bytes_accessed=4 * width * inner, transcendentals=0
        ),
    )(X, gate_up, gate_up)


def dh_step(g0, g1, g2, g3, wd, slope, silu, dact_g, dact_u, whole):
    @pl.when(pl.program_id(0) == 0)
    def _():
        for k, piece in enumerate((g0, g1, g2, g3)):
            whole[k * CAP : k * CAP + CAP, :] = piece[...]

    dh = wide_dot(whole[...], wd[...])
    dact_g[...] = (dh * slope[...]).astype(BF)
    dact_u[...] = (dh * silu[...]).astype(BF)


def dh_call(gs, down_proj, slope, silu):
    inner, width = down_proj.shape
    rows = slope.shape[0]
    step = 256
    part = pl.BlockSpec((rows, step), lambda i: (0, i))
    return pl.pallas_call(
        dh_step,
        grid=(inner // step,),
        in_specs=[pl.BlockSpec((CAP, width), lambda i: (0, 0))] * 4
        + [pl.BlockSpec((step, width), lambda i: (i, 0)), part, part],
        out_specs=[part, part],
        out_shape=[shape(rows, inner)] * 2,
        scratch_shapes=[pltpu.VMEM((rows, width), BF)],
        compiler_params=pltpu.CompilerParams(vmem_limit_bytes=LIMIT),
        cost_estimate=pl.CostEstimate(
            flops=2 * rows * width * inner, bytes_accessed=2 * width * inner, transcendentals=0
        ),
    )(*gs, down_proj, slope, silu)


def back_step(dg, du, wt, b0, b1, b2, b3):
    inner = dg.shape[1]
    got = wide_dot(dg[...], wt[:, :inner]) + wide_dot(du[...], wt[:, inner:])
    for k, out in enumerate((b0, b1, b2, b3)):
        out[...] = got[k * CAP : k * CAP + CAP].astype(BF)


def back_call(dg, du, gate_up):
    rows, inner = dg.shape
    width = gate_up.shape[0]
    step = 512
    return pl.pallas_call(
        back_step,
        grid=(width // step,),
        in_specs=[pl.BlockSpec((rows, inner), lambda i: (0, 0))] * 2
        + [pl.BlockSpec((step, 2 * inner), lambda i: (i, 0))],
        out_specs=[pl.BlockSpec((CAP, step), lambda i: (0, i))] * 4,
        out_shape=[shape(CAP, width)] * 4,
        compiler_params=pltpu.CompilerParams(vmem_limit_bytes=LIMIT),
        cost_estimate=pl.CostEstimate(
            flops=4 * rows * width * inner, bytes_accessed=4 * width * inner, transcendentals=0
        ),
    )(dg, du, gate_up)


def tok_step(mask, a0, a1, a2, a3, out, whole):
    for k, piece in enumerate((a0, a1, a2, a3)):
        whole[k * CAP : k * CAP + CAP, :] = piece[...]
    out[...] = jnp.dot(mask[...], whole[...], preferred_element_type=F32).astype(BF)


def tile_step(axis, at, *refs):
    xs, ds, outs, xall, dall = refs[:4], refs[4:8], refs[8:12], refs[12], refs[13]
    rows = xs[0].shape[0]
    for p in range(4):
        xall[p * rows : p * rows + rows, :] = xs[p][...]
        dall[p * rows : p * rows + rows, :] = ds[p][...]
    for j in (1, 2, 3, 0):
        other = lax.rem(at[axis] + j, 4)
        for b in range(2):
            got = rows_dot(xall[:, aligned(b * 4 + other, 128)], dall[...])
            outs[j][b * 128 : b * 128 + 128, :] = got.astype(outs[j].dtype)


def tile_call(axis, at, xs, ds):
    rows, part = xs[0].shape
    inner = ds[0].shape[1]
    return call(
        functools.partial(tile_step, axis),
        [shape(256, inner, F32)] + [shape(256, inner)] * 3,
        9,
        [pltpu.VMEM((4 * rows, part), BF), pltpu.VMEM((4 * rows, inner), BF)],
        flops=8 * rows * part * inner,
        moved=8 * rows * (part + inner),
    )(at, *xs, *ds)


def down_step(at, *refs):
    gh, outs, gall, hall, total = refs[:4], refs[4:8], refs[8], refs[9], refs[10]
    rows = gh[0].shape[0]
    for p in range(4):
        gall[p * rows : p * rows + rows, :] = gh[p][:, :1024]
        hall[p * rows : p * rows + rows, :] = gh[p][:, 1024:]
    for b in range(6):
        cols = slice(b * 128, b * 128 + 128)
        total[cols, :] = rows_dot(hall[:, cols], gall[...])
    for j in (1, 2, 3, 0):
        other = lax.rem(at[1] + j, 4)
        for b in range(2):
            outs[j][b * 96 : b * 96 + 96, :] = total[aligned(b * 4 + other, 96), :].astype(outs[j].dtype)


def down_call(at, gh):
    rows, wide = gh[0].shape
    inner = wide - 1024
    return call(
        down_step,
        [shape(192, 1024, F32)] + [shape(192, 1024)] * 3,
        5,
        [
            pltpu.VMEM((4 * rows, 1024), BF),
            pltpu.VMEM((4 * rows, inner), BF),
            pltpu.VMEM((inner, 1024), F32),
        ],
        flops=8 * rows * 1024 * inner,
        moved=8 * rows * wide,
    )(at, *gh)


def sum_step(at, own, r1, r2, r3, keep, send):
    half = keep.shape[0]
    w = at[0]

    def part(i):
        rows = aligned(i, half)
        return own[rows, :] + r1[rows, :].astype(F32) + r2[rows, :].astype(F32) + r3[rows, :].astype(F32)

    send[...] = part(1 - w).astype(BF)
    keep[...] = part(w)


def sum_call(at, own, got):
    rows, cols = own.shape
    return call(
        sum_step, [shape(rows // 2, cols, F32), shape(rows // 2, cols)], 5, moved=10 * rows * cols
    )(at, own, *got)


def shards(tokens, cotangent, routes, gates, gate_up, down_proj):
    gate_up, down_proj = gate_up[0], down_proj[0]
    w, x, y = lax.axis_index("w"), lax.axis_index("x"), lax.axis_index("y")
    at = jnp.stack([w, x, y]).astype(jnp.int32)
    me = lax.axis_index(("v", "c"))
    toks, width = tokens.shape
    inner = down_proj.shape[0]
    experts = jnp.bitwise_xor(me, jnp.arange(4, dtype=jnp.int32))
    matches = routes[:, :, None] == experts[None, None, :]
    member = jnp.any(matches, axis=1)
    weight = jnp.sum(jnp.where(matches, gates[:, :, None], F32(0.0)), axis=1)
    position = jnp.cumsum(member.astype(jnp.int32), axis=0) - 1
    select = member[:, :, None] & (
        position[:, :, None] == jnp.arange(CAP, dtype=jnp.int32)[None, None, :]
    )
    mask = select.astype(BF).reshape(toks, 4 * CAP)
    slot_gate = jnp.sum(jnp.where(select, weight[:, :, None], F32(0.0)), axis=0).reshape(4 * CAP, 1)
    send_x = rows_dot(mask, tokens).astype(BF).reshape(4, CAP, width)
    send_g = (rows_dot(mask, cotangent) * slot_gate).astype(BF).reshape(4, CAP, width)
    xs = [send_x[0]] + [swap_expert(send_x[k], k) for k in (1, 2, 3)]
    gs = [send_g[0]] + [swap_expert(send_g[k], k) for k in (1, 2, 3)]
    rows = 4 * CAP

    part = shape(rows, width // 4)
    packed = call(pack_x, [shape(rows, width)] + [part] * 8, 5, moved=8 * rows * width)(at, *xs)
    X = packed[0]
    xa = [shift(packed[1 + j], "x", j) for j in range(4)]
    xb = [shift(packed[5 + j], "y", j) for j in range(4)]
    hidden, slope, silu = act_call(X, gate_up, inner)
    dact_g, dact_u = dh_call(gs, down_proj, slope, silu)
    da = [shift(dact_g, "x", j) for j in range(4)]
    db = [shift(dact_u, "y", j) for j in range(4)]

    gh = call(pack_g, [shape(rows, width // 4 + inner)] * 4, 6, moved=8 * rows * width // 2)(
        at, *gs, hidden
    )
    gh = [shift(gh[j], "y", j) for j in range(4)]

    back = back_call(dact_g, dact_u, gate_up)
    arrived = [back[0]] + [swap_expert(back[k], k) for k in (1, 2, 3)]
    token_grad = call(
        tok_step,
        [shape(toks, width)],
        5,
        [pltpu.VMEM((rows, width), BF)],
        flops=2 * toks * rows * width,
        moved=2 * (rows + toks) * width,
        scalars=0,
    )(mask, *arrived)[0]

    def half(axis, name, xs, ds):
        parts = tile_call(axis, at, xs, ds)
        keep, send = sum_call(at, parts[0], [shift(parts[j], name, j) for j in (1, 2, 3)])
        return (keep + swap_w(send).astype(F32)).astype(BF)

    parts = down_call(at, gh)
    keep, send = sum_call(at, parts[0], [shift(parts[j], "x", j) for j in (1, 2, 3)])
    down = (keep + swap_w(send).astype(F32)).astype(BF).reshape(4, 24, width // 4)
    cols = [
        shift(lax.dynamic_index_in_dim(down, (y + j) % 4, 0, False), "y", j) for j in range(4)
    ]
    turned = jnp.concatenate(cols[::-1] + cols[::-1], axis=1)
    down_grad = lax.dynamic_slice_in_dim(turned, (3 - y) * (width // 4), width, 1)

    gate_grad = half(2, "y", xa, da)
    up_grad = half(1, "x", xb, db)
    return token_grad, jnp.concatenate([gate_grad, up_grad], axis=1)[None], down_grad[None]


def solution(mesh):
    fine = Mesh(mesh.devices.reshape(2, 4, 4, 2, 2), AXES)
    rows, expert, dp = P(AXES, None), ("v", "c"), ("w", "x", "y")
    in_specs = (rows, rows, rows, rows, P(expert, None, None), P(expert, None, None))
    out_specs = (rows, P(expert, dp, None), P(expert, dp, None))
    return jax.shard_map(
        shards, mesh=fine, in_specs=in_specs, out_specs=out_specs, check_vma=False
    )
```

```python
import functools

import jax
import jax.numpy as jnp
from jax import lax
from jax.experimental import pallas as pl
from jax.experimental.pallas import tpu as pltpu
from jax.sharding import Mesh, PartitionSpec as P

CAP = 48
BF = jnp.bfloat16
F32 = jnp.float32
AXES = ("w", "x", "y", "v", "c")
VMEM = pl.BlockSpec(memory_space=pltpu.VMEM)
SMEM = pl.BlockSpec(memory_space=pltpu.SMEM)
MB = 1024 * 1024


def swap_expert(a):
    return lax.all_to_all(a, ("v", "c"), split_axis=0, concat_axis=0, tiled=True)


def shift(a, axis, j):
    if j == 0:
        return a
    return lax.ppermute(a, axis, [(i, (i + j) % 4) for i in range(4)])


def swap_w(a):
    return lax.ppermute(a, "w", [(0, 1), (1, 0)])


def rows_dot(a, b):
    return lax.dot_general(a, b, (((0,), (0,)), ((), ())), preferred_element_type=F32)


def wide_dot(a, b):
    return lax.dot_general(a, b, (((1,), (1,)), ((), ())), preferred_element_type=F32)


def shape(rows, cols, dtype=BF):
    return jax.ShapeDtypeStruct((rows, cols), dtype)


def call(body, outs, ins, scratch=(), flops=0, moved=0, scalars=1, after=0, limit=8):
    return pl.pallas_call(
        body,
        out_shape=outs,
        in_specs=[SMEM] * scalars + [VMEM] * (ins - scalars) + [pl.BlockSpec(memory_space=pl.ANY)] * after,
        out_specs=[VMEM] * len(outs),
        scratch_shapes=list(scratch),
        compiler_params=pltpu.CompilerParams(vmem_limit_bytes=limit * MB),
        cost_estimate=pl.CostEstimate(flops=flops, bytes_accessed=moved, transcendentals=0),
    )


def aligned(i, size):
    return pl.ds(pl.multiple_of(i * size, size), size)


def pack_x(at, whole, *outs):
    for j in range(4):
        for b in range(2):
            cols = aligned(b * 4 + lax.rem(at[1] + j, 4), 512)
            outs[j][:, b * 512 : b * 512 + 512] = whole[:, cols]


def pack_g(whole, hidden, *rest):
    out, part = rest[-1], whole.shape[1] // 4
    for i in range(4):
        out[i, :, :part] = whole[:, i * part : i * part + part]
        out[i, :, part:] = hidden[...]


def act_step(x, wg, wu, hidden, slope, silu):
    gpart = jnp.dot(x[...], wg[...], preferred_element_type=F32)
    upart = jnp.dot(x[...], wu[...], preferred_element_type=F32)
    sig = jax.nn.sigmoid(gpart)
    soft = gpart * sig
    hidden[...] = (soft * upart).astype(BF)
    slope[...] = upart * (sig * (1.0 + gpart * (1.0 - sig)))
    silu[...] = soft


def act_call(X, gate_up, inner):
    rows, width = X.shape
    step = 256
    n = inner // step
    out = pl.BlockSpec((rows, step), lambda i: (0, i))
    return pl.pallas_call(
        act_step,
        grid=(n,),
        in_specs=[
            pl.BlockSpec((rows, width), lambda i: (0, 0)),
            pl.BlockSpec((width, step), lambda i: (0, i)),
            pl.BlockSpec((width, step), lambda i: (0, i + n)),
        ],
        out_specs=[out, out, out],
        out_shape=[shape(rows, inner), shape(rows, inner, F32), shape(rows, inner, F32)],
        compiler_params=pltpu.CompilerParams(vmem_limit_bytes=16 * MB),
        cost_estimate=pl.CostEstimate(
            flops=4 * rows * width * inner, bytes_accessed=4 * width * inner, transcendentals=0
        ),
    )(X, gate_up, gate_up)


def dh_step(whole, wd, slope, silu, *rest):
    dact = rest[-1]
    dh = wide_dot(whole[...], wd[...])
    dact[0] = (dh * slope[...]).astype(BF)
    dact[1] = (dh * silu[...]).astype(BF)


def dh_call(G, down_proj, slope, silu, after):
    inner, width = down_proj.shape
    rows = slope.shape[0]
    step = 256
    part = pl.BlockSpec((rows, step), lambda i: (0, i))
    return pl.pallas_call(
        dh_step,
        grid=(inner // step,),
        in_specs=[
            pl.BlockSpec((rows, width), lambda i: (0, 0)),
            pl.BlockSpec((step, width), lambda i: (i, 0)),
            part,
            part,
        ]
        + [pl.BlockSpec(memory_space=pl.ANY)] * len(after),
        out_specs=pl.BlockSpec((2, rows, step), lambda i: (0, 0, i)),
        out_shape=jax.ShapeDtypeStruct((2, rows, inner), BF),
        compiler_params=pltpu.CompilerParams(vmem_limit_bytes=16 * MB),
        cost_estimate=pl.CostEstimate(
            flops=2 * rows * width * inner, bytes_accessed=2 * width * inner, transcendentals=0
        ),
    )(G, down_proj, slope, silu, *after)


def back_step(dact, wt, *rest):
    out, inner = rest[-1], dact.shape[2]
    out[...] = (wide_dot(dact[0], wt[:, :inner]) + wide_dot(dact[1], wt[:, inner:])).astype(BF)


def back_call(dact, gate_up, after):
    rows, inner = dact.shape[1:]
    width = gate_up.shape[0]
    step = 512
    return pl.pallas_call(
        back_step,
        grid=(width // step,),
        in_specs=[pl.BlockSpec((2, rows, inner), lambda i: (0, 0, 0))]
        + [pl.BlockSpec((step, 2 * inner), lambda i: (i, 0))]
        + [pl.BlockSpec(memory_space=pl.ANY)] * len(after),
        out_specs=pl.BlockSpec((rows, step), lambda i: (0, i)),
        out_shape=shape(rows, width),
        compiler_params=pltpu.CompilerParams(vmem_limit_bytes=16 * MB),
        cost_estimate=pl.CostEstimate(
            flops=4 * rows * width * inner, bytes_accessed=4 * width * inner, transcendentals=0
        ),
    )(dact, gate_up, *after)


def tok_step(mask, whole, out):
    out[...] = jnp.dot(mask[...], whole[...], preferred_element_type=F32).astype(BF)


def tile_step(at, *refs):
    xs, ds, outs, xall, dall = refs[:4], refs[4:8], refs[-6:-2], refs[-2], refs[-1]
    rows, inner = ds[0].shape[1:]
    for p in range(4):
        part = slice(p * rows, p * rows + rows)
        xall[part, :] = xs[p][...]
        for h in range(2):
            dall[part, h * inner : h * inner + inner] = ds[p][h]
    for j in (1, 2, 3, 0):
        other = lax.rem(at[2] + j, 4)
        for b in range(2):
            got = rows_dot(xall[:, aligned(b * 4 + other, 128)], dall[...])
            outs[j][b * 128 : b * 128 + 128, :] = got.astype(outs[j].dtype)


def tile_call(at, xs, ds, after):
    rows, part = xs[0].shape
    wide = 2 * ds[0].shape[2]
    return call(
        tile_step,
        [shape(256, wide, F32)] + [shape(256, wide)] * 3,
        9,
        [pltpu.VMEM((4 * rows, part), BF), pltpu.VMEM((4 * rows, wide), BF)],
        flops=8 * rows * part * wide,
        moved=8 * rows * (part + wide),
        after=len(after),
        limit=12,
    )(at, *xs, *ds, *after)


def down_step(at, both, *rest):
    outs, gall, hall, total = rest[-7:-3], rest[-3], rest[-2], rest[-1]
    rows, part, inner = both.shape[1], gall.shape[1], hall.shape[1]
    for i in range(4):
        gall[i * rows : i * rows + rows, :] = both[i, :, :part]
        hall[i * rows : i * rows + rows, :] = both[i, :, part:]
    for b in range(inner // 128):
        cols = slice(b * 128, b * 128 + 128)
        total[cols, :] = rows_dot(hall[:, cols], gall[...])
    for j in (1, 2, 3, 0):
        other = lax.rem(at[1] + j, 4)
        for b in range(2):
            outs[j][b * 96 : b * 96 + 96, :] = total[aligned(b * 4 + other, 96), :].astype(outs[j].dtype)


def down_call(at, both, part, after):
    rows, inner = both.shape[1], both.shape[2] - part
    return call(
        down_step,
        [shape(192, part, F32)] + [shape(192, part)] * 3,
        2,
        [
            pltpu.VMEM((4 * rows, part), BF),
            pltpu.VMEM((4 * rows, inner), BF),
            pltpu.VMEM((inner, part), F32),
        ],
        flops=8 * rows * part * inner,
        moved=8 * rows * (part + inner),
        after=len(after),
        limit=16,
    )(at, both, *after)


def sum_step(at, *refs):
    parts, keep, send = refs[:4], refs[-2], refs[-1]
    half = keep.shape[0]

    def part(i):
        rows = aligned(i, half)
        return sum((r[rows, :].astype(F32) for r in parts[1:]), parts[0][rows, :])

    send[...] = part(1 - at[0]).astype(BF)
    keep[...] = part(at[0])


def sum_call(at, parts, after):
    rows, cols = parts[0].shape
    outs = [shape(rows // 2, cols, F32), shape(rows // 2, cols)]
    return call(sum_step, outs, 5, moved=10 * rows * cols, after=len(after))(at, *parts, *after)


def shards(tokens, cotangent, routes, gates, gate_up, down_proj):
    gate_up, down_proj = gate_up[0], down_proj[0]
    w, x, y = lax.axis_index("w"), lax.axis_index("x"), lax.axis_index("y")
    at = jnp.stack([w, x, y]).astype(jnp.int32)
    toks, width = tokens.shape
    inner = down_proj.shape[0]
    experts = jnp.arange(4, dtype=jnp.int32)
    matches = routes[:, :, None] == experts[None, None, :]
    member = jnp.any(matches, axis=1)
    weight = jnp.sum(jnp.where(matches, gates[:, :, None], F32(0.0)), axis=1)
    position = jnp.cumsum(member.astype(jnp.int32), axis=0) - 1
    select = member[:, :, None] & (
        position[:, :, None] == jnp.arange(CAP, dtype=jnp.int32)[None, None, :]
    )
    mask = select.astype(BF).reshape(toks, 4 * CAP)
    slot_gate = jnp.sum(jnp.where(select, weight[:, :, None], F32(0.0)), axis=0).reshape(4 * CAP, 1)
    send_x = rows_dot(mask, tokens).astype(BF).reshape(4, CAP, width)
    send_g = (rows_dot(mask, cotangent) * slot_gate).astype(BF).reshape(4, CAP, width)
    rows = 4 * CAP
    X = swap_expert(send_x).reshape(rows, width)
    G = swap_expert(send_g).reshape(rows, width)

    part = width // 4
    packed = call(pack_x, [shape(rows, part)] * 4, 2, moved=4 * rows * width)(at, X)
    xa = [shift(packed[j], "x", j) for j in range(4)]
    hidden, slope, silu = act_call(X, gate_up, inner)
    sent = call(
        pack_g,
        [jax.ShapeDtypeStruct((4, rows, part + inner), BF)],
        2,
        moved=4 * rows * width,
        scalars=0,
        after=3,
    )(G, hidden, *xa[1:])[0]
    both = lax.all_to_all(sent, "y", split_axis=0, concat_axis=0, tiled=True)
    dact = dh_call(G, down_proj, slope, silu, [sent])
    da = [shift(dact, "x", j) for j in range(4)]
    parts = tile_call(at, xa, da, [])
    gate = [parts[0]] + [shift(parts[j], "y", j) for j in (1, 2, 3)]
    back = back_call(dact, gate_up, [da[2]])
    arrived = swap_expert(back.reshape(4, CAP, width)).reshape(rows, width)
    token_grad = call(
        tok_step,
        [shape(toks, width)],
        2,
        flops=2 * toks * rows * width,
        moved=2 * (rows + toks) * width,
        scalars=0,
    )(mask, arrived)[0]
    parts = down_call(at, both, part, [])
    down = [parts[0]] + [shift(parts[j], "x", j) for j in (1, 2, 3)]

    keep, send = sum_call(at, down, [])
    down_grad = (keep + swap_w(send).astype(F32)).astype(BF).reshape(4, 24, part)
    down_grad = lax.all_to_all(down_grad, "y", split_axis=0, concat_axis=0, tiled=True)
    down_grad = jnp.concatenate([down_grad[i] for i in range(4)], axis=1)

    keep, send = sum_call(at, gate, [token_grad])
    gate_up_grad = (keep + swap_w(send).astype(F32)).astype(BF)
    return token_grad, gate_up_grad[None], down_grad[None]


def solution(mesh):
    fine = Mesh(mesh.devices.reshape(2, 4, 4, 2, 2), AXES)
    rows, expert, dp = P(AXES, None), ("v", "c"), ("w", "x", "y")
    in_specs = (rows, rows, rows, rows, P(expert, None, None), P(expert, None, None))
    out_specs = (rows, P(expert, dp, None), P(expert, dp, None))
    return jax.shard_map(
        shards, mesh=fine, in_specs=in_specs, out_specs=out_specs, check_vma=False
    )
```

```python
import functools

import jax
import jax.numpy as jnp
from jax import lax
from jax.experimental import pallas as pl
from jax.experimental.pallas import tpu as pltpu
from jax.sharding import Mesh, PartitionSpec as P

CAP = 48
BF = jnp.bfloat16
F32 = jnp.float32
AXES = ("w", "x", "y", "v", "c")
VMEM = pl.BlockSpec(memory_space=pltpu.VMEM)
SMEM = pl.BlockSpec(memory_space=pltpu.SMEM)
MB = 1024 * 1024


def swap_expert(a, k):
    return lax.ppermute(a, ("v", "c"), [(i, i ^ k) for i in range(4)])


def shift(a, axis, j):
    if j == 0:
        return a
    return lax.ppermute(a, axis, [(i, (i + j) % 4) for i in range(4)])


def swap_w(a):
    return lax.ppermute(a, "w", [(0, 1), (1, 0)])


def rows_dot(a, b):
    return lax.dot_general(a, b, (((0,), (0,)), ((), ())), preferred_element_type=F32)


def wide_dot(a, b):
    return lax.dot_general(a, b, (((1,), (1,)), ((), ())), preferred_element_type=F32)


def shape(rows, cols, dtype=BF):
    return jax.ShapeDtypeStruct((rows, cols), dtype)


def call(body, outs, ins, scratch=(), flops=0, moved=0, scalars=1, after=0, limit=8):
    return pl.pallas_call(
        body,
        out_shape=outs,
        in_specs=[SMEM] * scalars + [VMEM] * (ins - scalars) + [pl.BlockSpec(memory_space=pl.ANY)] * after,
        out_specs=[VMEM] * len(outs),
        scratch_shapes=list(scratch),
        compiler_params=pltpu.CompilerParams(vmem_limit_bytes=limit * MB),
        cost_estimate=pl.CostEstimate(flops=flops, bytes_accessed=moved, transcendentals=0),
    )


def aligned(i, size):
    return pl.ds(pl.multiple_of(i * size, size), size)


def pack_x(at, x0, x1, x2, x3, *outs):
    whole = outs[4]
    for k, piece in enumerate((x0, x1, x2, x3)):
        rows = slice(k * CAP, k * CAP + CAP)
        whole[rows, :] = piece[...]
        for j in range(4):
            for b in range(2):
                cols = aligned(b * 4 + lax.rem(at[1] + j, 4), 512)
                outs[j][rows, b * 512 : b * 512 + 512] = piece[:, cols]


def pack_g(g0, g1, g2, g3, hidden, *rest):
    out, part = rest[-1], g0.shape[1] // 4
    for i in range(4):
        for k, piece in enumerate((g0, g1, g2, g3)):
            out[i, k * CAP : k * CAP + CAP, :part] = piece[:, i * part : i * part + part]
        out[i, :, part:] = hidden[...]


def act_step(x, wg, wu, hidden, slope, silu):
    gpart = jnp.dot(x[...], wg[...], preferred_element_type=F32)
    upart = jnp.dot(x[...], wu[...], preferred_element_type=F32)
    sig = jax.nn.sigmoid(gpart)
    soft = gpart * sig
    hidden[...] = (soft * upart).astype(BF)
    slope[...] = upart * (sig * (1.0 + gpart * (1.0 - sig)))
    silu[...] = soft


def act_call(X, gate_up, inner):
    rows, width = X.shape
    step = 256
    n = inner // step
    out = pl.BlockSpec((rows, step), lambda i: (0, i))
    return pl.pallas_call(
        act_step,
        grid=(n,),
        in_specs=[
            pl.BlockSpec((rows, width), lambda i: (0, 0)),
            pl.BlockSpec((width, step), lambda i: (0, i)),
            pl.BlockSpec((width, step), lambda i: (0, i + n)),
        ],
        out_specs=[out, out, out],
        out_shape=[shape(rows, inner), shape(rows, inner, F32), shape(rows, inner, F32)],
        compiler_params=pltpu.CompilerParams(vmem_limit_bytes=48 * MB),
        cost_estimate=pl.CostEstimate(
            flops=4 * rows * width * inner, bytes_accessed=4 * width * inner, transcendentals=0
        ),
    )(X, gate_up, gate_up)


def dh_step(g0, g1, g2, g3, wd, slope, silu, *rest):
    dact, whole = rest[-2:]

    @pl.when(pl.program_id(0) == 0)
    def _():
        for k, piece in enumerate((g0, g1, g2, g3)):
            whole[k * CAP : k * CAP + CAP, :] = piece[...]

    dh = wide_dot(whole[...], wd[...])
    dact[0] = (dh * slope[...]).astype(BF)
    dact[1] = (dh * silu[...]).astype(BF)


def dh_call(gs, down_proj, slope, silu, after):
    inner, width = down_proj.shape
    rows = slope.shape[0]
    step = 256
    part = pl.BlockSpec((rows, step), lambda i: (0, i))
    return pl.pallas_call(
        dh_step,
        grid=(inner // step,),
        in_specs=[pl.BlockSpec((CAP, width), lambda i: (0, 0))] * 4
        + [pl.BlockSpec((step, width), lambda i: (i, 0)), part, part]
        + [pl.BlockSpec(memory_space=pl.ANY)] * len(after),
        out_specs=pl.BlockSpec((2, rows, step), lambda i: (0, 0, i)),
        out_shape=jax.ShapeDtypeStruct((2, rows, inner), BF),
        scratch_shapes=[pltpu.VMEM((rows, width), BF)],
        compiler_params=pltpu.CompilerParams(vmem_limit_bytes=48 * MB),
        cost_estimate=pl.CostEstimate(
            flops=2 * rows * width * inner, bytes_accessed=2 * width * inner, transcendentals=0
        ),
    )(*gs, down_proj, slope, silu, *after)


def back_step(at, dact, wt, *rest):
    out, inner = rest[-1], dact.shape[2]
    got = wide_dot(dact[0], wt[:, :inner]) + wide_dot(dact[1], wt[:, inner:])
    for k in range(4):
        out[jnp.bitwise_xor(at[3], k)] = got[k * CAP : k * CAP + CAP].astype(BF)


def back_call(at, dact, gate_up, after):
    rows, inner = dact.shape[1:]
    width = gate_up.shape[0]
    step = 512
    return pl.pallas_call(
        back_step,
        grid=(width // step,),
        in_specs=[SMEM, pl.BlockSpec((2, rows, inner), lambda i: (0, 0, 0))]
        + [pl.BlockSpec((step, 2 * inner), lambda i: (i, 0))]
        + [pl.BlockSpec(memory_space=pl.ANY)] * len(after),
        out_specs=pl.BlockSpec((4, CAP, step), lambda i: (0, 0, i)),
        out_shape=jax.ShapeDtypeStruct((4, CAP, width), BF),
        compiler_params=pltpu.CompilerParams(vmem_limit_bytes=48 * MB),
        cost_estimate=pl.CostEstimate(
            flops=4 * rows * width * inner, bytes_accessed=4 * width * inner, transcendentals=0
        ),
    )(at, dact, gate_up, *after)


def tok_step(at, mask, arrived, out, whole):
    for k in range(4):
        whole[k * CAP : k * CAP + CAP, :] = arrived[jnp.bitwise_xor(at[3], k)]
    out[...] = jnp.dot(mask[...], whole[...], preferred_element_type=F32).astype(BF)


def tile_step(at, *refs):
    xs, ds, outs, xall, dall = refs[:4], refs[4:8], refs[-6:-2], refs[-2], refs[-1]
    rows, inner = ds[0].shape[1:]
    for p in range(4):
        part = slice(p * rows, p * rows + rows)
        xall[part, :] = xs[p][...]
        for h in range(2):
            dall[part, h * inner : h * inner + inner] = ds[p][h]
    for j in (1, 2, 3, 0):
        other = lax.rem(at[2] + j, 4)
        for b in range(2):
            got = rows_dot(xall[:, aligned(b * 4 + other, 128)], dall[...])
            outs[j][b * 128 : b * 128 + 128, :] = got.astype(outs[j].dtype)


def tile_call(at, xs, ds, after):
    rows, part = xs[0].shape
    wide = 2 * ds[0].shape[2]
    return call(
        tile_step,
        [shape(256, wide, F32)] + [shape(256, wide)] * 3,
        9,
        [pltpu.VMEM((4 * rows, part), BF), pltpu.VMEM((4 * rows, wide), BF)],
        flops=8 * rows * part * wide,
        moved=8 * rows * (part + wide),
        after=len(after),
        limit=12,
    )(at, *xs, *ds, *after)


def down_step(at, both, *rest):
    outs, gall, hall, total = rest[-7:-3], rest[-3], rest[-2], rest[-1]
    rows, part, inner = both.shape[1], gall.shape[1], hall.shape[1]
    for i in range(4):
        gall[i * rows : i * rows + rows, :] = both[i, :, :part]
        hall[i * rows : i * rows + rows, :] = both[i, :, part:]
    for b in range(inner // 128):
        cols = slice(b * 128, b * 128 + 128)
        total[cols, :] = rows_dot(hall[:, cols], gall[...])
    for j in (1, 2, 3, 0):
        other = lax.rem(at[1] + j, 4)
        for b in range(2):
            outs[j][b * 96 : b * 96 + 96, :] = total[aligned(b * 4 + other, 96), :].astype(outs[j].dtype)


def down_call(at, both, part, after):
    rows, inner = both.shape[1], both.shape[2] - part
    return call(
        down_step,
        [shape(192, part, F32)] + [shape(192, part)] * 3,
        2,
        [
            pltpu.VMEM((4 * rows, part), BF),
            pltpu.VMEM((4 * rows, inner), BF),
            pltpu.VMEM((inner, part), F32),
        ],
        flops=8 * rows * part * inner,
        moved=8 * rows * (part + inner),
        after=len(after),
        limit=16,
    )(at, both, *after)


def sum_step(at, *refs):
    parts, keep, send = refs[:4], refs[-2], refs[-1]
    half = keep.shape[0]

    def part(i):
        rows = aligned(i, half)
        return sum((r[rows, :].astype(F32) for r in parts[1:]), parts[0][rows, :])

    send[...] = part(1 - at[0]).astype(BF)
    keep[...] = part(at[0])


def sum_call(at, parts, after):
    rows, cols = parts[0].shape
    outs = [shape(rows // 2, cols, F32), shape(rows // 2, cols)]
    return call(sum_step, outs, 5, moved=10 * rows * cols, after=len(after))(at, *parts, *after)


def shards(tokens, cotangent, routes, gates, gate_up, down_proj):
    gate_up, down_proj = gate_up[0], down_proj[0]
    w, x, y = lax.axis_index("w"), lax.axis_index("x"), lax.axis_index("y")
    me = lax.axis_index(("v", "c"))
    at = jnp.stack([w, x, y, me]).astype(jnp.int32)
    toks, width = tokens.shape
    inner = down_proj.shape[0]
    experts = jnp.bitwise_xor(me, jnp.arange(4, dtype=jnp.int32))
    matches = routes[:, :, None] == experts[None, None, :]
    member = jnp.any(matches, axis=1)
    weight = jnp.sum(jnp.where(matches, gates[:, :, None], F32(0.0)), axis=1)
    position = jnp.cumsum(member.astype(jnp.int32), axis=0) - 1
    select = member[:, :, None] & (
        position[:, :, None] == jnp.arange(CAP, dtype=jnp.int32)[None, None, :]
    )
    mask = select.astype(BF).reshape(toks, 4 * CAP)
    slot_gate = jnp.sum(jnp.where(select, weight[:, :, None], F32(0.0)), axis=0).reshape(4 * CAP, 1)
    send_x = rows_dot(mask, tokens).astype(BF).reshape(4, CAP, width)
    send_g = (rows_dot(mask, cotangent) * slot_gate).astype(BF).reshape(4, CAP, width)
    rows = 4 * CAP
    xs = [send_x[0]] + [swap_expert(send_x[k], k) for k in (1, 2, 3)]
    gs = [send_g[0]] + [swap_expert(send_g[k], k) for k in (1, 2, 3)]

    part = width // 4
    packed = call(
        pack_x, [shape(rows, part)] * 4 + [shape(rows, width)], 5, moved=4 * rows * width
    )(at, *xs)
    xa = [shift(packed[j], "x", j) for j in range(4)]
    hidden, slope, silu = act_call(packed[4], gate_up, inner)
    dact = dh_call(gs, down_proj, slope, silu, xa[1:])
    da = [shift(dact, "x", j) for j in range(4)]
    sent = call(
        pack_g,
        [jax.ShapeDtypeStruct((4, rows, part + inner), BF)],
        5,
        moved=4 * rows * width,
        scalars=0,
        after=1,
    )(*gs, hidden, dact)[0]
    both = lax.all_to_all(sent, "y", split_axis=0, concat_axis=0, tiled=True)
    parts = tile_call(at, xa, da, [])
    gate = [parts[0]] + [shift(parts[j], "y", j) for j in (1, 2, 3)]
    back = back_call(at, dact, gate_up, [da[1], sent])
    arrived = lax.all_to_all(back, ("v", "c"), split_axis=0, concat_axis=0, tiled=True)
    token_grad = call(
        tok_step,
        [shape(toks, width)],
        3,
        [pltpu.VMEM((rows, width), BF)],
        flops=2 * toks * rows * width,
        moved=2 * (rows + toks) * width,
    )(at, mask, arrived)[0]
    parts = down_call(at, both, part, [])
    down = [parts[0]] + [shift(parts[j], "x", j) for j in (1, 2, 3)]

    keep, send = sum_call(at, down, [])
    down_grad = (keep + swap_w(send).astype(F32)).astype(BF).reshape(4, 24, part)
    down_grad = lax.all_to_all(down_grad, "y", split_axis=0, concat_axis=0, tiled=True)
    down_grad = jnp.concatenate([down_grad[i] for i in range(4)], axis=1)

    keep, send = sum_call(at, gate, [token_grad])
    gate_up_grad = (keep + swap_w(send).astype(F32)).astype(BF)
    return token_grad, gate_up_grad[None], down_grad[None]


def solution(mesh):
    fine = Mesh(mesh.devices.reshape(2, 4, 4, 2, 2), AXES)
    rows, expert, dp = P(AXES, None), ("v", "c"), ("w", "x", "y")
    in_specs = (rows, rows, rows, rows, P(expert, None, None), P(expert, None, None))
    out_specs = (rows, P(expert, dp, None), P(expert, dp, None))
    return jax.shard_map(
        shards, mesh=fine, in_specs=in_specs, out_specs=out_specs, check_vma=False
    )
```

```python
import functools

import jax
import jax.numpy as jnp
from jax import lax
from jax.experimental import pallas as pl
from jax.experimental.pallas import tpu as pltpu
from jax.sharding import Mesh, PartitionSpec as P

CAP = 48
BF = jnp.bfloat16
F32 = jnp.float32
AXES = ("w", "x", "y", "v", "c")
VMEM = pl.BlockSpec(memory_space=pltpu.VMEM)
SMEM = pl.BlockSpec(memory_space=pltpu.SMEM)
MB = 1024 * 1024


def swap_expert(a, k):
    return lax.ppermute(a, ("v", "c"), [(i, i ^ k) for i in range(4)])


def shift(a, axis, j):
    if j == 0:
        return a
    return lax.ppermute(a, axis, [(i, (i + j) % 4) for i in range(4)])


def swap_w(a):
    return lax.ppermute(a, "w", [(0, 1), (1, 0)])


def rows_dot(a, b):
    return lax.dot_general(a, b, (((0,), (0,)), ((), ())), preferred_element_type=F32)


def wide_dot(a, b):
    return lax.dot_general(a, b, (((1,), (1,)), ((), ())), preferred_element_type=F32)


def shape(rows, cols, dtype=BF):
    return jax.ShapeDtypeStruct((rows, cols), dtype)


def call(body, outs, ins, scratch=(), flops=0, moved=0, scalars=1, after=0, limit=8):
    return pl.pallas_call(
        body,
        out_shape=outs,
        in_specs=[SMEM] * scalars + [VMEM] * (ins - scalars) + [pl.BlockSpec(memory_space=pl.ANY)] * after,
        out_specs=[VMEM] * len(outs),
        scratch_shapes=list(scratch),
        compiler_params=pltpu.CompilerParams(vmem_limit_bytes=limit * MB),
        cost_estimate=pl.CostEstimate(flops=flops, bytes_accessed=moved, transcendentals=0),
    )


def aligned(i, size):
    return pl.ds(pl.multiple_of(i * size, size), size)


def pack_x(at, x0, x1, x2, x3, *outs):
    whole = outs[4]
    for k, piece in enumerate((x0, x1, x2, x3)):
        rows = slice(k * CAP, k * CAP + CAP)
        whole[rows, :] = piece[...]
        for j in range(4):
            for b in range(2):
                cols = aligned(b * 4 + lax.rem(at[1] + j, 4), 512)
                outs[j][rows, b * 512 : b * 512 + 512] = piece[:, cols]


def pack_g(g0, g1, g2, g3, hidden, *rest):
    out, part = rest[-1], g0.shape[1] // 4
    for i in range(4):
        for k, piece in enumerate((g0, g1, g2, g3)):
            out[i, k * CAP : k * CAP + CAP, :part] = piece[:, i * part : i * part + part]
        out[i, :, part:] = hidden[...]


def act_step(x, wg, wu, hidden, slope, silu):
    gpart = jnp.dot(x[...], wg[...], preferred_element_type=F32)
    upart = jnp.dot(x[...], wu[...], preferred_element_type=F32)
    sig = jax.nn.sigmoid(gpart)
    soft = gpart * sig
    hidden[...] = (soft * upart).astype(BF)
    slope[...] = upart * (sig * (1.0 + gpart * (1.0 - sig)))
    silu[...] = soft


def act_call(X, gate_up, inner):
    rows, width = X.shape
    step = 256
    n = inner // step
    out = pl.BlockSpec((rows, step), lambda i: (0, i))
    return pl.pallas_call(
        act_step,
        grid=(n,),
        in_specs=[
            pl.BlockSpec((rows, width), lambda i: (0, 0)),
            pl.BlockSpec((width, step), lambda i: (0, i)),
            pl.BlockSpec((width, step), lambda i: (0, i + n)),
        ],
        out_specs=[out, out, out],
        out_shape=[shape(rows, inner), shape(rows, inner, F32), shape(rows, inner, F32)],
        compiler_params=pltpu.CompilerParams(vmem_limit_bytes=48 * MB),
        cost_estimate=pl.CostEstimate(
            flops=4 * rows * width * inner, bytes_accessed=4 * width * inner, transcendentals=0
        ),
    )(X, gate_up, gate_up)


def dh_step(g0, g1, g2, g3, wd, slope, silu, *rest):
    dact_g, dact_u, whole = rest[-3:]

    @pl.when(pl.program_id(0) == 0)
    def _():
        for k, piece in enumerate((g0, g1, g2, g3)):
            whole[k * CAP : k * CAP + CAP, :] = piece[...]

    dh = wide_dot(whole[...], wd[...])
    dact_g[...] = (dh * slope[...]).astype(BF)
    dact_u[...] = (dh * silu[...]).astype(BF)


def dh_call(gs, down_proj, slope, silu, after):
    inner, width = down_proj.shape
    rows = slope.shape[0]
    step = 256
    part = pl.BlockSpec((rows, step), lambda i: (0, i))
    return pl.pallas_call(
        dh_step,
        grid=(inner // step,),
        in_specs=[pl.BlockSpec((CAP, width), lambda i: (0, 0))] * 4
        + [pl.BlockSpec((step, width), lambda i: (i, 0)), part, part]
        + [pl.BlockSpec(memory_space=pl.ANY)] * len(after),
        out_specs=[part, part],
        out_shape=[shape(rows, inner)] * 2,
        scratch_shapes=[pltpu.VMEM((rows, width), BF)],
        compiler_params=pltpu.CompilerParams(vmem_limit_bytes=48 * MB),
        cost_estimate=pl.CostEstimate(
            flops=2 * rows * width * inner, bytes_accessed=2 * width * inner, transcendentals=0
        ),
    )(*gs, down_proj, slope, silu, *after)


def back_step(at, dg, du, wt, *rest):
    out, inner = rest[-1], dg.shape[1]
    got = wide_dot(dg[...], wt[:, :inner]) + wide_dot(du[...], wt[:, inner:])
    for k in range(4):
        out[jnp.bitwise_xor(at[3], k)] = got[k * CAP : k * CAP + CAP].astype(BF)


def back_call(at, dg, du, gate_up, after):
    rows, inner = dg.shape
    width = gate_up.shape[0]
    step = 512
    return pl.pallas_call(
        back_step,
        grid=(width // step,),
        in_specs=[SMEM]
        + [pl.BlockSpec((rows, inner), lambda i: (0, 0))] * 2
        + [pl.BlockSpec((step, 2 * inner), lambda i: (i, 0))]
        + [pl.BlockSpec(memory_space=pl.ANY)] * len(after),
        out_specs=pl.BlockSpec((4, CAP, step), lambda i: (0, 0, i)),
        out_shape=jax.ShapeDtypeStruct((4, CAP, width), BF),
        compiler_params=pltpu.CompilerParams(vmem_limit_bytes=48 * MB),
        cost_estimate=pl.CostEstimate(
            flops=4 * rows * width * inner, bytes_accessed=4 * width * inner, transcendentals=0
        ),
    )(at, dg, du, gate_up, *after)


def tok_step(at, mask, arrived, out, whole):
    for k in range(4):
        whole[k * CAP : k * CAP + CAP, :] = arrived[jnp.bitwise_xor(at[3], k)]
    out[...] = jnp.dot(mask[...], whole[...], preferred_element_type=F32).astype(BF)


def tile_step(at, *refs):
    xs, ds, outs, xall, dall = refs[:4], refs[4:8], refs[-6:-2], refs[-2], refs[-1]
    rows = xs[0].shape[0]
    for p in range(4):
        xall[p * rows : p * rows + rows, :] = xs[p][...]
        dall[p * rows : p * rows + rows, :] = ds[p][...]
    for j in (1, 2, 3, 0):
        other = lax.rem(at[2] + j, 4)
        for b in range(2):
            got = rows_dot(xall[:, aligned(b * 4 + other, 128)], dall[...])
            outs[j][b * 128 : b * 128 + 128, :] = got.astype(outs[j].dtype)


def tile_call(at, xs, ds, after):
    rows, part = xs[0].shape
    inner = ds[0].shape[1]
    return call(
        tile_step,
        [shape(256, inner, F32)] + [shape(256, inner)] * 3,
        9,
        [pltpu.VMEM((4 * rows, part), BF), pltpu.VMEM((4 * rows, inner), BF)],
        flops=8 * rows * part * inner,
        moved=8 * rows * (part + inner),
        after=len(after),
        limit=12,
    )(at, *xs, *ds, *after)


def down_step(at, both, *rest):
    outs, gall, hall, total = rest[-7:-3], rest[-3], rest[-2], rest[-1]
    rows, part, inner = both.shape[1], gall.shape[1], hall.shape[1]
    for i in range(4):
        gall[i * rows : i * rows + rows, :] = both[i, :, :part]
        hall[i * rows : i * rows + rows, :] = both[i, :, part:]
    for b in range(inner // 128):
        cols = slice(b * 128, b * 128 + 128)
        total[cols, :] = rows_dot(hall[:, cols], gall[...])
    for j in (1, 2, 3, 0):
        other = lax.rem(at[1] + j, 4)
        for b in range(2):
            outs[j][b * 96 : b * 96 + 96, :] = total[aligned(b * 4 + other, 96), :].astype(outs[j].dtype)


def down_call(at, both, part, after):
    rows, inner = both.shape[1], both.shape[2] - part
    return call(
        down_step,
        [shape(192, part, F32)] + [shape(192, part)] * 3,
        2,
        [
            pltpu.VMEM((4 * rows, part), BF),
            pltpu.VMEM((4 * rows, inner), BF),
            pltpu.VMEM((inner, part), F32),
        ],
        flops=8 * rows * part * inner,
        moved=8 * rows * (part + inner),
        after=len(after),
        limit=16,
    )(at, both, *after)


def sum_step(at, *refs):
    parts, keep, send = refs[:4], refs[-2], refs[-1]
    half = keep.shape[0]

    def part(i):
        rows = aligned(i, half)
        return sum((r[rows, :].astype(F32) for r in parts[1:]), parts[0][rows, :])

    send[...] = part(1 - at[0]).astype(BF)
    keep[...] = part(at[0])


def sum_call(at, parts, after):
    rows, cols = parts[0].shape
    outs = [shape(rows // 2, cols, F32), shape(rows // 2, cols)]
    return call(sum_step, outs, 5, moved=10 * rows * cols, after=len(after))(at, *parts, *after)


def shards(tokens, cotangent, routes, gates, gate_up, down_proj):
    gate_up, down_proj = gate_up[0], down_proj[0]
    w, x, y = lax.axis_index("w"), lax.axis_index("x"), lax.axis_index("y")
    me = lax.axis_index(("v", "c"))
    at = jnp.stack([w, x, y, me]).astype(jnp.int32)
    toks, width = tokens.shape
    inner = down_proj.shape[0]
    experts = jnp.bitwise_xor(me, jnp.arange(4, dtype=jnp.int32))
    matches = routes[:, :, None] == experts[None, None, :]
    member = jnp.any(matches, axis=1)
    weight = jnp.sum(jnp.where(matches, gates[:, :, None], F32(0.0)), axis=1)
    position = jnp.cumsum(member.astype(jnp.int32), axis=0) - 1
    select = member[:, :, None] & (
        position[:, :, None] == jnp.arange(CAP, dtype=jnp.int32)[None, None, :]
    )
    mask = select.astype(BF).reshape(toks, 4 * CAP)
    slot_gate = jnp.sum(jnp.where(select, weight[:, :, None], F32(0.0)), axis=0).reshape(4 * CAP, 1)
    send_x = rows_dot(mask, tokens).astype(BF).reshape(4, CAP, width)
    send_g = (rows_dot(mask, cotangent) * slot_gate).astype(BF).reshape(4, CAP, width)
    rows = 4 * CAP
    xs = [send_x[0]] + [swap_expert(send_x[k], k) for k in (1, 2, 3)]
    gs = [send_g[0]] + [swap_expert(send_g[k], k) for k in (1, 2, 3)]

    part = width // 4
    packed = call(
        pack_x, [shape(rows, part)] * 4 + [shape(rows, width)], 5, moved=4 * rows * width
    )(at, *xs)
    xa = [shift(packed[j], "x", j) for j in range(4)]
    hidden, slope, silu = act_call(packed[4], gate_up, inner)
    sent = call(
        pack_g,
        [jax.ShapeDtypeStruct((4, rows, part + inner), BF)],
        5,
        moved=4 * rows * width,
        scalars=0,
        after=2,
    )(*gs, hidden, xa[1], xa[3])[0]
    dact_g, dact_u = dh_call(gs, down_proj, slope, silu, [sent])
    da_g = [shift(dact_g, "x", j) for j in range(4)]
    da_u = [shift(dact_u, "x", j) for j in range(4)]
    both = lax.all_to_all(sent, "y", split_axis=0, concat_axis=0, tiled=True)
    def half(ds, after):
        parts = tile_call(at, xa, ds, after)
        return [parts[0]] + [shift(parts[j], "y", j) for j in (1, 2, 3)]

    back = back_call(at, dact_g, dact_u, gate_up, [da_g[1]])
    gate = half(da_g, [back])
    up = half(da_u, [])
    parts = down_call(at, both, part, [up[0]])
    down = [parts[0]] + [shift(parts[j], "x", j) for j in (1, 2, 3)]

    arrived = lax.all_to_all(back, ("v", "c"), split_axis=0, concat_axis=0, tiled=True)
    token_grad = call(
        tok_step,
        [shape(toks, width)],
        3,
        [pltpu.VMEM((rows, width), BF)],
        flops=2 * toks * rows * width,
        moved=2 * (rows + toks) * width,
    )(at, mask, arrived)[0]
    keep, send = sum_call(at, down, [])
    down_grad = (keep + swap_w(send).astype(F32)).astype(BF).reshape(4, 24, part)
    cols = [
        shift(lax.dynamic_index_in_dim(down_grad, (y + j) % 4, 0, False), "y", j) for j in range(4)
    ]
    turned = jnp.stack(cols[::-1] + cols[::-1])
    mine = lax.dynamic_slice_in_dim(turned, 3 - y, 4, 0)
    down_grad = jnp.concatenate([mine[i] for i in range(4)], axis=1)

    def last(parts, after):
        keep, send = sum_call(at, parts, after)
        return (keep + swap_w(send).astype(F32)).astype(BF)

    gate_up_grad = jnp.concatenate([last(gate, []), last(up, [])], axis=1)
    return token_grad, gate_up_grad[None], down_grad[None]


def solution(mesh):
    fine = Mesh(mesh.devices.reshape(2, 4, 4, 2, 2), AXES)
    rows, expert, dp = P(AXES, None), ("v", "c"), ("w", "x", "y")
    in_specs = (rows, rows, rows, rows, P(expert, None, None), P(expert, None, None))
    out_specs = (rows, P(expert, dp, None), P(expert, dp, None))
    return jax.shard_map(
        shards, mesh=fine, in_specs=in_specs, out_specs=out_specs, check_vma=False
    )
```

```python
import functools

import jax
import jax.numpy as jnp
from jax import lax
from jax.experimental import pallas as pl
from jax.experimental.pallas import tpu as pltpu
from jax.sharding import Mesh, PartitionSpec as P

CAP = 48
BF = jnp.bfloat16
F32 = jnp.float32
AXES = ("w", "x", "y", "v", "c")
VMEM = pl.BlockSpec(memory_space=pltpu.VMEM)
SMEM = pl.BlockSpec(memory_space=pltpu.SMEM)
MB = 1024 * 1024


def swap_expert(a, k):
    return lax.ppermute(a, ("v", "c"), [(i, i ^ k) for i in range(4)])


def shift(a, axis, j):
    if j == 0:
        return a
    return lax.ppermute(a, axis, [(i, (i + j) % 4) for i in range(4)])


def swap_w(a):
    return lax.ppermute(a, "w", [(0, 1), (1, 0)])


def rows_dot(a, b):
    return lax.dot_general(a, b, (((0,), (0,)), ((), ())), preferred_element_type=F32)


def wide_dot(a, b):
    return lax.dot_general(a, b, (((1,), (1,)), ((), ())), preferred_element_type=F32)


def shape(rows, cols, dtype=BF):
    return jax.ShapeDtypeStruct((rows, cols), dtype)


def call(body, outs, ins, scratch=(), flops=0, moved=0, scalars=1, after=0, limit=8):
    return pl.pallas_call(
        body,
        out_shape=outs,
        in_specs=[SMEM] * scalars + [VMEM] * (ins - scalars) + [pl.BlockSpec(memory_space=pl.ANY)] * after,
        out_specs=[VMEM] * len(outs),
        scratch_shapes=list(scratch),
        compiler_params=pltpu.CompilerParams(vmem_limit_bytes=limit * MB),
        cost_estimate=pl.CostEstimate(flops=flops, bytes_accessed=moved, transcendentals=0),
    )


def aligned(i, size):
    return pl.ds(pl.multiple_of(i * size, size), size)


def pack_x(at, x0, x1, x2, x3, *outs):
    whole = outs[4]
    for k, piece in enumerate((x0, x1, x2, x3)):
        rows = slice(k * CAP, k * CAP + CAP)
        whole[rows, :] = piece[...]
        for j in range(4):
            for b in range(2):
                cols = aligned(b * 4 + lax.rem(at[1] + j, 4), 512)
                outs[j][rows, b * 512 : b * 512 + 512] = piece[:, cols]


def pack_g(g0, g1, g2, g3, hidden, *rest):
    out, part = rest[-1], g0.shape[1] // 4
    for i in range(4):
        for k, piece in enumerate((g0, g1, g2, g3)):
            out[i, k * CAP : k * CAP + CAP, :part] = piece[:, i * part : i * part + part]
        out[i, :, part:] = hidden[...]


def fetch(pieces, buf, sems):
    copies = [
        pltpu.make_async_copy(piece, buf.at[i], sems.at[i]) for i, piece in enumerate(pieces)
    ]
    for copy in copies:
        copy.start()
    return copies


def act_step(x, weights, hidden, slope, silu, buf, sems):
    inner = hidden.shape[1]
    step = buf.shape[2]
    n = inner // step
    copies = fetch(
        [weights.at[:, pl.ds(h * inner + i * step, step)] for i in range(n) for h in range(2)],
        buf,
        sems,
    )
    for i in range(n):
        cols = slice(i * step, i * step + step)
        copies[2 * i].wait()
        gpart = jnp.dot(x[...], buf[2 * i], preferred_element_type=F32)
        copies[2 * i + 1].wait()
        upart = jnp.dot(x[...], buf[2 * i + 1], preferred_element_type=F32)
        sig = jax.nn.sigmoid(gpart)
        soft = gpart * sig
        hidden[:, cols] = (soft * upart).astype(BF)
        slope[:, cols] = upart * (sig * (1.0 + gpart * (1.0 - sig)))
        silu[:, cols] = soft


def weigh(body, outs, ins, weights, scratch, flops, limit, after, scalars=0):
    return pl.pallas_call(
        body,
        out_shape=outs,
        in_specs=[SMEM] * scalars
        + [VMEM] * ins
        + [pl.BlockSpec(memory_space=pltpu.HBM)]
        + [pl.BlockSpec(memory_space=pl.ANY)] * after,
        out_specs=[VMEM] * len(outs),
        scratch_shapes=scratch,
        compiler_params=pltpu.CompilerParams(vmem_limit_bytes=limit * MB),
        cost_estimate=pl.CostEstimate(
            flops=flops, bytes_accessed=2 * weights.size, transcendentals=0
        ),
    )


def act_call(X, gate_up, inner):
    rows, width = X.shape
    step = 256
    n = 2 * inner // step
    outs = [shape(rows, inner), shape(rows, inner, F32), shape(rows, inner, F32)]
    scratch = [pltpu.VMEM((n, width, step), BF), pltpu.SemaphoreType.DMA((n,))]
    flops = 4 * rows * width * inner
    return weigh(act_step, outs, 1, gate_up, scratch, flops, 18, 0)(X, gate_up)


def dh_step(g0, g1, g2, g3, slope, silu, weights, *rest):
    dact_g, dact_u, whole, buf, sems = rest[-5:]
    step = buf.shape[1]
    n = buf.shape[0]
    copies = fetch([weights.at[pl.ds(i * step, step), :] for i in range(n)], buf, sems)
    for k, piece in enumerate((g0, g1, g2, g3)):
        whole[k * CAP : k * CAP + CAP, :] = piece[...]
    for i in range(n):
        cols = slice(i * step, i * step + step)
        copies[i].wait()
        dh = wide_dot(whole[...], buf[i])
        dact_g[:, cols] = (dh * slope[:, cols]).astype(BF)
        dact_u[:, cols] = (dh * silu[:, cols]).astype(BF)


def dh_call(gs, down_proj, slope, silu, after):
    inner, width = down_proj.shape
    rows = slope.shape[0]
    step = 256
    n = inner // step
    scratch = [
        pltpu.VMEM((rows, width), BF),
        pltpu.VMEM((n, step, width), BF),
        pltpu.SemaphoreType.DMA((n,)),
    ]
    flops = 2 * rows * width * inner
    return weigh(dh_step, [shape(rows, inner)] * 2, 6, down_proj, scratch, flops, 14, len(after))(
        *gs, slope, silu, down_proj, *after
    )


def back_step(at, dg, du, weights, out, passed, buf, sems):
    inner, step, n = dg.shape[1], buf.shape[1], buf.shape[0]
    copies = fetch([weights.at[pl.ds(i * step, step), :] for i in range(n)], buf, sems)
    passed[...] = du[...]
    for i in range(n):
        copies[i].wait()
        got = wide_dot(dg[...], buf[i, :, :inner]) + wide_dot(du[...], buf[i, :, inner:])
        for k in range(4):
            out[jnp.bitwise_xor(at[3], k), :, i * step : i * step + step] = got[
                k * CAP : k * CAP + CAP
            ].astype(BF)


def back_call(at, dg, du, gate_up):
    rows, inner = dg.shape
    width = gate_up.shape[0]
    step = 512
    n = width // step
    outs = [jax.ShapeDtypeStruct((4, CAP, width), BF), shape(rows, inner)]
    scratch = [pltpu.VMEM((n, step, 2 * inner), BF), pltpu.SemaphoreType.DMA((n,))]
    flops = 4 * rows * width * inner
    return weigh(back_step, outs, 2, gate_up, scratch, flops, 18, 0, 1)(at, dg, du, gate_up)


def tok_step(at, mask, arrived, out, whole):
    for k in range(4):
        whole[k * CAP : k * CAP + CAP, :] = arrived[jnp.bitwise_xor(at[3], k)]
    out[...] = jnp.dot(mask[...], whole[...], preferred_element_type=F32).astype(BF)


def tile_step(at, *refs):
    xs, ds, outs, xall, dall = refs[:4], refs[4:8], refs[-6:-2], refs[-2], refs[-1]
    rows = xs[0].shape[0]
    for p in range(4):
        xall[p * rows : p * rows + rows, :] = xs[p][...]
        dall[p * rows : p * rows + rows, :] = ds[p][...]
    for j in (1, 2, 3, 0):
        other = lax.rem(at[2] + j, 4)
        for b in range(2):
            got = rows_dot(xall[:, aligned(b * 4 + other, 128)], dall[...])
            outs[j][b * 128 : b * 128 + 128, :] = got.astype(outs[j].dtype)


def tile_call(at, xs, ds, after):
    rows, part = xs[0].shape
    inner = ds[0].shape[1]
    return call(
        tile_step,
        [shape(256, inner, F32)] + [shape(256, inner)] * 3,
        9,
        [pltpu.VMEM((4 * rows, part), BF), pltpu.VMEM((4 * rows, inner), BF)],
        flops=8 * rows * part * inner,
        moved=8 * rows * (part + inner),
        after=len(after),
        limit=12,
    )(at, *xs, *ds, *after)


def down_step(at, both, *rest):
    outs, gall, hall, total = rest[-7:-3], rest[-3], rest[-2], rest[-1]
    rows, part, inner = both.shape[1], gall.shape[1], hall.shape[1]
    for i in range(4):
        gall[i * rows : i * rows + rows, :] = both[i, :, :part]
        hall[i * rows : i * rows + rows, :] = both[i, :, part:]
    for b in range(inner // 128):
        cols = slice(b * 128, b * 128 + 128)
        total[cols, :] = rows_dot(hall[:, cols], gall[...])
    for j in (1, 2, 3, 0):
        other = lax.rem(at[1] + j, 4)
        for b in range(2):
            outs[j][b * 96 : b * 96 + 96, :] = total[aligned(b * 4 + other, 96), :].astype(outs[j].dtype)


def down_call(at, both, part, after):
    rows, inner = both.shape[1], both.shape[2] - part
    return call(
        down_step,
        [shape(192, part, F32)] + [shape(192, part)] * 3,
        2,
        [
            pltpu.VMEM((4 * rows, part), BF),
            pltpu.VMEM((4 * rows, inner), BF),
            pltpu.VMEM((inner, part), F32),
        ],
        flops=8 * rows * part * inner,
        moved=8 * rows * (part + inner),
        after=len(after),
        limit=16,
    )(at, both, *after)


def sum_step(at, *refs):
    parts, keep, send = refs[:4], refs[-2], refs[-1]
    half = keep.shape[0]

    def part(i):
        rows = aligned(i, half)
        return sum((r[rows, :].astype(F32) for r in parts[1:]), parts[0][rows, :])

    send[...] = part(1 - at[0]).astype(BF)
    keep[...] = part(at[0])


def sum_call(at, parts, after):
    rows, cols = parts[0].shape
    outs = [shape(rows // 2, cols, F32), shape(rows // 2, cols)]
    return call(sum_step, outs, 5, moved=10 * rows * cols, after=len(after))(at, *parts, *after)


def shards(tokens, cotangent, routes, gates, gate_up, down_proj):
    gate_up, down_proj = gate_up[0], down_proj[0]
    w, x, y = lax.axis_index("w"), lax.axis_index("x"), lax.axis_index("y")
    me = lax.axis_index(("v", "c"))
    at = jnp.stack([w, x, y, me]).astype(jnp.int32)
    toks, width = tokens.shape
    inner = down_proj.shape[0]
    experts = jnp.bitwise_xor(me, jnp.arange(4, dtype=jnp.int32))
    matches = routes[:, :, None] == experts[None, None, :]
    member = jnp.any(matches, axis=1)
    weight = jnp.sum(jnp.where(matches, gates[:, :, None], F32(0.0)), axis=1)
    position = jnp.cumsum(member.astype(jnp.int32), axis=0) - 1
    select = member[:, :, None] & (
        position[:, :, None] == jnp.arange(CAP, dtype=jnp.int32)[None, None, :]
    )
    mask = select.astype(BF).reshape(toks, 4 * CAP)
    slot_gate = jnp.sum(jnp.where(select, weight[:, :, None], F32(0.0)), axis=0).reshape(4 * CAP, 1)
    send_x = rows_dot(mask, tokens).astype(BF).reshape(4, CAP, width)
    send_g = (rows_dot(mask, cotangent) * slot_gate).astype(BF).reshape(4, CAP, width)
    rows = 4 * CAP
    xs = [send_x[0]] + [swap_expert(send_x[k], k) for k in (1, 2, 3)]
    gs = [send_g[0]] + [swap_expert(send_g[k], k) for k in (1, 2, 3)]

    part = width // 4
    packed = call(
        pack_x, [shape(rows, part)] * 4 + [shape(rows, width)], 5, moved=4 * rows * width
    )(at, *xs)
    xa = [shift(packed[j], "x", j) for j in range(4)]
    hidden, slope, silu = act_call(packed[4], gate_up, inner)
    sent = call(
        pack_g,
        [jax.ShapeDtypeStruct((4, rows, part + inner), BF)],
        5,
        moved=4 * rows * width,
        scalars=0,
        after=2,
    )(*gs, hidden, xa[1], xa[3])[0]
    dact_g, dact_u = dh_call(gs, down_proj, slope, silu, [sent])
    da_g = [shift(dact_g, "x", j) for j in range(4)]
    back, passed = back_call(at, dact_g, dact_u, gate_up)
    da_u = [shift(passed, "x", j) for j in range(4)]
    both = lax.all_to_all(sent, "y", split_axis=0, concat_axis=0, tiled=True)
    def half(ds, after):
        parts = tile_call(at, xa, ds, after)
        return [parts[0]] + [shift(parts[j], "y", j) for j in (1, 2, 3)]

    gate = half(da_g, [back])
    parts = down_call(at, both, part, [gate[0]])
    down = [parts[0]] + [shift(parts[j], "x", j) for j in (1, 2, 3)]

    up = half(da_u, [down[0]])
    arrived = lax.all_to_all(back, ("v", "c"), split_axis=0, concat_axis=0, tiled=True)
    token_grad = call(
        tok_step,
        [shape(toks, width)],
        3,
        [pltpu.VMEM((rows, width), BF)],
        flops=2 * toks * rows * width,
        moved=2 * (rows + toks) * width,
    )(at, mask, arrived)[0]
    keep, send = sum_call(at, down, [])
    down_grad = (keep + swap_w(send).astype(F32)).astype(BF).reshape(4, 24, part)
    cols = [
        shift(lax.dynamic_index_in_dim(down_grad, (y + j) % 4, 0, False), "y", j) for j in range(4)
    ]
    turned = jnp.stack(cols[::-1] + cols[::-1])
    mine = lax.dynamic_slice_in_dim(turned, 3 - y, 4, 0)
    down_grad = jnp.concatenate([mine[i] for i in range(4)], axis=1)

    def last(parts, after):
        keep, send = sum_call(at, parts, after)
        return (keep + swap_w(send).astype(F32)).astype(BF)

    gate_up_grad = jnp.concatenate([last(gate, []), last(up, [token_grad])], axis=1)
    return token_grad, gate_up_grad[None], down_grad[None]


def solution(mesh):
    fine = Mesh(mesh.devices.reshape(2, 4, 4, 2, 2), AXES)
    rows, expert, dp = P(AXES, None), ("v", "c"), ("w", "x", "y")
    in_specs = (rows, rows, rows, rows, P(expert, None, None), P(expert, None, None))
    out_specs = (rows, P(expert, dp, None), P(expert, dp, None))
    return jax.shard_map(
        shards, mesh=fine, in_specs=in_specs, out_specs=out_specs, check_vma=False
    )
```

```python
import jax
import jax.numpy as jnp
from jax import lax
from jax.experimental import pallas as pl
from jax.experimental.pallas import tpu as pltpu
from jax.sharding import Mesh, PartitionSpec as P

CAP = 48
BF = jnp.bfloat16
F32 = jnp.float32
MB = 1024 * 1024
AXES = ("w", "x", "y", "v", "c")
VMEM = pl.BlockSpec(memory_space=pltpu.VMEM)
SMEM = pl.BlockSpec(memory_space=pltpu.SMEM)
ANY = pl.BlockSpec(memory_space=pl.ANY)
HBM = pl.BlockSpec(memory_space=pltpu.HBM)
MARK = jax.ShapeDtypeStruct((8, 128), F32)


def swap_expert(a, k):
    return lax.ppermute(a, ("v", "c"), [(i, i ^ k) for i in range(4)])


def shift(a, axis, j):
    if j == 0:
        return a
    return lax.ppermute(a, axis, [(i, (i + j) % 4) for i in range(4)])


def swap_w(a):
    return lax.ppermute(a, "w", [(0, 1), (1, 0)])


def rows_dot(a, b):
    return lax.dot_general(a, b, (((0,), (0,)), ((), ())), preferred_element_type=F32)


def wide_dot(a, b):
    return lax.dot_general(a, b, (((1,), (1,)), ((), ())), preferred_element_type=F32)


def shape(*dims, dtype=BF):
    return jax.ShapeDtypeStruct(dims, dtype)


def aligned(i, size):
    return pl.ds(pl.multiple_of(i * size, size), size)


def call(body, ins, outs, scratch=(), flops=0, moved=0, limit=8, placed=()):
    specs = {"s": SMEM, "v": VMEM, "a": ANY}
    return pl.pallas_call(
        body,
        out_shape=[pltpu.HBM(o.shape, o.dtype) if i in placed else o for i, o in enumerate(outs)],
        in_specs=[specs[i] for i in ins],
        out_specs=[HBM if o in placed else VMEM for o in range(len(outs))],
        scratch_shapes=list(scratch),
        compiler_params=pltpu.CompilerParams(vmem_limit_bytes=limit * MB),
        cost_estimate=pl.CostEstimate(flops=flops, bytes_accessed=moved, transcendentals=0),
    )


def fetch(pairs, sems):
    copies = [pltpu.make_async_copy(s, d, sems.at[i]) for i, (s, d) in enumerate(pairs)]
    for copy in copies:
        copy.start()
    return copies


def land(pairs, sems):
    for copy in fetch(pairs, sems):
        copy.wait()


def sems(n):
    return pltpu.SemaphoreType.DMA((n,))


def pack_x(at, x0, x1, x2, x3, *outs):
    whole = outs[4]
    for k, piece in enumerate((x0, x1, x2, x3)):
        rows = slice(k * CAP, k * CAP + CAP)
        whole[rows, :] = piece[...]
        for j in range(4):
            for b in range(2):
                cols = aligned(b * 4 + lax.rem(at[1] + j, 4), 512)
                outs[j][rows, b * 512 : b * 512 + 512] = piece[:, cols]


def pack_g(g0, g1, g2, g3, hidden, *rest):
    out, mark, sem = rest[-3:]
    part, inner = g0.shape[1] // 4, hidden.shape[1]
    mark[...] = jnp.zeros_like(mark)
    pairs = []
    for i in range(4):
        for k, piece in enumerate((g0, g1, g2, g3)):
            to = out.at[i, pl.ds(k * CAP, CAP), pl.ds(0, part)]
            pairs.append((piece.at[:, pl.ds(i * part, part)], to))
        pairs.append((hidden, out.at[i, :, pl.ds(part, inner)]))
    land(pairs, sem)


def act_step(x, weights, hidden, slope, silu, buf, sem):
    inner, step = hidden.shape[1], buf.shape[2]
    n = inner // step
    cuts = [(i, h) for i in range(n) for h in range(2)]
    copies = fetch(
        [
            (weights.at[:, pl.ds(h * inner + i * step, step)], buf.at[2 * i + h])
            for i, h in cuts
        ],
        sem,
    )
    for i in range(n):
        cols = slice(i * step, i * step + step)
        copies[2 * i].wait()
        gpart = jnp.dot(x[...], buf[2 * i], preferred_element_type=F32)
        copies[2 * i + 1].wait()
        upart = jnp.dot(x[...], buf[2 * i + 1], preferred_element_type=F32)
        sig = jax.nn.sigmoid(gpart)
        soft = gpart * sig
        hidden[:, cols] = (soft * upart).astype(BF)
        slope[:, cols] = upart * (sig * (1.0 + gpart * (1.0 - sig)))
        silu[:, cols] = soft


def dh_step(g0, g1, g2, g3, slope, silu, weights, *rest):
    dact, whole, buf, sem, gsem = rest[-5:]
    n, step = buf.shape[:2]
    copies = fetch([(weights.at[pl.ds(i * step, step), :], buf.at[i]) for i in range(n)], sem)
    land([(g, whole.at[pl.ds(k * CAP, CAP), :]) for k, g in enumerate((g0, g1, g2, g3))], gsem)
    for i in range(n):
        cols = slice(i * step, i * step + step)
        copies[i].wait()
        dh = wide_dot(whole[...], buf[i])
        dact[0, :, cols] = (dh * slope[:, cols]).astype(BF)
        dact[1, :, cols] = (dh * silu[:, cols]).astype(BF)


def back_step(dact, weights, *rest):
    outs, mark, buf, sem = rest[-7:-3], *rest[-3:]
    n, step, inner = buf.shape[0], buf.shape[1], dact.shape[2]
    copies = fetch([(weights.at[pl.ds(i * step, step), :], buf.at[i]) for i in range(n)], sem)
    mark[...] = jnp.zeros_like(mark)
    for i in range(n):
        copies[i].wait()
        got = wide_dot(dact[0], buf[i, :, :inner]) + wide_dot(dact[1], buf[i, :, inner:])
        for k in range(4):
            outs[k][:, i * step : i * step + step] = got[k * CAP : k * CAP + CAP].astype(BF)


def tok_step(mask, a0, a1, a2, a3, out, mark, whole, sem):
    pieces = (a0, a1, a2, a3)
    land([(a, whole.at[pl.ds(k * CAP, CAP), :]) for k, a in enumerate(pieces)], sem)
    mark[...] = jnp.zeros_like(mark)
    out[...] = jnp.dot(mask[...], whole[...], preferred_element_type=F32).astype(BF)


def tile_step(*refs):
    xs, ds = refs[:4], refs[4:8]
    out, mark, xall, dall, buf, sem, osem = refs[-7:]
    rows = xs[0].shape[0]
    part = [pl.ds(p * rows, rows) for p in range(4)]
    inner = ds[0].shape[2]
    land(
        [(xs[p], xall.at[part[p], :]) for p in range(4)]
        + [
            (ds[p].at[h], dall.at[part[p], pl.ds(h * inner, inner)])
            for p in range(4)
            for h in range(2)
        ],
        sem,
    )
    mark[...] = jnp.zeros_like(mark)
    copies = []
    for j in range(4):
        for b in range(2):
            got = rows_dot(xall[:, b * 512 + j * 128 : b * 512 + j * 128 + 128], dall[...])
            buf[j, b * 128 : b * 128 + 128, :] = got.astype(BF)
        copies.append(pltpu.make_async_copy(buf.at[j], out.at[j], osem.at[j]))
        copies[-1].start()
    for copy in copies:
        copy.wait()


def tile_call(xs, ds, after):
    rows, part = xs[0].shape
    wide = 2 * ds[0].shape[2]
    return call(
        tile_step,
        "a" * (8 + len(after)),
        [shape(4, 256, wide), MARK],
        [
            pltpu.VMEM((4 * rows, part), BF),
            pltpu.VMEM((4 * rows, wide), BF),
            pltpu.VMEM((4, 256, wide), BF),
            sems(12),
            sems(4),
        ],
        flops=8 * rows * part * wide,
        moved=8 * rows * (part + wide),
        limit=16,
        placed=(0,),
    )(*xs, *ds, *after)


def down_step(at, both, *rest):
    outs, mark, gall, hall, total, sem = rest[-9:-5], *rest[-5:]
    rows, part, inner = both.shape[1], gall.shape[1], hall.shape[1]
    pairs = []
    for i in range(4):
        pairs.append((both.at[i, :, pl.ds(0, part)], gall.at[pl.ds(i * rows, rows), :]))
        pairs.append((both.at[i, :, pl.ds(part, inner)], hall.at[pl.ds(i * rows, rows), :]))
    land(pairs, sem)
    mark[...] = jnp.zeros_like(mark)
    for b in range(inner // 128):
        cols = slice(b * 128, b * 128 + 128)
        total[cols, :] = rows_dot(hall[:, cols], gall[...])
    for j in (1, 2, 3, 0):
        other = lax.rem(at[1] + j, 4)
        for b in range(2):
            outs[j][b * 96 : b * 96 + 96, :] = total[aligned(b * 4 + other, 96), :].astype(
                outs[j].dtype
            )


def gate_sum(at, parts, *rest):
    keep, send, g, sem = rest[-4:]
    half = keep.shape[0]
    land([(parts, g)], sem)

    def part(i):
        return sum(g[p, aligned(i, half), :].astype(F32) for p in range(4))

    send[...] = part(1 - at[0]).astype(BF)
    keep[...] = part(at[0])


def sum_step(at, own, r1, r2, r3, *rest):
    keep, send, f, g, sem = rest[-5:]
    half = keep.shape[0]
    land([(own, f), (r1, g.at[0]), (r2, g.at[1]), (r3, g.at[2])], sem)

    def part(i):
        rows = aligned(i, half)
        return f[rows, :] + sum(g[p, rows, :].astype(F32) for p in range(3))

    send[...] = part(1 - at[0]).astype(BF)
    keep[...] = part(at[0])


def sum_call(at, parts, after):
    rows, cols = parts[0].shape
    return call(
        sum_step,
        "saaaa" + "a" * len(after),
        [shape(rows // 2, cols, dtype=F32), shape(rows // 2, cols)],
        [pltpu.VMEM((rows, cols), F32), pltpu.VMEM((3, rows, cols), BF), sems(4)],
        moved=10 * rows * cols,
        limit=12,
    )(at, *parts, *after)


def shards(tokens, cotangent, routes, gates, gate_up, down_proj):
    gate_up = pltpu.with_memory_space_constraint(gate_up[0], pltpu.HBM)
    down_proj = pltpu.with_memory_space_constraint(down_proj[0], pltpu.HBM)
    w, x, y = lax.axis_index("w"), lax.axis_index("x"), lax.axis_index("y")
    me = lax.axis_index(("v", "c"))
    at = jnp.stack([w, x, y, me]).astype(jnp.int32)
    toks, width = tokens.shape
    inner = down_proj.shape[0]
    rows, part = 4 * CAP, width // 4
    experts = jnp.bitwise_xor(me, jnp.arange(4, dtype=jnp.int32))
    matches = routes[:, :, None] == experts[None, None, :]
    member = jnp.any(matches, axis=1)
    weight = jnp.sum(jnp.where(matches, gates[:, :, None], F32(0.0)), axis=1)
    position = jnp.cumsum(member.astype(jnp.int32), axis=0) - 1
    select = member[:, :, None] & (
        position[:, :, None] == jnp.arange(CAP, dtype=jnp.int32)[None, None, :]
    )
    mask = select.astype(BF).reshape(toks, rows)
    slot_gate = jnp.sum(jnp.where(select, weight[:, :, None], F32(0.0)), axis=0).reshape(rows, 1)
    send_x = rows_dot(mask, tokens).astype(BF).reshape(4, CAP, width)
    send_g = (rows_dot(mask, cotangent) * slot_gate).astype(BF).reshape(4, CAP, width)
    xs = [send_x[0]] + [swap_expert(send_x[k], k) for k in (1, 2, 3)]
    gs = [send_g[0]] + [swap_expert(send_g[k], k) for k in (1, 2, 3)]

    packed = call(
        pack_x, "svvvv", [shape(rows, part)] * 4 + [shape(rows, width)], moved=4 * rows * width
    )(at, *xs)
    xa = [shift(packed[j], "x", j) for j in range(4)]
    n = 2 * inner // 256
    hidden, slope, silu = call(
        act_step,
        "va",
        [shape(rows, inner), shape(rows, inner, dtype=F32), shape(rows, inner, dtype=F32)],
        [pltpu.VMEM((n, width, 256), BF), sems(n)],
        flops=4 * rows * width * inner,
        moved=4 * width * inner,
        limit=18,
    )(packed[4], gate_up)
    sent, sent_mark = call(
        pack_g,
        "aaaaaaa",
        [shape(4, rows, part + inner), MARK],
        [sems(20)],
        moved=4 * rows * width,
        placed=(0,),
    )(*gs, hidden, xa[1], xa[3])
    both = lax.all_to_all(sent, "y", split_axis=0, concat_axis=0, tiled=True)
    n = inner // 256
    dact = call(
        dh_step,
        "aaaavvaa",
        [shape(2, rows, inner)],
        [pltpu.VMEM((rows, width), BF), pltpu.VMEM((n, 256, width), BF), sems(n), sems(4)],
        flops=2 * rows * width * inner,
        moved=2 * width * inner,
        limit=12,
    )(*gs, slope, silu, down_proj, sent_mark)[0]
    da = [shift(dact, "x", j) for j in range(4)]
    n = width // 512
    *back, back_mark = call(
        back_step,
        "vaa",
        [shape(CAP, width)] * 4 + [MARK],
        [pltpu.VMEM((n, 512, 2 * inner), BF), sems(n)],
        flops=4 * rows * width * inner,
        moved=4 * width * inner,
        limit=18,
    )(dact, gate_up, da[1])
    *parts, mark = call(
        down_step,
        "saa",
        [shape(192, part, dtype=F32)] + [shape(192, part)] * 3 + [MARK],
        [
            pltpu.VMEM((4 * rows, part), BF),
            pltpu.VMEM((4 * rows, inner), BF),
            pltpu.VMEM((inner, part), F32),
            sems(8),
        ],
        flops=8 * rows * part * inner,
        moved=8 * rows * (part + inner),
        limit=16,
    )(at, both, back_mark)
    down = [parts[0]] + [shift(parts[j], "x", j) for j in (1, 2, 3)]
    parts, _ = tile_call(xa, da, [mark])
    gate = lax.all_to_all(parts, "y", split_axis=0, concat_axis=0, tiled=True)
    arrived = [back[0]] + [swap_expert(back[k], k) for k in (1, 2, 3)]
    token_grad, tok_mark = call(
        tok_step,
        "vaaaa",
        [shape(toks, width), MARK],
        [pltpu.VMEM((rows, width), BF), sems(4)],
        flops=2 * toks * rows * width,
        moved=2 * (rows + toks) * width,
    )(mask, *arrived)

    keep, send = sum_call(at, down, [])
    down_grad = (keep + swap_w(send).astype(F32)).astype(BF).reshape(4, 24, part)
    cols = [
        shift(lax.dynamic_index_in_dim(down_grad, (y + j) % 4, 0, False), "y", j) for j in range(4)
    ]
    turned = jnp.stack(cols[::-1] + cols[::-1])
    mine = lax.dynamic_slice_in_dim(turned, 3 - y, 4, 0)
    down_grad = jnp.concatenate([mine[i] for i in range(4)], axis=1)

    keep, send = call(
        gate_sum,
        "saa",
        [shape(128, 2 * inner, dtype=F32), shape(128, 2 * inner)],
        [pltpu.VMEM((4, 256, 2 * inner), BF), sems(1)],
        moved=16 * 256 * inner,
    )(at, gate, tok_mark)
    gate_up_grad = (keep + swap_w(send).astype(F32)).astype(BF)
    return token_grad, gate_up_grad[None], down_grad[None]


def solution(mesh):
    fine = Mesh(mesh.devices.reshape(2, 4, 4, 2, 2), AXES)
    rows, expert, dp = P(AXES, None), ("v", "c"), ("w", "x", "y")
    in_specs = (rows, rows, rows, rows, P(expert, None, None), P(expert, None, None))
    out_specs = (rows, P(expert, dp, None), P(expert, dp, None))
    return jax.shard_map(
        shards, mesh=fine, in_specs=in_specs, out_specs=out_specs, check_vma=False
    )
```

```python
import jax
import jax.numpy as jnp
from jax import lax
from jax.experimental import pallas as pl
from jax.experimental.pallas import tpu as pltpu
from jax.sharding import Mesh, PartitionSpec as P

CAP = 48
BF = jnp.bfloat16
F32 = jnp.float32
MB = 1024 * 1024
AXES = ("w", "x", "y", "v", "c")
VMEM = pl.BlockSpec(memory_space=pltpu.VMEM)
SMEM = pl.BlockSpec(memory_space=pltpu.SMEM)
ANY = pl.BlockSpec(memory_space=pl.ANY)
HBM = pl.BlockSpec(memory_space=pltpu.HBM)
MARK = jax.ShapeDtypeStruct((8, 128), F32)


def swap_expert(a, k):
    return lax.ppermute(a, ("v", "c"), [(i, i ^ k) for i in range(4)])


def shift(a, axis, j):
    if j == 0:
        return a
    return lax.ppermute(a, axis, [(i, (i + j) % 4) for i in range(4)])


def swap_w(a):
    return lax.ppermute(a, "w", [(0, 1), (1, 0)])


def rows_dot(a, b):
    return lax.dot_general(a, b, (((0,), (0,)), ((), ())), preferred_element_type=F32)


def wide_dot(a, b):
    return lax.dot_general(a, b, (((1,), (1,)), ((), ())), preferred_element_type=F32)


def shape(*dims, dtype=BF):
    return jax.ShapeDtypeStruct(dims, dtype)


def aligned(i, size):
    return pl.ds(pl.multiple_of(i * size, size), size)


def call(body, ins, outs, scratch=(), flops=0, moved=0, limit=8, placed=()):
    specs = {"s": SMEM, "v": VMEM, "a": ANY}
    return pl.pallas_call(
        body,
        out_shape=[pltpu.HBM(o.shape, o.dtype) if i in placed else o for i, o in enumerate(outs)],
        in_specs=[specs[i] for i in ins],
        out_specs=[HBM if o in placed else VMEM for o in range(len(outs))],
        scratch_shapes=list(scratch),
        compiler_params=pltpu.CompilerParams(vmem_limit_bytes=limit * MB),
        cost_estimate=pl.CostEstimate(flops=flops, bytes_accessed=moved, transcendentals=0),
    )


def fetch(pairs, sems):
    copies = [pltpu.make_async_copy(s, d, sems.at[i]) for i, (s, d) in enumerate(pairs)]
    for copy in copies:
        copy.start()
    return copies


def land(pairs, sems):
    for copy in fetch(pairs, sems):
        copy.wait()


def sems(n):
    return pltpu.SemaphoreType.DMA((n,))


def pack_x(at, x0, x1, x2, x3, *outs):
    whole = outs[4]
    for k, piece in enumerate((x0, x1, x2, x3)):
        rows = slice(k * CAP, k * CAP + CAP)
        whole[rows, :] = piece[...]
        for j in range(4):
            for b in range(2):
                cols = aligned(b * 4 + lax.rem(at[1] + j, 4), 512)
                outs[j][rows, b * 512 : b * 512 + 512] = piece[:, cols]


def pack_g(g0, g1, g2, g3, hidden, *rest):
    out, mark, sem = rest[-3:]
    part, inner = g0.shape[1] // 4, hidden.shape[1]
    mark[...] = jnp.zeros_like(mark)
    pairs = []
    for i in range(4):
        for k, piece in enumerate((g0, g1, g2, g3)):
            to = out.at[i, pl.ds(k * CAP, CAP), pl.ds(0, part)]
            pairs.append((piece.at[:, pl.ds(i * part, part)], to))
        pairs.append((hidden, out.at[i, :, pl.ds(part, inner)]))
    land(pairs, sem)


def act_step(x, weights, hidden, slope, silu, buf, sem):
    inner, step = hidden.shape[1], buf.shape[2]
    n = inner // step
    cuts = [(i, h) for i in range(n) for h in range(2)]
    copies = fetch(
        [
            (weights.at[:, pl.ds(h * inner + i * step, step)], buf.at[2 * i + h])
            for i, h in cuts
        ],
        sem,
    )
    for i in range(n):
        cols = slice(i * step, i * step + step)
        copies[2 * i].wait()
        gpart = jnp.dot(x[...], buf[2 * i], preferred_element_type=F32)
        copies[2 * i + 1].wait()
        upart = jnp.dot(x[...], buf[2 * i + 1], preferred_element_type=F32)
        sig = jax.nn.sigmoid(gpart)
        soft = gpart * sig
        hidden[:, cols] = (soft * upart).astype(BF)
        slope[:, cols] = upart * (sig * (1.0 + gpart * (1.0 - sig)))
        silu[:, cols] = soft


def dh_step(g0, g1, g2, g3, slope, silu, weights, *rest):
    dact, whole, factors, buf, sem, gsem = rest[-6:]
    n, step = buf.shape[:2]
    copies = fetch([(weights.at[pl.ds(i * step, step), :], buf.at[i]) for i in range(n)], sem)
    pieces = [(g, whole.at[pl.ds(k * CAP, CAP), :]) for k, g in enumerate((g0, g1, g2, g3))]
    land(pieces + [(slope, factors.at[0]), (silu, factors.at[1])], gsem)
    for i in range(n):
        cols = slice(i * step, i * step + step)
        copies[i].wait()
        dh = wide_dot(whole[...], buf[i])
        dact[0, :, cols] = (dh * factors[0, :, cols]).astype(BF)
        dact[1, :, cols] = (dh * factors[1, :, cols]).astype(BF)


def back_step(dact, weights, *rest):
    outs, mark, buf, sem = rest[-7:-3], *rest[-3:]
    n, step, inner = buf.shape[0], buf.shape[1], dact.shape[2]
    copies = fetch([(weights.at[pl.ds(i * step, step), :], buf.at[i]) for i in range(n)], sem)
    mark[...] = jnp.zeros_like(mark)
    for i in range(n):
        copies[i].wait()
        got = wide_dot(dact[0], buf[i, :, :inner]) + wide_dot(dact[1], buf[i, :, inner:])
        for k in range(4):
            outs[k][:, i * step : i * step + step] = got[k * CAP : k * CAP + CAP].astype(BF)


def tok_step(mask, a0, a1, a2, a3, *rest):
    out, whole, sem = rest[-3:]
    pieces = (a0, a1, a2, a3)
    land([(a, whole.at[pl.ds(k * CAP, CAP), :]) for k, a in enumerate(pieces)], sem)
    out[...] = jnp.dot(mask[...], whole[...], preferred_element_type=F32).astype(BF)


def tile_step(*refs):
    xs, ds = refs[:4], refs[4:8]
    out, mark, xall, dall, buf, sem, osem = refs[-7:]
    rows = xs[0].shape[0]
    part = [pl.ds(p * rows, rows) for p in range(4)]
    inner = ds[0].shape[2]
    land(
        [(xs[p], xall.at[part[p], :]) for p in range(4)]
        + [
            (ds[p].at[h], dall.at[part[p], pl.ds(h * inner, inner)])
            for p in range(4)
            for h in range(2)
        ],
        sem,
    )
    mark[...] = jnp.zeros_like(mark)
    copies = []
    for b in range(2):
        got = rows_dot(xall[:, b * 512 : b * 512 + 512], dall[...])
        for j in range(4):
            buf[j, b * 128 : b * 128 + 128, :] = got[j * 128 : j * 128 + 128].astype(BF)
            if b == 1:
                copies.append(pltpu.make_async_copy(buf.at[j], out.at[j], osem.at[j]))
                copies[-1].start()
    for copy in copies:
        copy.wait()


def tile_call(xs, ds, after):
    rows, part = xs[0].shape
    wide = 2 * ds[0].shape[2]
    return call(
        tile_step,
        "a" * (8 + len(after)),
        [shape(4, 256, wide), MARK],
        [
            pltpu.VMEM((4 * rows, part), BF),
            pltpu.VMEM((4 * rows, wide), BF),
            pltpu.VMEM((4, 256, wide), BF),
            sems(12),
            sems(4),
        ],
        flops=8 * rows * part * wide,
        moved=8 * rows * (part + wide),
        limit=24,
        placed=(0,),
    )(*xs, *ds, *after)


def down_step(at, both, *rest):
    outs, mark, gall, hall, total, sem = rest[-9:-5], *rest[-5:]
    rows, part, inner = both.shape[1], gall.shape[1], hall.shape[1]
    pairs = []
    for i in range(4):
        pairs.append((both.at[i, :, pl.ds(0, part)], gall.at[pl.ds(i * rows, rows), :]))
        pairs.append((both.at[i, :, pl.ds(part, inner)], hall.at[pl.ds(i * rows, rows), :]))
    land(pairs, sem)
    mark[...] = jnp.zeros_like(mark)
    for b in range(2):
        cols = slice(b * inner // 2, (b + 1) * inner // 2)
        total[cols, :] = rows_dot(hall[:, cols], gall[...])
    for j in (1, 2, 3, 0):
        other = lax.rem(at[1] + j, 4)
        for b in range(2):
            outs[j][b * 96 : b * 96 + 96, :] = total[aligned(b * 4 + other, 96), :].astype(
                outs[j].dtype
            )


def gate_sum(at, parts, keep, send, mark, g, sem):
    half = keep.shape[0]
    copies = fetch([(parts.at[i], g.at[i]) for i in range(4)], sem)
    for copy in copies:
        copy.wait()
    mark[...] = jnp.zeros_like(mark)

    def part(i):
        return sum(g[p, aligned(i, half), :].astype(F32) for p in range(4))

    send[...] = part(1 - at[0]).astype(BF)
    keep[...] = part(at[0])


def sum_step(at, own, r1, r2, r3, *rest):
    keep, send, f, g, sem = rest[-5:]
    half = keep.shape[0]
    land([(own, f), (r1, g.at[0]), (r2, g.at[1]), (r3, g.at[2])], sem)

    def part(i):
        rows = aligned(i, half)
        return f[rows, :] + sum(g[p, rows, :].astype(F32) for p in range(3))

    send[...] = part(1 - at[0]).astype(BF)
    keep[...] = part(at[0])


def sum_call(at, parts, after):
    rows, cols = parts[0].shape
    return call(
        sum_step,
        "saaaa" + "a" * len(after),
        [shape(rows // 2, cols, dtype=F32), shape(rows // 2, cols)],
        [pltpu.VMEM((rows, cols), F32), pltpu.VMEM((3, rows, cols), BF), sems(4)],
        moved=10 * rows * cols,
        limit=12,
    )(at, *parts, *after)


def shards(tokens, cotangent, routes, gates, gate_up, down_proj):
    gate_up = pltpu.with_memory_space_constraint(gate_up[0], pltpu.HBM)
    down_proj = pltpu.with_memory_space_constraint(down_proj[0], pltpu.HBM)
    w, x, y = lax.axis_index("w"), lax.axis_index("x"), lax.axis_index("y")
    me = lax.axis_index(("v", "c"))
    at = jnp.stack([w, x, y, me]).astype(jnp.int32)
    toks, width = tokens.shape
    inner = down_proj.shape[0]
    rows, part = 4 * CAP, width // 4
    experts = jnp.bitwise_xor(me, jnp.arange(4, dtype=jnp.int32))
    matches = routes[:, :, None] == experts[None, None, :]
    member = jnp.any(matches, axis=1)
    weight = jnp.sum(jnp.where(matches, gates[:, :, None], F32(0.0)), axis=1)
    position = jnp.cumsum(member.astype(jnp.int32), axis=0) - 1
    select = member[:, :, None] & (
        position[:, :, None] == jnp.arange(CAP, dtype=jnp.int32)[None, None, :]
    )
    mask = select.astype(BF).reshape(toks, rows)
    slot_gate = jnp.sum(jnp.where(select, weight[:, :, None], F32(0.0)), axis=0).reshape(rows, 1)
    send_x = rows_dot(mask, tokens).astype(BF).reshape(4, CAP, width)
    send_g = (rows_dot(mask, cotangent) * slot_gate).astype(BF).reshape(4, CAP, width)
    xs = [send_x[0]] + [swap_expert(send_x[k], k) for k in (1, 2, 3)]
    gs = [send_g[0]] + [swap_expert(send_g[k], k) for k in (1, 2, 3)]

    packed = call(
        pack_x, "svvvv", [shape(rows, part)] * 4 + [shape(rows, width)], moved=4 * rows * width
    )(at, *xs)
    xa = [shift(packed[j], "x", j) for j in range(4)]
    n = 2 * inner // 256
    hidden, slope, silu = call(
        act_step,
        "va",
        [shape(rows, inner), shape(rows, inner, dtype=F32), shape(rows, inner, dtype=F32)],
        [pltpu.VMEM((n, width, 256), BF), sems(n)],
        flops=4 * rows * width * inner,
        moved=4 * width * inner,
        limit=18,
    )(packed[4], gate_up)
    sent, sent_mark = call(
        pack_g,
        "aaaaaaa",
        [shape(4, rows, part + inner), MARK],
        [sems(20)],
        moved=4 * rows * width,
        placed=(0,),
    )(*gs, hidden, xa[1], xa[3])
    both = lax.all_to_all(sent, "y", split_axis=0, concat_axis=0, tiled=True)
    n = inner // 256
    dact = call(
        dh_step,
        "aaaaaaaa",
        [shape(2, rows, inner)],
        [
            pltpu.VMEM((rows, width), BF),
            pltpu.VMEM((2, rows, inner), F32),
            pltpu.VMEM((n, 256, width), BF),
            sems(n),
            sems(6),
        ],
        flops=2 * rows * width * inner,
        moved=2 * width * inner,
        limit=14,
    )(*gs, slope, silu, down_proj, sent_mark)[0]
    da = [shift(dact, "x", j) for j in range(4)]
    n = width // 512
    *back, back_mark = call(
        back_step,
        "vaaa",
        [shape(CAP, width)] * 4 + [MARK],
        [pltpu.VMEM((n, 512, 2 * inner), BF), sems(n)],
        flops=4 * rows * width * inner,
        moved=4 * width * inner,
        limit=18,
    )(dact, gate_up, da[1], xa[2])
    *parts, mark = call(
        down_step,
        "saa",
        [shape(192, part, dtype=F32)] + [shape(192, part)] * 3 + [MARK],
        [
            pltpu.VMEM((4 * rows, part), BF),
            pltpu.VMEM((4 * rows, inner), BF),
            pltpu.VMEM((inner, part), F32),
            sems(8),
        ],
        flops=8 * rows * part * inner,
        moved=8 * rows * (part + inner),
        limit=16,
    )(at, both, back_mark)
    down = [parts[0]] + [shift(parts[j], "x", j) for j in (1, 2, 3)]
    parts, _ = tile_call(xa, da, [mark])
    gate = lax.all_to_all(parts, "y", split_axis=0, concat_axis=0, tiled=True)
    arrived = [back[0]] + [swap_expert(back[k], k) for k in (1, 2, 3)]
    keep, send, mark = call(
        gate_sum,
        "sa",
        [shape(128, 2 * inner, dtype=F32), shape(128, 2 * inner), MARK],
        [pltpu.VMEM((4, 256, 2 * inner), BF), sems(4)],
        moved=16 * 256 * inner,
        limit=12,
    )(at, gate)
    gate_up_grad = (keep + swap_w(send).astype(F32)).astype(BF)
    token_grad = call(
        tok_step,
        "vaaaaa",
        [shape(toks, width)],
        [pltpu.VMEM((rows, width), BF), sems(4)],
        flops=2 * toks * rows * width,
        moved=2 * (rows + toks) * width,
    )(mask, *arrived, mark)[0]

    keep, send = sum_call(at, down, [])
    down_grad = (keep + swap_w(send).astype(F32)).astype(BF).reshape(4, 24, part)
    cols = [
        shift(lax.dynamic_index_in_dim(down_grad, (y + j) % 4, 0, False), "y", j) for j in range(4)
    ]
    turned = jnp.stack(cols[::-1] + cols[::-1])
    mine = lax.dynamic_slice_in_dim(turned, 3 - y, 4, 0)
    down_grad = jnp.concatenate([mine[i] for i in range(4)], axis=1)

    return token_grad, gate_up_grad[None], down_grad[None]


def solution(mesh):
    fine = Mesh(mesh.devices.reshape(2, 4, 4, 2, 2), AXES)
    rows, expert, dp = P(AXES, None), ("v", "c"), ("w", "x", "y")
    in_specs = (rows, rows, rows, rows, P(expert, None, None), P(expert, None, None))
    out_specs = (rows, P(expert, dp, None), P(expert, dp, None))
    return jax.shard_map(
        shards, mesh=fine, in_specs=in_specs, out_specs=out_specs, check_vma=False
    )
```

```python
import jax
import jax.numpy as jnp
from jax import lax
from jax.experimental import pallas as pl
from jax.experimental.pallas import tpu as pltpu
from jax.sharding import Mesh, PartitionSpec as P

CAP = 48
BF = jnp.bfloat16
F32 = jnp.float32
MB = 1024 * 1024
AXES = ("w", "x", "y", "v", "c")
VMEM = pl.BlockSpec(memory_space=pltpu.VMEM)
SMEM = pl.BlockSpec(memory_space=pltpu.SMEM)
ANY = pl.BlockSpec(memory_space=pl.ANY)
HBM = pl.BlockSpec(memory_space=pltpu.HBM)
MARK = jax.ShapeDtypeStruct((8, 128), F32)


def swap_expert(a, k):
    return lax.ppermute(a, ("v", "c"), [(i, i ^ k) for i in range(4)])


def shift(a, axis, j):
    if j == 0:
        return a
    return lax.ppermute(a, axis, [(i, (i + j) % 4) for i in range(4)])


def swap_w(a):
    return lax.ppermute(a, "w", [(0, 1), (1, 0)])


def rows_dot(a, b):
    return lax.dot_general(a, b, (((0,), (0,)), ((), ())), preferred_element_type=F32)


def wide_dot(a, b):
    return lax.dot_general(a, b, (((1,), (1,)), ((), ())), preferred_element_type=F32)


def shape(*dims, dtype=BF):
    return jax.ShapeDtypeStruct(dims, dtype)


def aligned(i, size):
    return pl.ds(pl.multiple_of(i * size, size), size)


def call(body, ins, outs, scratch=(), flops=0, moved=0, limit=8, placed=()):
    specs = {"s": SMEM, "v": VMEM, "a": ANY}
    return pl.pallas_call(
        body,
        out_shape=[pltpu.HBM(o.shape, o.dtype) if i in placed else o for i, o in enumerate(outs)],
        in_specs=[specs[i] for i in ins],
        out_specs=[HBM if o in placed else VMEM for o in range(len(outs))],
        scratch_shapes=list(scratch),
        compiler_params=pltpu.CompilerParams(vmem_limit_bytes=limit * MB),
        cost_estimate=pl.CostEstimate(flops=flops, bytes_accessed=moved, transcendentals=0),
    )


def fetch(pairs, sems):
    copies = [pltpu.make_async_copy(s, d, sems.at[i]) for i, (s, d) in enumerate(pairs)]
    for copy in copies:
        copy.start()
    return copies


def land(pairs, sems):
    for copy in fetch(pairs, sems):
        copy.wait()


def sems(n):
    return pltpu.SemaphoreType.DMA((n,))


def pack_x(at, x0, x1, x2, x3, *outs):
    whole = outs[4]
    for k, piece in enumerate((x0, x1, x2, x3)):
        rows = slice(k * CAP, k * CAP + CAP)
        whole[rows, :] = piece[...]
        for j in range(4):
            for b in range(2):
                cols = aligned(b * 4 + lax.rem(at[1] + j, 4), 512)
                outs[j][rows, b * 512 : b * 512 + 512] = piece[:, cols]


def pack_g(g0, g1, g2, g3, hidden, *rest):
    out, mark, sem = rest[-3:]
    part, inner = g0.shape[1] // 4, hidden.shape[1]
    mark[...] = jnp.zeros_like(mark)
    pairs = []
    for i in range(4):
        for k, piece in enumerate((g0, g1, g2, g3)):
            to = out.at[i, pl.ds(k * CAP, CAP), pl.ds(0, part)]
            pairs.append((piece.at[:, pl.ds(i * part, part)], to))
        pairs.append((hidden, out.at[i, :, pl.ds(part, inner)]))
    land(pairs, sem)


def act_step(x, weights, hidden, slope, silu, buf, sem):
    inner, step = hidden.shape[1], buf.shape[2]
    n = inner // step
    cuts = [(i, h) for i in range(n) for h in range(2)]
    copies = fetch(
        [
            (weights.at[:, pl.ds(h * inner + i * step, step)], buf.at[2 * i + h])
            for i, h in cuts
        ],
        sem,
    )
    for i in range(n):
        cols = slice(i * step, i * step + step)
        copies[2 * i].wait()
        gpart = jnp.dot(x[...], buf[2 * i], preferred_element_type=F32)
        copies[2 * i + 1].wait()
        upart = jnp.dot(x[...], buf[2 * i + 1], preferred_element_type=F32)
        sig = jax.nn.sigmoid(gpart)
        soft = gpart * sig
        hidden[:, cols] = (soft * upart).astype(BF)
        slope[:, cols] = upart * (sig * (1.0 + gpart * (1.0 - sig)))
        silu[:, cols] = soft


def dh_step(g0, g1, g2, g3, slope, silu, weights, *rest):
    dact, mark, whole, factors, buf, sem, gsem = rest[-7:]
    mark[...] = jnp.zeros_like(mark)
    n, step = buf.shape[:2]
    copies = fetch([(weights.at[pl.ds(i * step, step), :], buf.at[i]) for i in range(n)], sem)
    pieces = [(g, whole.at[pl.ds(k * CAP, CAP), :]) for k, g in enumerate((g0, g1, g2, g3))]
    land(pieces + [(slope, factors.at[0]), (silu, factors.at[1])], gsem)
    for i in range(n):
        cols = slice(i * step, i * step + step)
        copies[i].wait()
        dh = wide_dot(whole[...], buf[i])
        dact[0, :, cols] = (dh * factors[0, :, cols]).astype(BF)
        dact[1, :, cols] = (dh * factors[1, :, cols]).astype(BF)


def back_step(dact, weights, *rest):
    outs, mark, buf, sem = rest[-7:-3], *rest[-3:]
    n, step, inner = buf.shape[0], buf.shape[1], dact.shape[2]
    copies = fetch([(weights.at[pl.ds(i * step, step), :], buf.at[i]) for i in range(n)], sem)
    mark[...] = jnp.zeros_like(mark)
    for i in range(n):
        copies[i].wait()
        got = wide_dot(dact[0], buf[i, :, :inner]) + wide_dot(dact[1], buf[i, :, inner:])
        for k in range(4):
            outs[k][:, i * step : i * step + step] = got[k * CAP : k * CAP + CAP].astype(BF)


def tok_step(mask, a0, a1, a2, a3, *rest):
    out, whole, sem = rest[-3:]
    pieces = (a0, a1, a2, a3)
    land([(a, whole.at[pl.ds(k * CAP, CAP), :]) for k, a in enumerate(pieces)], sem)
    out[...] = jnp.dot(mask[...], whole[...], preferred_element_type=F32).astype(BF)


def tile_step(*refs):
    xs, ds = refs[:4], refs[4:8]
    out, mark, xall, dall, buf, sem, osem = refs[-7:]
    rows = xs[0].shape[0]
    part = [pl.ds(p * rows, rows) for p in range(4)]
    inner = ds[0].shape[2]
    land(
        [(xs[p], xall.at[part[p], :]) for p in range(4)]
        + [
            (ds[p].at[h], dall.at[part[p], pl.ds(h * inner, inner)])
            for p in range(4)
            for h in range(2)
        ],
        sem,
    )
    mark[...] = jnp.zeros_like(mark)
    copies = []
    for b in range(2):
        got = rows_dot(xall[:, b * 512 : b * 512 + 512], dall[...])
        for j in range(4):
            buf[j, b * 128 : b * 128 + 128, :] = got[j * 128 : j * 128 + 128].astype(BF)
            if b == 1:
                copies.append(pltpu.make_async_copy(buf.at[j], out.at[j], osem.at[j]))
                copies[-1].start()
    for copy in copies:
        copy.wait()


def tile_call(xs, ds, after):
    rows, part = xs[0].shape
    wide = 2 * ds[0].shape[2]
    return call(
        tile_step,
        "a" * (8 + len(after)),
        [shape(4, 256, wide), MARK],
        [
            pltpu.VMEM((4 * rows, part), BF),
            pltpu.VMEM((4 * rows, wide), BF),
            pltpu.VMEM((4, 256, wide), BF),
            sems(12),
            sems(4),
        ],
        flops=8 * rows * part * wide,
        moved=8 * rows * (part + wide),
        limit=24,
        placed=(0,),
    )(*xs, *ds, *after)


def down_step(at, both, *rest):
    outs, mark, gall, hall, total, sem = rest[-9:-5], *rest[-5:]
    rows, part, inner = both.shape[1], gall.shape[1], hall.shape[1]
    pairs = []
    for i in range(4):
        pairs.append((both.at[i, :, pl.ds(0, part)], gall.at[pl.ds(i * rows, rows), :]))
        pairs.append((both.at[i, :, pl.ds(part, inner)], hall.at[pl.ds(i * rows, rows), :]))
    land(pairs, sem)
    mark[...] = jnp.zeros_like(mark)
    for b in range(2):
        cols = slice(b * inner // 2, (b + 1) * inner // 2)
        total[cols, :] = rows_dot(hall[:, cols], gall[...])
    for j in (1, 2, 3, 0):
        other = lax.rem(at[1] + j, 4)
        for b in range(2):
            outs[j][b * 96 : b * 96 + 96, :] = total[aligned(b * 4 + other, 96), :].astype(
                outs[j].dtype
            )


def gate_sum(at, parts, keep, send, mark, g, sem):
    half = keep.shape[0]
    copies = fetch([(parts.at[i], g.at[i]) for i in range(4)], sem)
    for copy in copies:
        copy.wait()
    mark[...] = jnp.zeros_like(mark)

    def part(i):
        return sum(g[p, aligned(i, half), :].astype(F32) for p in range(4))

    send[...] = part(1 - at[0]).astype(BF)
    keep[...] = part(at[0])


def sum_step(at, own, r1, r2, r3, *rest):
    keep, send, f, g, sem = rest[-5:]
    half = keep.shape[0]
    land([(own, f), (r1, g.at[0]), (r2, g.at[1]), (r3, g.at[2])], sem)

    def part(i):
        rows = aligned(i, half)
        return f[rows, :] + sum(g[p, rows, :].astype(F32) for p in range(3))

    send[...] = part(1 - at[0]).astype(BF)
    keep[...] = part(at[0])


def sum_call(at, parts, after):
    rows, cols = parts[0].shape
    return call(
        sum_step,
        "saaaa" + "a" * len(after),
        [shape(rows // 2, cols, dtype=F32), shape(rows // 2, cols)],
        [pltpu.VMEM((rows, cols), F32), pltpu.VMEM((3, rows, cols), BF), sems(4)],
        moved=10 * rows * cols,
        limit=12,
    )(at, *parts, *after)


def shards(tokens, cotangent, routes, gates, gate_up, down_proj):
    gate_up = pltpu.with_memory_space_constraint(gate_up[0], pltpu.HBM)
    down_proj = pltpu.with_memory_space_constraint(down_proj[0], pltpu.HBM)
    w, x, y = lax.axis_index("w"), lax.axis_index("x"), lax.axis_index("y")
    me = lax.axis_index(("v", "c"))
    at = jnp.stack([w, x, y, me]).astype(jnp.int32)
    toks, width = tokens.shape
    inner = down_proj.shape[0]
    rows, part = 4 * CAP, width // 4
    experts = jnp.bitwise_xor(me, jnp.arange(4, dtype=jnp.int32))
    matches = routes[:, :, None] == experts[None, None, :]
    member = jnp.any(matches, axis=1)
    weight = jnp.sum(jnp.where(matches, gates[:, :, None], F32(0.0)), axis=1)
    position = jnp.cumsum(member.astype(jnp.int32), axis=0) - 1
    select = member[:, :, None] & (
        position[:, :, None] == jnp.arange(CAP, dtype=jnp.int32)[None, None, :]
    )
    mask = select.astype(BF).reshape(toks, rows)
    slot_gate = jnp.sum(jnp.where(select, weight[:, :, None], F32(0.0)), axis=0).reshape(rows, 1)
    send_x = rows_dot(mask, tokens).astype(BF).reshape(4, CAP, width)
    send_g = (rows_dot(mask, cotangent) * slot_gate).astype(BF).reshape(4, CAP, width)
    xs = [send_x[0]] + [swap_expert(send_x[k], k) for k in (1, 2, 3)]
    gs = [send_g[0]] + [swap_expert(send_g[k], k) for k in (1, 2, 3)]

    packed = call(
        pack_x, "svvvv", [shape(rows, part)] * 4 + [shape(rows, width)], moved=4 * rows * width
    )(at, *xs)
    xa = [shift(packed[j], "x", j) for j in range(4)]
    n = 2 * inner // 256
    hidden, slope, silu = call(
        act_step,
        "va",
        [shape(rows, inner), shape(rows, inner, dtype=F32), shape(rows, inner, dtype=F32)],
        [pltpu.VMEM((n, width, 256), BF), sems(n)],
        flops=4 * rows * width * inner,
        moved=4 * width * inner,
        limit=18,
    )(packed[4], gate_up)
    sent, sent_mark = call(
        pack_g,
        "aaaaaaa",
        [shape(4, rows, part + inner), MARK],
        [sems(20)],
        moved=4 * rows * width,
        placed=(0,),
    )(*gs, hidden, xa[1], xa[3])
    both = lax.all_to_all(sent, "y", split_axis=0, concat_axis=0, tiled=True)
    n = inner // 256
    dact, mark = call(
        dh_step,
        "aaaaaaaa",
        [shape(2, rows, inner), MARK],
        [
            pltpu.VMEM((rows, width), BF),
            pltpu.VMEM((2, rows, inner), F32),
            pltpu.VMEM((n, 256, width), BF),
            sems(n),
            sems(6),
        ],
        flops=2 * rows * width * inner,
        moved=2 * width * inner,
        limit=14,
    )(*gs, slope, silu, down_proj, sent_mark)
    da = [shift(dact, "x", j) for j in range(4)]
    n = width // 512
    *back, back_mark = call(
        back_step,
        "vaa",
        [shape(CAP, width)] * 4 + [MARK],
        [pltpu.VMEM((n, 512, 2 * inner), BF), sems(n)],
        flops=4 * rows * width * inner,
        moved=4 * width * inner,
        limit=18,
    )(dact, gate_up, swap_expert(mark, 1))
    *parts, mark = call(
        down_step,
        "saa",
        [shape(192, part, dtype=F32)] + [shape(192, part)] * 3 + [MARK],
        [
            pltpu.VMEM((4 * rows, part), BF),
            pltpu.VMEM((4 * rows, inner), BF),
            pltpu.VMEM((inner, part), F32),
            sems(8),
        ],
        flops=8 * rows * part * inner,
        moved=8 * rows * (part + inner),
        limit=16,
    )(at, both, back_mark)
    down = [parts[0]] + [shift(parts[j], "x", j) for j in (1, 2, 3)]
    parts, _ = tile_call(xa, da, [mark])
    gate = lax.all_to_all(parts, "y", split_axis=0, concat_axis=0, tiled=True)
    arrived = [back[0]] + [swap_expert(back[k], k) for k in (1, 2, 3)]
    keep, send, mark = call(
        gate_sum,
        "sa",
        [shape(128, 2 * inner, dtype=F32), shape(128, 2 * inner), MARK],
        [pltpu.VMEM((4, 256, 2 * inner), BF), sems(4)],
        moved=16 * 256 * inner,
        limit=12,
    )(at, gate)
    gate_up_grad = (keep + swap_w(send).astype(F32)).astype(BF)
    token_grad = call(
        tok_step,
        "vaaaaa",
        [shape(toks, width)],
        [pltpu.VMEM((rows, width), BF), sems(4)],
        flops=2 * toks * rows * width,
        moved=2 * (rows + toks) * width,
    )(mask, *arrived, mark)[0]

    keep, send = sum_call(at, down, [])
    down_grad = (keep + swap_w(send).astype(F32)).astype(BF).reshape(4, 24, part)
    cols = [
        shift(lax.dynamic_index_in_dim(down_grad, (y + j) % 4, 0, False), "y", j) for j in range(4)
    ]
    turned = jnp.stack(cols[::-1] + cols[::-1])
    mine = lax.dynamic_slice_in_dim(turned, 3 - y, 4, 0)
    down_grad = jnp.concatenate([mine[i] for i in range(4)], axis=1)

    return token_grad, gate_up_grad[None], down_grad[None]


def solution(mesh):
    fine = Mesh(mesh.devices.reshape(2, 4, 4, 2, 2), AXES)
    rows, expert, dp = P(AXES, None), ("v", "c"), ("w", "x", "y")
    in_specs = (rows, rows, rows, rows, P(expert, None, None), P(expert, None, None))
    out_specs = (rows, P(expert, dp, None), P(expert, dp, None))
    return jax.shard_map(
        shards, mesh=fine, in_specs=in_specs, out_specs=out_specs, check_vma=False
    )
```

```python
import jax
import jax.numpy as jnp
from jax import lax
from jax.experimental import pallas as pl
from jax.experimental.pallas import tpu as pltpu
from jax.sharding import Mesh, PartitionSpec as P

CAP = 48
BF = jnp.bfloat16
F32 = jnp.float32
MB = 1024 * 1024
AXES = ("w", "x", "y", "v", "c")
VMEM = pl.BlockSpec(memory_space=pltpu.VMEM)
SMEM = pl.BlockSpec(memory_space=pltpu.SMEM)
ANY = pl.BlockSpec(memory_space=pl.ANY)
HBM = pl.BlockSpec(memory_space=pltpu.HBM)
MARK = jax.ShapeDtypeStruct((8, 128), F32)


def swap_expert(a, k):
    return lax.ppermute(a, ("v", "c"), [(i, i ^ k) for i in range(4)])


def shift(a, axis, j):
    if j == 0:
        return a
    return lax.ppermute(a, axis, [(i, (i + j) % 4) for i in range(4)])


def swap_w(a):
    return lax.ppermute(a, "w", [(0, 1), (1, 0)])


def rows_dot(a, b):
    return lax.dot_general(a, b, (((0,), (0,)), ((), ())), preferred_element_type=F32)


def wide_dot(a, b):
    return lax.dot_general(a, b, (((1,), (1,)), ((), ())), preferred_element_type=F32)


def shape(*dims, dtype=BF):
    return jax.ShapeDtypeStruct(dims, dtype)


def aligned(i, size):
    return pl.ds(pl.multiple_of(i * size, size), size)


def call(body, ins, outs, scratch=(), flops=0, moved=0, limit=8, placed=()):
    specs = {"s": SMEM, "v": VMEM, "a": ANY}
    return pl.pallas_call(
        body,
        out_shape=[pltpu.HBM(o.shape, o.dtype) if i in placed else o for i, o in enumerate(outs)],
        in_specs=[specs[i] for i in ins],
        out_specs=[HBM if o in placed else VMEM for o in range(len(outs))],
        scratch_shapes=list(scratch),
        compiler_params=pltpu.CompilerParams(vmem_limit_bytes=limit * MB),
        cost_estimate=pl.CostEstimate(flops=flops, bytes_accessed=moved, transcendentals=0),
    )


def fetch(pairs, sems):
    copies = [pltpu.make_async_copy(s, d, sems.at[i]) for i, (s, d) in enumerate(pairs)]
    for copy in copies:
        copy.start()
    return copies


def land(pairs, sems):
    for copy in fetch(pairs, sems):
        copy.wait()


def sems(n):
    return pltpu.SemaphoreType.DMA((n,))


def pack_x(at, x0, x1, x2, x3, *outs):
    whole = outs[4]
    for k, piece in enumerate((x0, x1, x2, x3)):
        rows = slice(k * CAP, k * CAP + CAP)
        whole[rows, :] = piece[...]
        for j in range(4):
            for b in range(2):
                cols = aligned(b * 4 + lax.rem(at[1] + j, 4), 512)
                outs[j][rows, b * 512 : b * 512 + 512] = piece[:, cols]


def pack_g(g0, g1, g2, g3, hidden, *rest):
    out, mark, sem = rest[-3:]
    part, inner = g0.shape[1] // 4, hidden.shape[1]
    mark[...] = jnp.zeros_like(mark)
    pairs = []
    for i in range(4):
        for k, piece in enumerate((g0, g1, g2, g3)):
            to = out.at[i, pl.ds(k * CAP, CAP), pl.ds(0, part)]
            pairs.append((piece.at[:, pl.ds(i * part, part)], to))
        pairs.append((hidden, out.at[i, :, pl.ds(part, inner)]))
    land(pairs, sem)


def act_step(x, weights, hidden, slope, silu, buf, sem):
    inner, step = hidden.shape[1], buf.shape[2]
    n = inner // step
    cuts = [(i, h) for i in range(n) for h in range(2)]
    copies = fetch(
        [
            (weights.at[:, pl.ds(h * inner + i * step, step)], buf.at[2 * i + h])
            for i, h in cuts
        ],
        sem,
    )
    for i in range(n):
        cols = slice(i * step, i * step + step)
        copies[2 * i].wait()
        gpart = jnp.dot(x[...], buf[2 * i], preferred_element_type=F32)
        copies[2 * i + 1].wait()
        upart = jnp.dot(x[...], buf[2 * i + 1], preferred_element_type=F32)
        sig = jax.nn.sigmoid(gpart)
        soft = gpart * sig
        hidden[:, cols] = (soft * upart).astype(BF)
        slope[:, cols] = upart * (sig * (1.0 + gpart * (1.0 - sig)))
        silu[:, cols] = soft


def dh_step(g0, g1, g2, g3, slope, silu, weights, *rest):
    dact, mark, whole, factors, buf, sem, gsem = rest[-7:]
    mark[...] = jnp.zeros_like(mark)
    n, step = buf.shape[:2]
    copies = fetch([(weights.at[pl.ds(i * step, step), :], buf.at[i]) for i in range(n)], sem)
    pieces = [(g, whole.at[pl.ds(k * CAP, CAP), :]) for k, g in enumerate((g0, g1, g2, g3))]
    land(pieces + [(slope, factors.at[0]), (silu, factors.at[1])], gsem)
    for i in range(n):
        cols = slice(i * step, i * step + step)
        copies[i].wait()
        dh = wide_dot(whole[...], buf[i])
        dact[0, :, cols] = (dh * factors[0, :, cols]).astype(BF)
        dact[1, :, cols] = (dh * factors[1, :, cols]).astype(BF)


def back_step(dact, weights, *rest):
    outs, mark, buf, sem = rest[-7:-3], *rest[-3:]
    n, step, inner = buf.shape[0], buf.shape[1], dact.shape[2]
    copies = fetch([(weights.at[pl.ds(i * step, step), :], buf.at[i]) for i in range(n)], sem)
    mark[...] = jnp.zeros_like(mark)
    for i in range(n):
        copies[i].wait()
        got = wide_dot(dact[0], buf[i, :, :inner]) + wide_dot(dact[1], buf[i, :, inner:])
        for k in range(4):
            outs[k][:, i * step : i * step + step] = got[k * CAP : k * CAP + CAP].astype(BF)


def tok_step(mask, a0, a1, a2, a3, *rest):
    out, whole, sem = rest[-3:]
    pieces = (a0, a1, a2, a3)
    land([(a, whole.at[pl.ds(k * CAP, CAP), :]) for k, a in enumerate(pieces)], sem)
    out[...] = jnp.dot(mask[...], whole[...], preferred_element_type=F32).astype(BF)


def tile_step(*refs):
    xs, ds = refs[:4], refs[4:8]
    out, mark, xall, dall, buf, sem, osem = refs[-7:]
    rows = xs[0].shape[0]
    part = [pl.ds(p * rows, rows) for p in range(4)]
    inner = ds[0].shape[2]
    land(
        [(xs[p], xall.at[part[p], :]) for p in range(4)]
        + [
            (ds[p].at[h], dall.at[part[p], pl.ds(h * inner, inner)])
            for p in range(4)
            for h in range(2)
        ],
        sem,
    )
    mark[...] = jnp.zeros_like(mark)
    copies = []
    for b in range(2):
        got = rows_dot(xall[:, b * 512 : b * 512 + 512], dall[...])
        for j in range(4):
            buf[j, b * 128 : b * 128 + 128, :] = got[j * 128 : j * 128 + 128].astype(BF)
            if b == 1:
                copies.append(pltpu.make_async_copy(buf.at[j], out.at[j], osem.at[j]))
                copies[-1].start()
    for copy in copies:
        copy.wait()


def tile_call(xs, ds, after):
    rows, part = xs[0].shape
    wide = 2 * ds[0].shape[2]
    return call(
        tile_step,
        "a" * (8 + len(after)),
        [shape(4, 256, wide), MARK],
        [
            pltpu.VMEM((4 * rows, part), BF),
            pltpu.VMEM((4 * rows, wide), BF),
            pltpu.VMEM((4, 256, wide), BF),
            sems(12),
            sems(4),
        ],
        flops=8 * rows * part * wide,
        moved=8 * rows * (part + wide),
        limit=24,
        placed=(0,),
    )(*xs, *ds, *after)


def down_step(at, both, *rest):
    outs, mark, gall, hall, total, sem = rest[-9:-5], *rest[-5:]
    rows, part, inner = both.shape[1], gall.shape[1], hall.shape[1]
    pairs = []
    for i in range(4):
        pairs.append((both.at[i, :, pl.ds(0, part)], gall.at[pl.ds(i * rows, rows), :]))
        pairs.append((both.at[i, :, pl.ds(part, inner)], hall.at[pl.ds(i * rows, rows), :]))
    land(pairs, sem)
    mark[...] = jnp.zeros_like(mark)
    for b in range(2):
        cols = slice(b * inner // 2, (b + 1) * inner // 2)
        total[cols, :] = rows_dot(hall[:, cols], gall[...])
    for j in (1, 2, 3, 0):
        other = lax.rem(at[1] + j, 4)
        for b in range(2):
            outs[j][b * 96 : b * 96 + 96, :] = total[aligned(b * 4 + other, 96), :].astype(
                outs[j].dtype
            )


def gate_sum(at, parts, keep, send, mark, g, sem):
    half = keep.shape[0]
    copies = fetch([(parts.at[i], g.at[i]) for i in range(4)], sem)
    for copy in copies:
        copy.wait()
    mark[...] = jnp.zeros_like(mark)

    def part(i):
        return sum(g[p, aligned(i, half), :].astype(F32) for p in range(4))

    send[...] = part(1 - at[0]).astype(BF)
    keep[...] = part(at[0])


def sum_step(at, own, r1, r2, r3, *rest):
    keep, send, f, g, sem = rest[-5:]
    half = keep.shape[0]
    land([(own, f), (r1, g.at[0]), (r2, g.at[1]), (r3, g.at[2])], sem)

    def part(i):
        rows = aligned(i, half)
        return f[rows, :] + sum(g[p, rows, :].astype(F32) for p in range(3))

    send[...] = part(1 - at[0]).astype(BF)
    keep[...] = part(at[0])


def sum_call(at, parts, after):
    rows, cols = parts[0].shape
    return call(
        sum_step,
        "saaaa" + "a" * len(after),
        [shape(rows // 2, cols, dtype=F32), shape(rows // 2, cols)],
        [pltpu.VMEM((rows, cols), F32), pltpu.VMEM((3, rows, cols), BF), sems(4)],
        limit=12,
    )(at, *parts, *after)


def shards(tokens, cotangent, routes, gates, gate_up, down_proj):
    gate_up = pltpu.with_memory_space_constraint(gate_up[0], pltpu.HBM)
    down_proj = pltpu.with_memory_space_constraint(down_proj[0], pltpu.HBM)
    w, x, y = lax.axis_index("w"), lax.axis_index("x"), lax.axis_index("y")
    me = lax.axis_index(("v", "c"))
    at = jnp.stack([w, x, y, me]).astype(jnp.int32)
    toks, width = tokens.shape
    inner = down_proj.shape[0]
    rows, part = 4 * CAP, width // 4
    experts = jnp.bitwise_xor(me, jnp.arange(4, dtype=jnp.int32))
    matches = routes[:, :, None] == experts[None, None, :]
    member = jnp.any(matches, axis=1)
    weight = jnp.sum(jnp.where(matches, gates[:, :, None], F32(0.0)), axis=1)
    position = jnp.cumsum(member.astype(jnp.int32), axis=0) - 1
    select = member[:, :, None] & (
        position[:, :, None] == jnp.arange(CAP, dtype=jnp.int32)[None, None, :]
    )
    mask = select.astype(BF).reshape(toks, rows)
    slot_gate = jnp.sum(jnp.where(select, weight[:, :, None], F32(0.0)), axis=0).reshape(rows, 1)
    send_x = rows_dot(mask, tokens).astype(BF).reshape(4, CAP, width)
    send_g = (rows_dot(mask, cotangent) * slot_gate).astype(BF).reshape(4, CAP, width)
    xs = [send_x[0]] + [swap_expert(send_x[k], k) for k in (1, 2, 3)]
    gs = [send_g[0]] + [swap_expert(send_g[k], k) for k in (1, 2, 3)]

    packed = call(
        pack_x, "svvvv", [shape(rows, part)] * 4 + [shape(rows, width)], moved=4 * rows * width
    )(at, *xs)
    xa = [shift(packed[j], "x", j) for j in range(4)]
    n = 2 * inner // 256
    hidden, slope, silu = call(
        act_step,
        "va",
        [shape(rows, inner), shape(rows, inner, dtype=F32), shape(rows, inner, dtype=F32)],
        [pltpu.VMEM((n, width, 256), BF), sems(n)],
        flops=4 * rows * width * inner,
        moved=4 * width * inner,
        limit=18,
    )(packed[4], gate_up)
    n = inner // 256
    dact, mark = call(
        dh_step,
        "aaaaaaa",
        [shape(2, rows, inner), MARK],
        [
            pltpu.VMEM((rows, width), BF),
            pltpu.VMEM((2, rows, inner), F32),
            pltpu.VMEM((n, 256, width), BF),
            sems(n),
            sems(6),
        ],
        flops=2 * rows * width * inner,
        moved=2 * width * inner,
        limit=14,
    )(*gs, slope, silu, down_proj)
    da = [shift(dact, "x", j) for j in range(4)]
    sent, sent_mark = call(
        pack_g,
        "aaaaaaaaa",
        [shape(4, rows, part + inner), MARK],
        [sems(20)],
        moved=4 * rows * width,
        placed=(0,),
    )(*gs, hidden, *xa[1:], mark)
    both = lax.all_to_all(sent, "y", split_axis=0, concat_axis=0, tiled=True)
    n = width // 512
    *back, back_mark = call(
        back_step,
        "vaa",
        [shape(CAP, width)] * 4 + [MARK],
        [pltpu.VMEM((n, 512, 2 * inner), BF), sems(n)],
        flops=4 * rows * width * inner,
        moved=4 * width * inner,
        limit=18,
    )(dact, gate_up, sent_mark)
    parts, mark = tile_call(xa, da, [back_mark])
    gate = lax.all_to_all(parts, "y", split_axis=0, concat_axis=0, tiled=True)
    *parts, _ = call(
        down_step,
        "saa",
        [shape(192, part, dtype=F32)] + [shape(192, part)] * 3 + [MARK],
        [
            pltpu.VMEM((4 * rows, part), BF),
            pltpu.VMEM((4 * rows, inner), BF),
            pltpu.VMEM((inner, part), F32),
            sems(8),
        ],
        flops=8 * rows * part * inner,
        moved=8 * rows * (part + inner),
        limit=16,
    )(at, both, mark)
    down = [parts[0]] + [shift(parts[j], "x", j) for j in (1, 2, 3)]
    arrived = [back[0]] + [swap_expert(back[k], k) for k in (1, 2, 3)]
    keep, send, mark = call(
        gate_sum,
        "sa",
        [shape(128, 2 * inner, dtype=F32), shape(128, 2 * inner), MARK],
        [pltpu.VMEM((4, 256, 2 * inner), BF), sems(4)],
        limit=12,
    )(at, gate)
    gate_up_grad = (keep + swap_w(send).astype(F32)).astype(BF)
    token_grad = call(
        tok_step,
        "vaaaaa",
        [shape(toks, width)],
        [pltpu.VMEM((rows, width), BF), sems(4)],
    )(mask, *arrived, mark)[0]

    keep, send = sum_call(at, down, [])
    down_grad = (keep + swap_w(send).astype(F32)).astype(BF).reshape(4, 24, part)
    cols = [
        shift(lax.dynamic_index_in_dim(down_grad, (y + j) % 4, 0, False), "y", j) for j in range(4)
    ]
    turned = jnp.stack(cols[::-1] + cols[::-1])
    mine = lax.dynamic_slice_in_dim(turned, 3 - y, 4, 0)
    down_grad = jnp.concatenate([mine[i] for i in range(4)], axis=1)

    return token_grad, gate_up_grad[None], down_grad[None]


def solution(mesh):
    fine = Mesh(mesh.devices.reshape(2, 4, 4, 2, 2), AXES)
    rows, expert, dp = P(AXES, None), ("v", "c"), ("w", "x", "y")
    in_specs = (rows, rows, rows, rows, P(expert, None, None), P(expert, None, None))
    out_specs = (rows, P(expert, dp, None), P(expert, dp, None))
    return jax.shard_map(
        shards, mesh=fine, in_specs=in_specs, out_specs=out_specs, check_vma=False
    )
```

```python
import jax
import jax.numpy as jnp
from jax import lax
from jax.experimental import pallas as pl
from jax.experimental.pallas import tpu as pltpu
from jax.sharding import Mesh, PartitionSpec as P

CAP = 48
BF = jnp.bfloat16
F32 = jnp.float32
MB = 1024 * 1024
AXES = ("w", "x", "y", "v", "c")
VMEM = pl.BlockSpec(memory_space=pltpu.VMEM)
SMEM = pl.BlockSpec(memory_space=pltpu.SMEM)
ANY = pl.BlockSpec(memory_space=pl.ANY)
HBM = pl.BlockSpec(memory_space=pltpu.HBM)
MARK = jax.ShapeDtypeStruct((8, 128), F32)


def swap_expert(a, k):
    return lax.ppermute(a, ("v", "c"), [(i, i ^ k) for i in range(4)])


def shift(a, axis, j):
    if j == 0:
        return a
    return lax.ppermute(a, axis, [(i, (i + j) % 4) for i in range(4)])


def swap_w(a):
    return lax.ppermute(a, "w", [(0, 1), (1, 0)])


def rows_dot(a, b):
    return lax.dot_general(a, b, (((0,), (0,)), ((), ())), preferred_element_type=F32)


def wide_dot(a, b):
    return lax.dot_general(a, b, (((1,), (1,)), ((), ())), preferred_element_type=F32)


def shape(*dims, dtype=BF):
    return jax.ShapeDtypeStruct(dims, dtype)


def aligned(i, size):
    return pl.ds(pl.multiple_of(i * size, size), size)


def call(body, ins, outs, scratch=(), flops=0, moved=0, limit=8, placed=()):
    specs = {"s": SMEM, "v": VMEM, "a": ANY}
    return pl.pallas_call(
        body,
        out_shape=[pltpu.HBM(o.shape, o.dtype) if i in placed else o for i, o in enumerate(outs)],
        in_specs=[specs[i] for i in ins],
        out_specs=[HBM if o in placed else VMEM for o in range(len(outs))],
        scratch_shapes=list(scratch),
        compiler_params=pltpu.CompilerParams(vmem_limit_bytes=limit * MB),
        cost_estimate=pl.CostEstimate(flops=flops, bytes_accessed=moved, transcendentals=0),
    )


def fetch(pairs, sems):
    copies = [pltpu.make_async_copy(s, d, sems.at[i]) for i, (s, d) in enumerate(pairs)]
    for copy in copies:
        copy.start()
    return copies


def land(pairs, sems):
    for copy in fetch(pairs, sems):
        copy.wait()


def sems(n):
    return pltpu.SemaphoreType.DMA((n,))


def pack_x(at, x0, x1, x2, x3, *outs):
    whole = outs[4]
    for k, piece in enumerate((x0, x1, x2, x3)):
        rows = slice(k * CAP, k * CAP + CAP)
        whole[rows, :] = piece[...]
        for j in range(4):
            for b in range(2):
                cols = aligned(b * 4 + lax.rem(at[1] + j, 4), 512)
                outs[j][rows, b * 512 : b * 512 + 512] = piece[:, cols]


def pack_g(g0, g1, g2, g3, hidden, *rest):
    out, mark, sem = rest[-3:]
    part, inner = g0.shape[1] // 4, hidden.shape[1]
    mark[...] = jnp.zeros_like(mark)
    pairs = []
    for i in range(4):
        for k, piece in enumerate((g0, g1, g2, g3)):
            to = out.at[i, pl.ds(k * CAP, CAP), pl.ds(0, part)]
            pairs.append((piece.at[:, pl.ds(i * part, part)], to))
        pairs.append((hidden, out.at[i, :, pl.ds(part, inner)]))
    land(pairs, sem)


def act_step(x, weights, hidden, slope, silu, buf, sem):
    inner, step = hidden.shape[1], buf.shape[2]
    n = inner // step
    cuts = [(i, h) for i in range(n) for h in range(2)]
    copies = fetch(
        [
            (weights.at[:, pl.ds(h * inner + i * step, step)], buf.at[2 * i + h])
            for i, h in cuts
        ],
        sem,
    )
    for i in range(n):
        cols = slice(i * step, i * step + step)
        copies[2 * i].wait()
        gpart = jnp.dot(x[...], buf[2 * i], preferred_element_type=F32)
        copies[2 * i + 1].wait()
        upart = jnp.dot(x[...], buf[2 * i + 1], preferred_element_type=F32)
        sig = jax.nn.sigmoid(gpart)
        soft = gpart * sig
        hidden[:, cols] = (soft * upart).astype(BF)
        slope[:, cols] = upart * (sig * (1.0 + gpart * (1.0 - sig)))
        silu[:, cols] = soft


def dh_step(g0, g1, g2, g3, slope, silu, weights, *rest):
    dact, mark, whole, factors, buf, sem, gsem = rest[-7:]
    mark[...] = jnp.zeros_like(mark)
    n, step = buf.shape[:2]
    copies = fetch([(weights.at[pl.ds(i * step, step), :], buf.at[i]) for i in range(n)], sem)
    pieces = [(g, whole.at[pl.ds(k * CAP, CAP), :]) for k, g in enumerate((g0, g1, g2, g3))]
    land(pieces + [(slope, factors.at[0]), (silu, factors.at[1])], gsem)
    for i in range(n):
        cols = slice(i * step, i * step + step)
        copies[i].wait()
        dh = wide_dot(whole[...], buf[i])
        dact[0, :, cols] = (dh * factors[0, :, cols]).astype(BF)
        dact[1, :, cols] = (dh * factors[1, :, cols]).astype(BF)


def back_step(dact, weights, *rest):
    outs, mark, buf, sem = rest[-7:-3], *rest[-3:]
    n, step, inner = buf.shape[0], buf.shape[1], dact.shape[2]
    copies = fetch([(weights.at[pl.ds(i * step, step), :], buf.at[i]) for i in range(n)], sem)
    mark[...] = jnp.zeros_like(mark)
    for i in range(n):
        copies[i].wait()
        got = wide_dot(dact[0], buf[i, :, :inner]) + wide_dot(dact[1], buf[i, :, inner:])
        for k in range(4):
            outs[k][:, i * step : i * step + step] = got[k * CAP : k * CAP + CAP].astype(BF)


def tok_step(mask, a0, a1, a2, a3, out, mark, whole, sem):
    mark[...] = jnp.zeros_like(mark)
    pieces = (a0, a1, a2, a3)
    land([(a, whole.at[pl.ds(k * CAP, CAP), :]) for k, a in enumerate(pieces)], sem)
    out[...] = jnp.dot(mask[...], whole[...], preferred_element_type=F32).astype(BF)


def tile_step(*refs):
    xs, ds = refs[:4], refs[4:8]
    out, mark, xall, dall, buf, sem, osem = refs[-7:]
    rows = xs[0].shape[0]
    part = [pl.ds(p * rows, rows) for p in range(4)]
    inner = ds[0].shape[2]
    land(
        [(xs[p], xall.at[part[p], :]) for p in range(4)]
        + [
            (ds[p].at[h], dall.at[part[p], pl.ds(h * inner, inner)])
            for p in range(4)
            for h in range(2)
        ],
        sem,
    )
    mark[...] = jnp.zeros_like(mark)
    copies = []
    for b in range(2):
        got = rows_dot(xall[:, b * 512 : b * 512 + 512], dall[...])
        for j in range(4):
            buf[j, b * 128 : b * 128 + 128, :] = got[j * 128 : j * 128 + 128].astype(BF)
            if b == 1:
                copies.append(pltpu.make_async_copy(buf.at[j], out.at[j], osem.at[j]))
                copies[-1].start()
    for copy in copies:
        copy.wait()


def tile_call(xs, ds, after):
    rows, part = xs[0].shape
    wide = 2 * ds[0].shape[2]
    return call(
        tile_step,
        "a" * (8 + len(after)),
        [shape(4, 256, wide), MARK],
        [
            pltpu.VMEM((4 * rows, part), BF),
            pltpu.VMEM((4 * rows, wide), BF),
            pltpu.VMEM((4, 256, wide), BF),
            sems(12),
            sems(4),
        ],
        flops=8 * rows * part * wide,
        moved=8 * rows * (part + wide),
        limit=24,
        placed=(0,),
    )(*xs, *ds, *after)


def down_step(at, both, *rest):
    outs, mark, gall, hall, total, sem = rest[-9:-5], *rest[-5:]
    rows, part, inner = both.shape[1], gall.shape[1], hall.shape[1]
    pairs = []
    for i in range(4):
        pairs.append((both.at[i, :, pl.ds(0, part)], gall.at[pl.ds(i * rows, rows), :]))
        pairs.append((both.at[i, :, pl.ds(part, inner)], hall.at[pl.ds(i * rows, rows), :]))
    land(pairs, sem)
    mark[...] = jnp.zeros_like(mark)
    for b in range(2):
        cols = slice(b * inner // 2, (b + 1) * inner // 2)
        total[cols, :] = rows_dot(hall[:, cols], gall[...])
    for j in (1, 2, 3, 0):
        other = lax.rem(at[1] + j, 4)
        for b in range(2):
            outs[j][b * 96 : b * 96 + 96, :] = total[aligned(b * 4 + other, 96), :].astype(
                outs[j].dtype
            )


def gate_sum(at, parts, keep, send, mark, g, sem):
    mark[...] = jnp.zeros_like(mark)
    half = keep.shape[0]
    copies = fetch([(parts.at[i], g.at[i]) for i in range(4)], sem)
    for copy in copies:
        copy.wait()

    def part(i):
        return sum(g[p, aligned(i, half), :].astype(F32) for p in range(4))

    send[...] = part(1 - at[0]).astype(BF)
    keep[...] = part(at[0])


def sum_step(at, own, r1, r2, r3, *rest):
    keep, send, f, g, sem = rest[-5:]
    half = keep.shape[0]
    land([(own, f), (r1, g.at[0]), (r2, g.at[1]), (r3, g.at[2])], sem)

    def part(i):
        rows = aligned(i, half)
        return f[rows, :] + sum(g[p, rows, :].astype(F32) for p in range(3))

    send[...] = part(1 - at[0]).astype(BF)
    keep[...] = part(at[0])


def sum_call(at, parts, after):
    rows, cols = parts[0].shape
    return call(
        sum_step,
        "saaaa" + "a" * len(after),
        [shape(rows // 2, cols, dtype=F32), shape(rows // 2, cols)],
        [pltpu.VMEM((rows, cols), F32), pltpu.VMEM((3, rows, cols), BF), sems(4)],
        limit=12,
    )(at, *parts, *after)


def join_step(keep, theirs, mark, out):
    out[...] = (keep[...] + theirs[...].astype(F32)).astype(BF)


def shards(tokens, cotangent, routes, gates, gate_up, down_proj):
    gate_up = pltpu.with_memory_space_constraint(gate_up[0], pltpu.HBM)
    down_proj = pltpu.with_memory_space_constraint(down_proj[0], pltpu.HBM)
    w, x, y = lax.axis_index("w"), lax.axis_index("x"), lax.axis_index("y")
    me = lax.axis_index(("v", "c"))
    at = jnp.stack([w, x, y, me]).astype(jnp.int32)
    toks, width = tokens.shape
    inner = down_proj.shape[0]
    rows, part = 4 * CAP, width // 4
    experts = jnp.bitwise_xor(me, jnp.arange(4, dtype=jnp.int32))
    matches = routes[:, :, None] == experts[None, None, :]
    member = jnp.any(matches, axis=1)
    weight = jnp.sum(jnp.where(matches, gates[:, :, None], F32(0.0)), axis=1)
    position = jnp.cumsum(member.astype(jnp.int32), axis=0) - 1
    select = member[:, :, None] & (
        position[:, :, None] == jnp.arange(CAP, dtype=jnp.int32)[None, None, :]
    )
    mask = select.astype(BF).reshape(toks, rows)
    slot_gate = jnp.sum(jnp.where(select, weight[:, :, None], F32(0.0)), axis=0).reshape(rows, 1)
    send_x = rows_dot(mask, tokens).astype(BF).reshape(4, CAP, width)
    send_g = (rows_dot(mask, cotangent) * slot_gate).astype(BF).reshape(4, CAP, width)
    xs = [send_x[0]] + [swap_expert(send_x[k], k) for k in (1, 2, 3)]
    gs = [send_g[0]] + [swap_expert(send_g[k], k) for k in (1, 2, 3)]

    packed = call(
        pack_x, "svvvv", [shape(rows, part)] * 4 + [shape(rows, width)], moved=4 * rows * width
    )(at, *xs)
    xa = [shift(packed[j], "x", j) for j in range(4)]
    n = 2 * inner // 256
    hidden, slope, silu = call(
        act_step,
        "va",
        [shape(rows, inner), shape(rows, inner, dtype=F32), shape(rows, inner, dtype=F32)],
        [pltpu.VMEM((n, width, 256), BF), sems(n)],
        flops=4 * rows * width * inner,
        moved=4 * width * inner,
        limit=18,
    )(packed[4], gate_up)
    n = inner // 256
    dact, mark = call(
        dh_step,
        "aaaaaaa",
        [shape(2, rows, inner), MARK],
        [
            pltpu.VMEM((rows, width), BF),
            pltpu.VMEM((2, rows, inner), F32),
            pltpu.VMEM((n, 256, width), BF),
            sems(n),
            sems(6),
        ],
        flops=2 * rows * width * inner,
        moved=2 * width * inner,
        limit=14,
    )(*gs, slope, silu, down_proj)
    da = [shift(dact, "x", j) for j in range(4)]
    sent, sent_mark = call(
        pack_g,
        "aaaaaaaaa",
        [shape(4, rows, part + inner), MARK],
        [sems(20)],
        moved=4 * rows * width,
        placed=(0,),
    )(*gs, hidden, *xa[1:], mark)
    both = lax.all_to_all(sent, "y", split_axis=0, concat_axis=0, tiled=True)
    n = width // 512
    *back, back_mark = call(
        back_step,
        "vaa",
        [shape(CAP, width)] * 4 + [MARK],
        [pltpu.VMEM((n, 512, 2 * inner), BF), sems(n)],
        flops=4 * rows * width * inner,
        moved=4 * width * inner,
        limit=18,
    )(dact, gate_up, sent_mark)
    arrived = [back[0]] + [swap_expert(back[k], k) for k in (1, 2, 3)]
    parts, mark = tile_call(xa, da, [arrived[2]])
    gate = lax.all_to_all(parts, "y", split_axis=0, concat_axis=0, tiled=True)
    *parts, _ = call(
        down_step,
        "saa",
        [shape(192, part, dtype=F32)] + [shape(192, part)] * 3 + [MARK],
        [
            pltpu.VMEM((4 * rows, part), BF),
            pltpu.VMEM((4 * rows, inner), BF),
            pltpu.VMEM((inner, part), F32),
            sems(8),
        ],
        flops=8 * rows * part * inner,
        moved=8 * rows * (part + inner),
        limit=16,
    )(at, both, mark)
    down = [parts[0]] + [shift(parts[j], "x", j) for j in (1, 2, 3)]
    token_grad, tok_mark = call(
        tok_step,
        "vaaaa",
        [shape(toks, width), MARK],
        [pltpu.VMEM((rows, width), BF), sems(4)],
    )(mask, *arrived)

    gate_keep, gate_send, mark = call(
        gate_sum,
        "sa",
        [shape(128, 2 * inner, dtype=F32), shape(128, 2 * inner), MARK],
        [pltpu.VMEM((4, 256, 2 * inner), BF), sems(4)],
        limit=12,
    )(at, gate)
    gate_up_grad = (gate_keep + swap_w(gate_send).astype(F32)).astype(BF)
    keep, send = sum_call(at, down, [tok_mark])
    down_grad = call(join_step, "vva", [shape(96, part)], moved=800 * part)(
        keep, swap_w(send), mark
    )[0].reshape(4, 24, part)
    cols = [
        shift(lax.dynamic_index_in_dim(down_grad, (y + j) % 4, 0, False), "y", j) for j in range(4)
    ]
    turned = jnp.stack(cols[::-1] + cols[::-1])
    mine = lax.dynamic_slice_in_dim(turned, 3 - y, 4, 0)
    down_grad = jnp.concatenate([mine[i] for i in range(4)], axis=1)

    return token_grad, gate_up_grad[None], down_grad[None]


def solution(mesh):
    fine = Mesh(mesh.devices.reshape(2, 4, 4, 2, 2), AXES)
    rows, expert, dp = P(AXES, None), ("v", "c"), ("w", "x", "y")
    in_specs = (rows, rows, rows, rows, P(expert, None, None), P(expert, None, None))
    out_specs = (rows, P(expert, dp, None), P(expert, dp, None))
    return jax.shard_map(
        shards, mesh=fine, in_specs=in_specs, out_specs=out_specs, check_vma=False
    )
```

```python
import jax
import jax.numpy as jnp
from jax import lax
from jax.experimental import pallas as pl
from jax.experimental.pallas import tpu as pltpu
from jax.sharding import Mesh, PartitionSpec as P

CAP = 48
BF = jnp.bfloat16
F32 = jnp.float32
MB = 1024 * 1024
AXES = ("w", "x", "y", "v", "c")
VMEM = pl.BlockSpec(memory_space=pltpu.VMEM)
SMEM = pl.BlockSpec(memory_space=pltpu.SMEM)
ANY = pl.BlockSpec(memory_space=pl.ANY)
HBM = pl.BlockSpec(memory_space=pltpu.HBM)
MARK = jax.ShapeDtypeStruct((8, 128), F32)


def swap_expert(a, k):
    return lax.ppermute(a, ("v", "c"), [(i, i ^ k) for i in range(4)])


def shift(a, axis, j):
    if j == 0:
        return a
    return lax.ppermute(a, axis, [(i, (i + j) % 4) for i in range(4)])


def swap_w(a):
    return lax.ppermute(a, "w", [(0, 1), (1, 0)])


def rows_dot(a, b):
    return lax.dot_general(a, b, (((0,), (0,)), ((), ())), preferred_element_type=F32)


def wide_dot(a, b):
    return lax.dot_general(a, b, (((1,), (1,)), ((), ())), preferred_element_type=F32)


def shape(*dims, dtype=BF):
    return jax.ShapeDtypeStruct(dims, dtype)


def aligned(i, size):
    return pl.ds(pl.multiple_of(i * size, size), size)


def call(body, ins, outs, scratch=(), flops=0, moved=0, limit=8, placed=()):
    specs = {"s": SMEM, "v": VMEM, "a": ANY}
    return pl.pallas_call(
        body,
        out_shape=[pltpu.HBM(o.shape, o.dtype) if i in placed else o for i, o in enumerate(outs)],
        in_specs=[specs[i] for i in ins],
        out_specs=[HBM if o in placed else VMEM for o in range(len(outs))],
        scratch_shapes=list(scratch),
        compiler_params=pltpu.CompilerParams(vmem_limit_bytes=limit * MB),
        cost_estimate=pl.CostEstimate(flops=flops, bytes_accessed=moved, transcendentals=0),
    )


def fetch(pairs, sems):
    copies = [pltpu.make_async_copy(s, d, sems.at[i]) for i, (s, d) in enumerate(pairs)]
    for copy in copies:
        copy.start()
    return copies


def land(pairs, sems):
    for copy in fetch(pairs, sems):
        copy.wait()


def sems(n):
    return pltpu.SemaphoreType.DMA((n,))


def pack_x(at, x0, x1, x2, x3, *outs):
    whole = outs[4]
    for k, piece in enumerate((x0, x1, x2, x3)):
        rows = slice(k * CAP, k * CAP + CAP)
        whole[rows, :] = piece[...]
        for j in range(4):
            for b in range(2):
                cols = aligned(b * 4 + lax.rem(at[1] + j, 4), 512)
                outs[j][rows, b * 512 : b * 512 + 512] = piece[:, cols]


def pack_g(g0, g1, g2, g3, hidden, *rest):
    out, mark, sem = rest[-3:]
    part, inner = g0.shape[1] // 4, hidden.shape[1]
    mark[...] = jnp.zeros_like(mark)
    pairs = []
    for i in range(4):
        for k, piece in enumerate((g0, g1, g2, g3)):
            to = out.at[i, pl.ds(k * CAP, CAP), pl.ds(0, part)]
            pairs.append((piece.at[:, pl.ds(i * part, part)], to))
        pairs.append((hidden, out.at[i, :, pl.ds(part, inner)]))
    land(pairs, sem)


def act_step(x, weights, hidden, slope, silu, buf, sem):
    inner, step = hidden.shape[1], buf.shape[2]
    n = inner // step
    cuts = [(i, h) for i in range(n) for h in range(2)]
    copies = fetch(
        [
            (weights.at[:, pl.ds(h * inner + i * step, step)], buf.at[2 * i + h])
            for i, h in cuts
        ],
        sem,
    )
    for i in range(n):
        cols = slice(i * step, i * step + step)
        copies[2 * i].wait()
        gpart = jnp.dot(x[...], buf[2 * i], preferred_element_type=F32)
        copies[2 * i + 1].wait()
        upart = jnp.dot(x[...], buf[2 * i + 1], preferred_element_type=F32)
        sig = jax.nn.sigmoid(gpart)
        soft = gpart * sig
        hidden[:, cols] = (soft * upart).astype(BF)
        slope[:, cols] = upart * (sig * (1.0 + gpart * (1.0 - sig)))
        silu[:, cols] = soft


def dh_step(g0, g1, g2, g3, slope, silu, weights, *rest):
    dact, mark, whole, factors, buf, sem, gsem = rest[-7:]
    mark[...] = jnp.zeros_like(mark)
    n, step = buf.shape[:2]
    copies = fetch([(weights.at[pl.ds(i * step, step), :], buf.at[i]) for i in range(n)], sem)
    pieces = [(g, whole.at[pl.ds(k * CAP, CAP), :]) for k, g in enumerate((g0, g1, g2, g3))]
    land(pieces + [(slope, factors.at[0]), (silu, factors.at[1])], gsem)
    for i in range(n):
        cols = slice(i * step, i * step + step)
        copies[i].wait()
        dh = wide_dot(whole[...], buf[i])
        dact[0, :, cols] = (dh * factors[0, :, cols]).astype(BF)
        dact[1, :, cols] = (dh * factors[1, :, cols]).astype(BF)


def back_step(dact, weights, *rest):
    outs, mark, buf, sem = rest[-7:-3], *rest[-3:]
    n, step, inner = buf.shape[0], buf.shape[1], dact.shape[2]
    copies = fetch([(weights.at[pl.ds(i * step, step), :], buf.at[i]) for i in range(n)], sem)
    mark[...] = jnp.zeros_like(mark)
    for i in range(n):
        copies[i].wait()
        got = wide_dot(dact[0], buf[i, :, :inner]) + wide_dot(dact[1], buf[i, :, inner:])
        for k in range(4):
            outs[k][:, i * step : i * step + step] = got[k * CAP : k * CAP + CAP].astype(BF)


def tok_step(mask, a0, a1, a2, a3, out, mark, whole, sem):
    mark[...] = jnp.zeros_like(mark)
    pieces = (a0, a1, a2, a3)
    land([(a, whole.at[pl.ds(k * CAP, CAP), :]) for k, a in enumerate(pieces)], sem)
    out[...] = jnp.dot(mask[...], whole[...], preferred_element_type=F32).astype(BF)


def tile_step(*refs):
    xs, ds = refs[:4], refs[4:8]
    out, mark, xall, dall, buf, sem, osem = refs[-7:]
    rows = xs[0].shape[0]
    part = [pl.ds(p * rows, rows) for p in range(4)]
    inner = ds[0].shape[2]
    land(
        [(xs[p], xall.at[part[p], :]) for p in range(4)]
        + [
            (ds[p].at[h], dall.at[part[p], pl.ds(h * inner, inner)])
            for p in range(4)
            for h in range(2)
        ],
        sem,
    )
    mark[...] = jnp.zeros_like(mark)
    copies = []
    for b in range(2):
        got = rows_dot(xall[:, b * 512 : b * 512 + 512], dall[...])
        for j in range(4):
            i = b * 4 + j
            buf[i] = got[j * 128 : j * 128 + 128].astype(BF)
            copies.append(pltpu.make_async_copy(buf.at[i], out.at[i], osem.at[i]))
            copies[-1].start()
    for copy in copies:
        copy.wait()


def tile_call(xs, ds, after):
    rows, part = xs[0].shape
    wide = 2 * ds[0].shape[2]
    return call(
        tile_step,
        "a" * (8 + len(after)),
        [shape(8, 128, wide), MARK],
        [
            pltpu.VMEM((4 * rows, part), BF),
            pltpu.VMEM((4 * rows, wide), BF),
            pltpu.VMEM((8, 128, wide), BF),
            sems(12),
            sems(8),
        ],
        flops=8 * rows * part * wide,
        moved=8 * rows * (part + wide),
        limit=24,
        placed=(0,),
    )(*xs, *ds, *after)


def down_step(at, both, *rest):
    outs, mark, gall, hall, total, sem = rest[-9:-5], *rest[-5:]
    rows, part, inner = both.shape[1], gall.shape[1], hall.shape[1]
    pairs = []
    for i in range(4):
        pairs.append((both.at[i, :, pl.ds(0, part)], gall.at[pl.ds(i * rows, rows), :]))
        pairs.append((both.at[i, :, pl.ds(part, inner)], hall.at[pl.ds(i * rows, rows), :]))
    land(pairs, sem)
    mark[...] = jnp.zeros_like(mark)
    for b in range(2):
        cols = slice(b * inner // 2, (b + 1) * inner // 2)
        total[cols, :] = rows_dot(hall[:, cols], gall[...])
    for j in (1, 2, 3, 0):
        other = lax.rem(at[1] + j, 4)
        for b in range(2):
            outs[j][b * 96 : b * 96 + 96, :] = total[aligned(b * 4 + other, 96), :].astype(
                outs[j].dtype
            )


def gate_sum(parts, out, mark, g, sem):
    copies = fetch([(parts.at[i], g.at[i]) for i in range(8)], sem)
    mark[...] = jnp.zeros_like(mark)
    for copy in copies:
        copy.wait()
    out[...] = sum(g[i].astype(F32) for i in range(8)).astype(BF)


def sum_step(at, own, r1, r2, r3, *rest):
    keep, send, f, g, sem = rest[-5:]
    half = keep.shape[0]
    land([(own, f), (r1, g.at[0]), (r2, g.at[1]), (r3, g.at[2])], sem)

    def part(i):
        rows = aligned(i, half)
        return f[rows, :] + sum(g[p, rows, :].astype(F32) for p in range(3))

    send[...] = part(1 - at[0]).astype(BF)
    keep[...] = part(at[0])


def sum_call(at, parts, after):
    rows, cols = parts[0].shape
    return call(
        sum_step,
        "saaaa" + "a" * len(after),
        [shape(rows // 2, cols, dtype=F32), shape(rows // 2, cols)],
        [pltpu.VMEM((rows, cols), F32), pltpu.VMEM((3, rows, cols), BF), sems(4)],
        limit=12,
    )(at, *parts, *after)


def join_step(at, c0, c1, c2, c3, mark, out):
    for j, piece in enumerate((c0, c1, c2, c3)):
        out[:, aligned(lax.rem(at[2] + 4 - j, 4), piece.shape[1])] = piece[...]


def shards(tokens, cotangent, routes, gates, gate_up, down_proj):
    gate_up = pltpu.with_memory_space_constraint(gate_up[0], pltpu.HBM)
    down_proj = pltpu.with_memory_space_constraint(down_proj[0], pltpu.HBM)
    w, x, y = lax.axis_index("w"), lax.axis_index("x"), lax.axis_index("y")
    me = lax.axis_index(("v", "c"))
    at = jnp.stack([w, x, y, me]).astype(jnp.int32)
    toks, width = tokens.shape
    inner = down_proj.shape[0]
    rows, part = 4 * CAP, width // 4
    experts = jnp.bitwise_xor(me, jnp.arange(4, dtype=jnp.int32))
    matches = routes[:, :, None] == experts[None, None, :]
    member = jnp.any(matches, axis=1)
    weight = jnp.sum(jnp.where(matches, gates[:, :, None], F32(0.0)), axis=1)
    position = jnp.cumsum(member.astype(jnp.int32), axis=0) - 1
    select = member[:, :, None] & (
        position[:, :, None] == jnp.arange(CAP, dtype=jnp.int32)[None, None, :]
    )
    mask = select.astype(BF).reshape(toks, rows)
    slot_gate = jnp.sum(jnp.where(select, weight[:, :, None], F32(0.0)), axis=0).reshape(rows, 1)
    send_x = rows_dot(mask, tokens).astype(BF).reshape(4, CAP, width)
    send_g = (rows_dot(mask, cotangent) * slot_gate).astype(BF).reshape(4, CAP, width)
    xs = [send_x[0]] + [swap_expert(send_x[k], k) for k in (1, 2, 3)]
    gs = [send_g[0]] + [swap_expert(send_g[k], k) for k in (1, 2, 3)]

    packed = call(
        pack_x, "svvvv", [shape(rows, part)] * 4 + [shape(rows, width)], moved=4 * rows * width
    )(at, *xs)
    xa = [shift(packed[j], "x", j) for j in range(4)]
    n = 2 * inner // 256
    hidden, slope, silu = call(
        act_step,
        "va",
        [shape(rows, inner), shape(rows, inner, dtype=F32), shape(rows, inner, dtype=F32)],
        [pltpu.VMEM((n, width, 256), BF), sems(n)],
        flops=4 * rows * width * inner,
        moved=4 * width * inner,
        limit=18,
    )(packed[4], gate_up)
    n = inner // 256
    dact, mark = call(
        dh_step,
        "aaaaaaa",
        [shape(2, rows, inner), MARK],
        [
            pltpu.VMEM((rows, width), BF),
            pltpu.VMEM((2, rows, inner), F32),
            pltpu.VMEM((n, 256, width), BF),
            sems(n),
            sems(6),
        ],
        flops=2 * rows * width * inner,
        moved=2 * width * inner,
        limit=14,
    )(*gs, slope, silu, down_proj)
    da = [shift(dact, "x", j) for j in range(4)]
    sent, sent_mark = call(
        pack_g,
        "aaaaaaaaa",
        [shape(4, rows, part + inner), MARK],
        [sems(20)],
        moved=4 * rows * width,
        placed=(0,),
    )(*gs, hidden, *xa[1:], mark)
    both = lax.all_to_all(sent, "y", split_axis=0, concat_axis=0, tiled=True)
    n = width // 512
    *back, back_mark = call(
        back_step,
        "vaa",
        [shape(CAP, width)] * 4 + [MARK],
        [pltpu.VMEM((n, 512, 2 * inner), BF), sems(n)],
        flops=4 * rows * width * inner,
        moved=4 * width * inner,
        limit=18,
    )(dact, gate_up, sent_mark)
    arrived = [back[0]] + [swap_expert(back[k], k) for k in (1, 2, 3)]
    parts, mark = tile_call(xa, da, [arrived[2]])
    gate = lax.all_to_all(parts, ("w", "y"), split_axis=0, concat_axis=0, tiled=True)
    *parts, _ = call(
        down_step,
        "saa",
        [shape(192, part, dtype=F32)] + [shape(192, part)] * 3 + [MARK],
        [
            pltpu.VMEM((4 * rows, part), BF),
            pltpu.VMEM((4 * rows, inner), BF),
            pltpu.VMEM((inner, part), F32),
            sems(8),
        ],
        flops=8 * rows * part * inner,
        moved=8 * rows * (part + inner),
        limit=16,
    )(at, both, mark)
    down = [parts[0]] + [shift(parts[j], "x", j) for j in (1, 2, 3)]
    token_grad, tok_mark = call(
        tok_step,
        "vaaaa",
        [shape(toks, width), MARK],
        [pltpu.VMEM((rows, width), BF), sems(4)],
    )(mask, *arrived)

    gate_up_grad, mark = call(
        gate_sum,
        "a",
        [shape(128, 2 * inner), MARK],
        [pltpu.VMEM((8, 128, 2 * inner), BF), sems(8)],
        limit=12,
    )(gate)
    keep, send = sum_call(at, down, [tok_mark])
    down_grad = (keep + swap_w(send).astype(F32)).astype(BF).reshape(4, 24, part)
    cols = [
        shift(lax.dynamic_index_in_dim(down_grad, (y + j) % 4, 0, False), "y", j) for j in range(4)
    ]
    down_grad = call(join_step, "svvvva", [shape(24, width)])(at, *cols, mark)[0]

    return token_grad, gate_up_grad[None], down_grad[None]


def solution(mesh):
    fine = Mesh(mesh.devices.reshape(2, 4, 4, 2, 2), AXES)
    rows, expert, dp = P(AXES, None), ("v", "c"), ("w", "x", "y")
    in_specs = (rows, rows, rows, rows, P(expert, None, None), P(expert, None, None))
    out_specs = (rows, P(expert, dp, None), P(expert, dp, None))
    return jax.shard_map(
        shards, mesh=fine, in_specs=in_specs, out_specs=out_specs, check_vma=False
    )
```

```python
import jax
import jax.numpy as jnp
from jax import lax
from jax.experimental import pallas as pl
from jax.experimental.pallas import tpu as pltpu
from jax.sharding import Mesh, PartitionSpec as P

CAP = 48
BF = jnp.bfloat16
F32 = jnp.float32
MB = 1024 * 1024
AXES = ("w", "x", "y", "v", "c")
VMEM = pl.BlockSpec(memory_space=pltpu.VMEM)
SMEM = pl.BlockSpec(memory_space=pltpu.SMEM)
ANY = pl.BlockSpec(memory_space=pl.ANY)
HBM = pl.BlockSpec(memory_space=pltpu.HBM)
MARK = jax.ShapeDtypeStruct((8, 128), F32)


def swap_expert(a, k):
    return lax.ppermute(a, ("v", "c"), [(i, i ^ k) for i in range(4)])


def shift(a, axis, j):
    if j == 0:
        return a
    return lax.ppermute(a, axis, [(i, (i + j) % 4) for i in range(4)])


def swap_w(a):
    return lax.ppermute(a, "w", [(0, 1), (1, 0)])


def rows_dot(a, b):
    return lax.dot_general(a, b, (((0,), (0,)), ((), ())), preferred_element_type=F32)


def wide_dot(a, b):
    return lax.dot_general(a, b, (((1,), (1,)), ((), ())), preferred_element_type=F32)


def shape(*dims, dtype=BF):
    return jax.ShapeDtypeStruct(dims, dtype)


def aligned(i, size):
    return pl.ds(pl.multiple_of(i * size, size), size)


def call(body, ins, outs, scratch=(), flops=0, moved=0, limit=8, placed=()):
    specs = {"s": SMEM, "v": VMEM, "a": ANY}
    return pl.pallas_call(
        body,
        out_shape=[pltpu.HBM(o.shape, o.dtype) if i in placed else o for i, o in enumerate(outs)],
        in_specs=[specs[i] for i in ins],
        out_specs=[HBM if o in placed else VMEM for o in range(len(outs))],
        scratch_shapes=list(scratch),
        compiler_params=pltpu.CompilerParams(vmem_limit_bytes=limit * MB),
        cost_estimate=pl.CostEstimate(flops=flops, bytes_accessed=moved, transcendentals=0),
    )


def fetch(pairs, sems):
    copies = [pltpu.make_async_copy(s, d, sems.at[i]) for i, (s, d) in enumerate(pairs)]
    for copy in copies:
        copy.start()
    return copies


def land(pairs, sems):
    for copy in fetch(pairs, sems):
        copy.wait()


def sems(n):
    return pltpu.SemaphoreType.DMA((n,))


def pack_x(at, x0, x1, x2, x3, *outs):
    whole = outs[4]
    for k, piece in enumerate((x0, x1, x2, x3)):
        rows = slice(k * CAP, k * CAP + CAP)
        whole[rows, :] = piece[...]
        for j in range(4):
            for b in range(2):
                cols = aligned(b * 4 + lax.rem(at[1] + j, 4), 512)
                outs[j][rows, b * 512 : b * 512 + 512] = piece[:, cols]


def pack_g(g0, g1, g2, g3, hidden, *rest):
    out, mark, sem = rest[-3:]
    part, inner = g0.shape[1] // 4, hidden.shape[1]
    mark[...] = jnp.zeros_like(mark)
    pairs = []
    for i in range(4):
        for k, piece in enumerate((g0, g1, g2, g3)):
            to = out.at[i, pl.ds(k * CAP, CAP), pl.ds(0, part)]
            pairs.append((piece.at[:, pl.ds(i * part, part)], to))
        pairs.append((hidden, out.at[i, :, pl.ds(part, inner)]))
    land(pairs, sem)


def act_step(x, weights, hidden, slope, silu, buf, sem):
    inner, step = hidden.shape[1], buf.shape[2]
    n = inner // step
    cuts = [(i, h) for i in range(n) for h in range(2)]
    copies = fetch(
        [
            (weights.at[:, pl.ds(h * inner + i * step, step)], buf.at[2 * i + h])
            for i, h in cuts
        ],
        sem,
    )
    for i in range(n):
        cols = slice(i * step, i * step + step)
        copies[2 * i].wait()
        gpart = jnp.dot(x[...], buf[2 * i], preferred_element_type=F32)
        copies[2 * i + 1].wait()
        upart = jnp.dot(x[...], buf[2 * i + 1], preferred_element_type=F32)
        sig = jax.nn.sigmoid(gpart)
        soft = gpart * sig
        hidden[:, cols] = (soft * upart).astype(BF)
        slope[:, cols] = upart * (sig * (1.0 + gpart * (1.0 - sig)))
        silu[:, cols] = soft


def dh_step(g0, g1, g2, g3, slope, silu, weights, *rest):
    dact, mark, whole, factors, buf, sem, gsem = rest[-7:]
    mark[...] = jnp.zeros_like(mark)
    n, step = buf.shape[:2]
    copies = fetch([(weights.at[pl.ds(i * step, step), :], buf.at[i]) for i in range(n)], sem)
    pieces = [(g, whole.at[pl.ds(k * CAP, CAP), :]) for k, g in enumerate((g0, g1, g2, g3))]
    land(pieces + [(slope, factors.at[0]), (silu, factors.at[1])], gsem)
    for i in range(n):
        cols = slice(i * step, i * step + step)
        copies[i].wait()
        dh = wide_dot(whole[...], buf[i])
        dact[0, :, cols] = (dh * factors[0, :, cols]).astype(BF)
        dact[1, :, cols] = (dh * factors[1, :, cols]).astype(BF)


def back_step(dact, weights, *rest):
    outs, mark, buf, sem = rest[-7:-3], *rest[-3:]
    n, step, inner = buf.shape[0], buf.shape[1], dact.shape[2]
    copies = fetch([(weights.at[pl.ds(i * step, step), :], buf.at[i]) for i in range(n)], sem)
    mark[...] = jnp.zeros_like(mark)
    for i in range(n):
        copies[i].wait()
        got = wide_dot(dact[0], buf[i, :, :inner]) + wide_dot(dact[1], buf[i, :, inner:])
        for k in range(4):
            outs[k][:, i * step : i * step + step] = got[k * CAP : k * CAP + CAP].astype(BF)


def tok_step(mask, a0, a1, a2, a3, out, mark, whole, sem):
    mark[...] = jnp.zeros_like(mark)
    pieces = (a0, a1, a2, a3)
    land([(a, whole.at[pl.ds(k * CAP, CAP), :]) for k, a in enumerate(pieces)], sem)
    out[...] = jnp.dot(mask[...], whole[...], preferred_element_type=F32).astype(BF)


def tile_step(*refs):
    xs, ds = refs[:4], refs[4:8]
    out, mark, xall, dall, buf, sem, osem = refs[-7:]
    rows = xs[0].shape[0]
    part = [pl.ds(p * rows, rows) for p in range(4)]
    inner = ds[0].shape[2]
    land(
        [(xs[p], xall.at[part[p], :]) for p in range(4)]
        + [
            (ds[p].at[h], dall.at[part[p], pl.ds(h * inner, inner)])
            for p in range(4)
            for h in range(2)
        ],
        sem,
    )
    mark[...] = jnp.zeros_like(mark)
    copies = []
    for b in range(2):
        got = rows_dot(xall[:, b * 512 : b * 512 + 512], dall[...])
        for j in range(4):
            i = b * 4 + j
            buf[i] = got[j * 128 : j * 128 + 128].astype(BF)
            copies.append(pltpu.make_async_copy(buf.at[i], out.at[i], osem.at[i]))
            copies[-1].start()
    for copy in copies:
        copy.wait()


def tile_call(xs, ds, after):
    rows, part = xs[0].shape
    wide = 2 * ds[0].shape[2]
    return call(
        tile_step,
        "a" * (8 + len(after)),
        [shape(8, 128, wide), MARK],
        [
            pltpu.VMEM((4 * rows, part), BF),
            pltpu.VMEM((4 * rows, wide), BF),
            pltpu.VMEM((8, 128, wide), BF),
            sems(12),
            sems(8),
        ],
        flops=8 * rows * part * wide,
        moved=8 * rows * (part + wide),
        limit=24,
        placed=(0,),
    )(*xs, *ds, *after)


def down_step(at, both, *rest):
    outs, mark, gall, hall, total, sem = rest[-9:-5], *rest[-5:]
    rows, part, inner = both.shape[1], gall.shape[1], hall.shape[1]
    pairs = []
    for i in range(4):
        pairs.append((both.at[i, :, pl.ds(0, part)], gall.at[pl.ds(i * rows, rows), :]))
        pairs.append((both.at[i, :, pl.ds(part, inner)], hall.at[pl.ds(i * rows, rows), :]))
    land(pairs, sem)
    mark[...] = jnp.zeros_like(mark)
    for b in range(2):
        cols = slice(b * inner // 2, (b + 1) * inner // 2)
        total[cols, :] = rows_dot(hall[:, cols], gall[...])
    for j in (1, 2, 3, 0):
        other = lax.rem(at[1] + j, 4)
        for b in range(2):
            outs[j][b * 96 : b * 96 + 96, :] = total[aligned(b * 4 + other, 96), :].astype(
                outs[j].dtype
            )


def gate_sum(parts, out, mark, g, sem):
    copies = fetch([(parts.at[i], g.at[i]) for i in range(8)], sem)
    mark[...] = jnp.zeros_like(mark)
    for copy in copies:
        copy.wait()
    out[...] = sum(g[i].astype(F32) for i in range(8)).astype(BF)


def sum_step(at, own, r1, r2, r3, *rest):
    keep, send, f, g, sem = rest[-5:]
    half = keep.shape[0]
    land([(own, f), (r1, g.at[0]), (r2, g.at[1]), (r3, g.at[2])], sem)

    def part(i):
        rows = aligned(i, half)
        return f[rows, :] + sum(g[p, rows, :].astype(F32) for p in range(3))

    send[...] = part(1 - at[0]).astype(BF)
    keep[...] = part(at[0])


def sum_call(at, parts, after):
    rows, cols = parts[0].shape
    return call(
        sum_step,
        "saaaa" + "a" * len(after),
        [shape(rows // 2, cols, dtype=F32), shape(rows // 2, cols)],
        [pltpu.VMEM((rows, cols), F32), pltpu.VMEM((3, rows, cols), BF), sems(4)],
        limit=12,
    )(at, *parts, *after)


def join_step(at, c0, c1, c2, c3, mark, out):
    for j, piece in enumerate((c0, c1, c2, c3)):
        out[:, aligned(lax.rem(at[2] + 4 - j, 4), piece.shape[1])] = piece[...]


def shards(tokens, cotangent, routes, gates, gate_up, down_proj):
    gate_up = pltpu.with_memory_space_constraint(gate_up[0], pltpu.HBM)
    down_proj = pltpu.with_memory_space_constraint(down_proj[0], pltpu.HBM)
    w, x, y = lax.axis_index("w"), lax.axis_index("x"), lax.axis_index("y")
    me = lax.axis_index(("v", "c"))
    at = jnp.stack([w, x, y, me]).astype(jnp.int32)
    toks, width = tokens.shape
    inner = down_proj.shape[0]
    rows, part = 4 * CAP, width // 4
    experts = jnp.bitwise_xor(me, jnp.arange(4, dtype=jnp.int32))
    matches = routes[:, :, None] == experts[None, None, :]
    member = jnp.any(matches, axis=1)
    weight = jnp.sum(jnp.where(matches, gates[:, :, None], F32(0.0)), axis=1)
    position = jnp.cumsum(member.astype(jnp.int32), axis=0) - 1
    select = member[:, :, None] & (
        position[:, :, None] == jnp.arange(CAP, dtype=jnp.int32)[None, None, :]
    )
    mask = select.astype(BF).reshape(toks, rows)
    slot_gate = jnp.sum(jnp.where(select, weight[:, :, None], F32(0.0)), axis=0).reshape(rows, 1)
    send_x = rows_dot(mask, tokens).astype(BF).reshape(4, CAP, width)
    send_g = (rows_dot(mask, cotangent) * slot_gate).astype(BF).reshape(4, CAP, width)
    xs = [send_x[0]] + [swap_expert(send_x[k], k) for k in (1, 2, 3)]
    gs = [send_g[0]] + [swap_expert(send_g[k], k) for k in (1, 2, 3)]

    packed = call(
        pack_x, "svvvv", [shape(rows, part)] * 4 + [shape(rows, width)], moved=4 * rows * width
    )(at, *xs)
    xa = [shift(packed[j], "x", j) for j in range(4)]
    n = 2 * inner // 256
    hidden, slope, silu = call(
        act_step,
        "va",
        [shape(rows, inner), shape(rows, inner, dtype=F32), shape(rows, inner, dtype=F32)],
        [pltpu.VMEM((n, width, 256), BF), sems(n)],
        flops=4 * rows * width * inner,
        moved=4 * width * inner,
        limit=18,
    )(packed[4], gate_up)
    n = inner // 256
    dact, mark = call(
        dh_step,
        "aaaaaaa",
        [shape(2, rows, inner), MARK],
        [
            pltpu.VMEM((rows, width), BF),
            pltpu.VMEM((2, rows, inner), F32),
            pltpu.VMEM((n, 256, width), BF),
            sems(n),
            sems(6),
        ],
        flops=2 * rows * width * inner,
        moved=2 * width * inner,
        limit=14,
    )(*gs, slope, silu, down_proj)
    da = [shift(dact, "x", j) for j in range(4)]
    sent, sent_mark = call(
        pack_g,
        "aaaaaaaaa",
        [shape(4, rows, part + inner), MARK],
        [sems(20)],
        moved=4 * rows * width,
        placed=(0,),
    )(*gs, hidden, *xa[1:], mark)
    both = lax.all_to_all(sent, "y", split_axis=0, concat_axis=0, tiled=True)
    n = width // 512
    *back, back_mark = call(
        back_step,
        "vaa",
        [shape(CAP, width)] * 4 + [MARK],
        [pltpu.VMEM((n, 512, 2 * inner), BF), sems(n)],
        flops=4 * rows * width * inner,
        moved=4 * width * inner,
        limit=18,
    )(dact, gate_up, sent_mark)
    arrived = [back[0]] + [swap_expert(back[k], k) for k in (1, 2, 3)]
    parts, mark = tile_call(xa, da, arrived[2:])
    gate = lax.all_to_all(parts, ("w", "y"), split_axis=0, concat_axis=0, tiled=True)
    *parts, _ = call(
        down_step,
        "saa",
        [shape(192, part, dtype=F32)] + [shape(192, part)] * 3 + [MARK],
        [
            pltpu.VMEM((4 * rows, part), BF),
            pltpu.VMEM((4 * rows, inner), BF),
            pltpu.VMEM((inner, part), F32),
            sems(8),
        ],
        flops=8 * rows * part * inner,
        moved=8 * rows * (part + inner),
        limit=16,
    )(at, both, mark)
    down = [parts[0]] + [shift(parts[j], "x", j) for j in (1, 2, 3)]
    token_grad, tok_mark = call(
        tok_step,
        "vaaaa",
        [shape(toks, width), MARK],
        [pltpu.VMEM((rows, width), BF), sems(4)],
    )(mask, *arrived)

    gate_up_grad, mark = call(
        gate_sum,
        "a",
        [shape(128, 2 * inner), MARK],
        [pltpu.VMEM((8, 128, 2 * inner), BF), sems(8)],
        limit=12,
    )(gate)
    keep, send = sum_call(at, down, [tok_mark])
    down_grad = (keep + swap_w(send).astype(F32)).astype(BF).reshape(4, 24, part)
    cols = [
        shift(lax.dynamic_index_in_dim(down_grad, (y + j) % 4, 0, False), "y", j) for j in range(4)
    ]
    down_grad = call(join_step, "svvvva", [shape(24, width)])(at, *cols, mark)[0]

    return token_grad, gate_up_grad[None], down_grad[None]


def solution(mesh):
    fine = Mesh(mesh.devices.reshape(2, 4, 4, 2, 2), AXES)
    rows, expert, dp = P(AXES, None), ("v", "c"), ("w", "x", "y")
    in_specs = (rows, rows, rows, rows, P(expert, None, None), P(expert, None, None))
    out_specs = (rows, P(expert, dp, None), P(expert, dp, None))
    return jax.shard_map(
        shards, mesh=fine, in_specs=in_specs, out_specs=out_specs, check_vma=False
    )
```

```python
import jax
import jax.numpy as jnp
from jax import lax
from jax.experimental import pallas as pl
from jax.experimental.pallas import tpu as pltpu
from jax.sharding import Mesh, PartitionSpec as P

CAP = 48
BF = jnp.bfloat16
F32 = jnp.float32
MB = 1024 * 1024
AXES = ("w", "x", "y", "v", "c")
VMEM = pl.BlockSpec(memory_space=pltpu.VMEM)
SMEM = pl.BlockSpec(memory_space=pltpu.SMEM)
ANY = pl.BlockSpec(memory_space=pl.ANY)
HBM = pl.BlockSpec(memory_space=pltpu.HBM)
MARK = jax.ShapeDtypeStruct((8, 128), F32)


def swap_expert(a, k):
    return lax.ppermute(a, ("v", "c"), [(i, i ^ k) for i in range(4)])


def shift(a, axis, j):
    if j == 0:
        return a
    return lax.ppermute(a, axis, [(i, (i + j) % 4) for i in range(4)])


def swap_w(a):
    return lax.ppermute(a, "w", [(0, 1), (1, 0)])


def rows_dot(a, b):
    return lax.dot_general(a, b, (((0,), (0,)), ((), ())), preferred_element_type=F32)


def wide_dot(a, b):
    return lax.dot_general(a, b, (((1,), (1,)), ((), ())), preferred_element_type=F32)


def shape(*dims, dtype=BF):
    return jax.ShapeDtypeStruct(dims, dtype)


def aligned(i, size):
    return pl.ds(pl.multiple_of(i * size, size), size)


def call(body, ins, outs, scratch=(), flops=0, moved=0, limit=8, placed=()):
    specs = {"s": SMEM, "v": VMEM, "a": ANY}
    return pl.pallas_call(
        body,
        out_shape=[pltpu.HBM(o.shape, o.dtype) if i in placed else o for i, o in enumerate(outs)],
        in_specs=[specs[i] for i in ins],
        out_specs=[HBM if o in placed else VMEM for o in range(len(outs))],
        scratch_shapes=list(scratch),
        compiler_params=pltpu.CompilerParams(vmem_limit_bytes=limit * MB),
        cost_estimate=pl.CostEstimate(flops=flops, bytes_accessed=moved, transcendentals=0),
    )


def fetch(pairs, sems):
    copies = [pltpu.make_async_copy(s, d, sems.at[i]) for i, (s, d) in enumerate(pairs)]
    for copy in copies:
        copy.start()
    return copies


def land(pairs, sems):
    for copy in fetch(pairs, sems):
        copy.wait()


def sems(n):
    return pltpu.SemaphoreType.DMA((n,))


def pack_x(at, x0, x1, x2, x3, *outs):
    whole = outs[4]
    for k, piece in enumerate((x0, x1, x2, x3)):
        rows = slice(k * CAP, k * CAP + CAP)
        whole[rows, :] = piece[...]
        for j in range(4):
            for b in range(2):
                cols = aligned(b * 4 + lax.rem(at[1] + j, 4), 512)
                outs[j][rows, b * 512 : b * 512 + 512] = piece[:, cols]


def pack_g(g0, g1, g2, g3, hidden, *rest):
    out, mark, sem = rest[-3:]
    part, inner = g0.shape[1] // 4, hidden.shape[1]
    mark[...] = jnp.zeros_like(mark)
    pairs = []
    for i in range(4):
        for k, piece in enumerate((g0, g1, g2, g3)):
            to = out.at[i, pl.ds(k * CAP, CAP), pl.ds(0, part)]
            pairs.append((piece.at[:, pl.ds(i * part, part)], to))
        pairs.append((hidden, out.at[i, :, pl.ds(part, inner)]))
    land(pairs, sem)


def act_step(x, weights, hidden, slope, silu, buf, sem):
    inner, step = hidden.shape[1], buf.shape[2]
    n = inner // step
    cuts = [(i, h) for i in range(n) for h in range(2)]
    copies = fetch(
        [
            (weights.at[:, pl.ds(h * inner + i * step, step)], buf.at[2 * i + h])
            for i, h in cuts
        ],
        sem,
    )
    for i in range(n):
        cols = slice(i * step, i * step + step)
        copies[2 * i].wait()
        gpart = jnp.dot(x[...], buf[2 * i], preferred_element_type=F32)
        copies[2 * i + 1].wait()
        upart = jnp.dot(x[...], buf[2 * i + 1], preferred_element_type=F32)
        sig = jax.nn.sigmoid(gpart)
        soft = gpart * sig
        hidden[:, cols] = (soft * upart).astype(BF)
        slope[:, cols] = upart * (sig * (1.0 + gpart * (1.0 - sig)))
        silu[:, cols] = soft


def dh_step(g0, g1, g2, g3, slope, silu, weights, *rest):
    dact, mark, whole, factors, buf, sem, gsem = rest[-7:]
    mark[...] = jnp.zeros_like(mark)
    n, step = buf.shape[:2]
    copies = fetch([(weights.at[pl.ds(i * step, step), :], buf.at[i]) for i in range(n)], sem)
    pieces = [(g, whole.at[pl.ds(k * CAP, CAP), :]) for k, g in enumerate((g0, g1, g2, g3))]
    land(pieces + [(slope, factors.at[0]), (silu, factors.at[1])], gsem)
    for i in range(n):
        cols = slice(i * step, i * step + step)
        copies[i].wait()
        dh = wide_dot(whole[...], buf[i])
        dact[0, :, cols] = (dh * factors[0, :, cols]).astype(BF)
        dact[1, :, cols] = (dh * factors[1, :, cols]).astype(BF)


def back_step(dact, weights, *rest):
    outs, mark, buf, sem = rest[-7:-3], *rest[-3:]
    n, step, inner = buf.shape[0], buf.shape[1], dact.shape[2]
    copies = fetch([(weights.at[pl.ds(i * step, step), :], buf.at[i]) for i in range(n)], sem)
    mark[...] = jnp.zeros_like(mark)
    for i in range(n):
        copies[i].wait()
        got = wide_dot(dact[0], buf[i, :, :inner]) + wide_dot(dact[1], buf[i, :, inner:])
        for k in range(4):
            outs[k][:, i * step : i * step + step] = got[k * CAP : k * CAP + CAP].astype(BF)


def tok_step(mask, a0, a1, a2, a3, out, mark, whole, sem):
    mark[...] = jnp.zeros_like(mark)
    pieces = (a0, a1, a2, a3)
    land([(a, whole.at[pl.ds(k * CAP, CAP), :]) for k, a in enumerate(pieces)], sem)
    out[...] = jnp.dot(mask[...], whole[...], preferred_element_type=F32).astype(BF)


def tile_step(at, *refs):
    xs, ds = refs[:4], refs[4:8]
    out, keep, send, mark, xall, dall, buf, sem, osem = refs[-9:]
    rows, inner = xs[0].shape[0], ds[0].shape[2]
    cut = buf.shape[2]
    part = [pl.ds(p * rows, rows) for p in range(4)]
    land(
        [(xs[p], xall.at[part[p], :]) for p in range(4)]
        + [
            (ds[p].at[h], dall.at[part[p], pl.ds(h * inner, inner)])
            for p in range(4)
            for h in range(2)
        ],
        sem,
    )
    mark[...] = jnp.zeros_like(mark)
    copies = []
    for b in range(2):
        got = rows_dot(xall[:, b * 512 : b * 512 + 512], dall[:, :cut])
        for j in range(4):
            buf[j, b * 128 : b * 128 + 128, :] = got[j * 128 : j * 128 + 128].astype(BF)
            if b == 1:
                copies.append(pltpu.make_async_copy(buf.at[j], out.at[j], osem.at[j]))
                copies[-1].start()
    send[...] = rows_dot(xall[:, aligned(1 - at[0], 512)], dall[:, cut:]).astype(BF)
    keep[...] = rows_dot(xall[:, aligned(at[0], 512)], dall[:, cut:])
    for copy in copies:
        copy.wait()


def tile_call(at, xs, ds, cut, after):
    rows, part = xs[0].shape
    wide = 2 * ds[0].shape[2]
    return call(
        tile_step,
        "s" + "a" * (8 + len(after)),
        [shape(4, 256, cut), shape(512, wide - cut, dtype=F32), shape(512, wide - cut), MARK],
        [
            pltpu.VMEM((4 * rows, part), BF),
            pltpu.VMEM((4 * rows, wide), BF),
            pltpu.VMEM((4, 256, cut), BF),
            sems(12),
            sems(4),
        ],
        flops=8 * rows * part * wide,
        moved=8 * rows * (part + wide),
        limit=24,
        placed=(0,),
    )(at, *xs, *ds, *after)


def middle_step(at, keep, theirs, own, *sends):
    for j in range(4):
        rows = aligned(lax.rem(at[2] + j, 4), 128)
        got = keep[rows, :] + theirs[rows, :].astype(F32)
        if j:
            sends[j - 1][...] = got.astype(BF)
        else:
            own[...] = got


def ring_sum(own, r1, r2, r3, after, out, mark):
    mark[...] = jnp.zeros_like(mark)
    out[...] = (own[...] + sum(r[...].astype(F32) for r in (r1, r2, r3))).astype(BF)


def down_step(at, both, *rest):
    outs, mark, gall, hall, total, sem = rest[-9:-5], *rest[-5:]
    rows, part, inner = both.shape[1], gall.shape[1], hall.shape[1]
    pairs = []
    for i in range(4):
        pairs.append((both.at[i, :, pl.ds(0, part)], gall.at[pl.ds(i * rows, rows), :]))
        pairs.append((both.at[i, :, pl.ds(part, inner)], hall.at[pl.ds(i * rows, rows), :]))
    land(pairs, sem)
    mark[...] = jnp.zeros_like(mark)
    for b in range(2):
        cols = slice(b * inner // 2, (b + 1) * inner // 2)
        total[cols, :] = rows_dot(hall[:, cols], gall[...])
    for j in (1, 2, 3, 0):
        other = lax.rem(at[1] + j, 4)
        for b in range(2):
            outs[j][b * 96 : b * 96 + 96, :] = total[aligned(b * 4 + other, 96), :].astype(
                outs[j].dtype
            )


def gate_sum(at, parts, keep, send, mark, g, sem):
    mark[...] = jnp.zeros_like(mark)
    half = keep.shape[0]
    copies = fetch([(parts.at[i], g.at[i]) for i in range(4)], sem)
    for copy in copies:
        copy.wait()

    def part(i):
        return sum(g[p, aligned(i, half), :].astype(F32) for p in range(4))

    send[...] = part(1 - at[0]).astype(BF)
    keep[...] = part(at[0])


def sum_step(at, own, r1, r2, r3, *rest):
    keep, send, f, g, sem = rest[-5:]
    half = keep.shape[0]
    land([(own, f), (r1, g.at[0]), (r2, g.at[1]), (r3, g.at[2])], sem)

    def part(i):
        rows = aligned(i, half)
        return f[rows, :] + sum(g[p, rows, :].astype(F32) for p in range(3))

    send[...] = part(1 - at[0]).astype(BF)
    keep[...] = part(at[0])


def sum_call(at, parts, after):
    rows, cols = parts[0].shape
    return call(
        sum_step,
        "saaaa" + "a" * len(after),
        [shape(rows // 2, cols, dtype=F32), shape(rows // 2, cols)],
        [pltpu.VMEM((rows, cols), F32), pltpu.VMEM((3, rows, cols), BF), sems(4)],
        limit=12,
    )(at, *parts, *after)


def join_step(at, c0, c1, c2, c3, mark, out):
    for j, piece in enumerate((c0, c1, c2, c3)):
        out[:, aligned(lax.rem(at[2] + 4 - j, 4), piece.shape[1])] = piece[...]


def shards(tokens, cotangent, routes, gates, gate_up, down_proj):
    gate_up = pltpu.with_memory_space_constraint(gate_up[0], pltpu.HBM)
    down_proj = pltpu.with_memory_space_constraint(down_proj[0], pltpu.HBM)
    w, x, y = lax.axis_index("w"), lax.axis_index("x"), lax.axis_index("y")
    me = lax.axis_index(("v", "c"))
    at = jnp.stack([w, x, y, me]).astype(jnp.int32)
    toks, width = tokens.shape
    inner = down_proj.shape[0]
    rows, part = 4 * CAP, width // 4
    experts = jnp.bitwise_xor(me, jnp.arange(4, dtype=jnp.int32))
    matches = routes[:, :, None] == experts[None, None, :]
    member = jnp.any(matches, axis=1)
    weight = jnp.sum(jnp.where(matches, gates[:, :, None], F32(0.0)), axis=1)
    position = jnp.cumsum(member.astype(jnp.int32), axis=0) - 1
    select = member[:, :, None] & (
        position[:, :, None] == jnp.arange(CAP, dtype=jnp.int32)[None, None, :]
    )
    mask = select.astype(BF).reshape(toks, rows)
    slot_gate = jnp.sum(jnp.where(select, weight[:, :, None], F32(0.0)), axis=0).reshape(rows, 1)
    send_x = rows_dot(mask, tokens).astype(BF).reshape(4, CAP, width)
    send_g = (rows_dot(mask, cotangent) * slot_gate).astype(BF).reshape(4, CAP, width)
    xs = [send_x[0]] + [swap_expert(send_x[k], k) for k in (1, 2, 3)]
    gs = [send_g[0]] + [swap_expert(send_g[k], k) for k in (1, 2, 3)]

    packed = call(
        pack_x, "svvvv", [shape(rows, part)] * 4 + [shape(rows, width)], moved=4 * rows * width
    )(at, *xs)
    xa = [shift(packed[j], "x", j) for j in range(4)]
    n = 2 * inner // 256
    hidden, slope, silu = call(
        act_step,
        "va",
        [shape(rows, inner), shape(rows, inner, dtype=F32), shape(rows, inner, dtype=F32)],
        [pltpu.VMEM((n, width, 256), BF), sems(n)],
        flops=4 * rows * width * inner,
        moved=4 * width * inner,
        limit=18,
    )(packed[4], gate_up)
    n = inner // 256
    dact, mark = call(
        dh_step,
        "aaaaaaa",
        [shape(2, rows, inner), MARK],
        [
            pltpu.VMEM((rows, width), BF),
            pltpu.VMEM((2, rows, inner), F32),
            pltpu.VMEM((n, 256, width), BF),
            sems(n),
            sems(6),
        ],
        flops=2 * rows * width * inner,
        moved=2 * width * inner,
        limit=14,
    )(*gs, slope, silu, down_proj)
    da = [shift(dact, "x", j) for j in range(4)]
    sent, sent_mark = call(
        pack_g,
        "aaaaaaaaa",
        [shape(4, rows, part + inner), MARK],
        [sems(20)],
        moved=4 * rows * width,
        placed=(0,),
    )(*gs, hidden, *xa[1:], mark)
    both = lax.all_to_all(sent, "y", split_axis=0, concat_axis=0, tiled=True)
    n = width // 512
    *back, back_mark = call(
        back_step,
        "vaa",
        [shape(CAP, width)] * 4 + [MARK],
        [pltpu.VMEM((n, 512, 2 * inner), BF), sems(n)],
        flops=4 * rows * width * inner,
        moved=4 * width * inner,
        limit=18,
    )(dact, gate_up, sent_mark)
    arrived = [back[0]] + [swap_expert(back[k], k) for k in (1, 2, 3)]
    cut = 896
    parts, side_keep, side_send, mark = tile_call(at, xa, da, cut, arrived[2:])
    gate = lax.all_to_all(parts, "y", split_axis=0, concat_axis=0, tiled=True)
    *parts, _ = call(
        down_step,
        "saa",
        [shape(192, part, dtype=F32)] + [shape(192, part)] * 3 + [MARK],
        [
            pltpu.VMEM((4 * rows, part), BF),
            pltpu.VMEM((4 * rows, inner), BF),
            pltpu.VMEM((inner, part), F32),
            sems(8),
        ],
        flops=8 * rows * part * inner,
        moved=8 * rows * (part + inner),
        limit=16,
    )(at, both, mark)
    down = [parts[0]] + [shift(parts[j], "x", j) for j in (1, 2, 3)]
    token_grad, tok_mark = call(
        tok_step,
        "vaaaa",
        [shape(toks, width), MARK],
        [pltpu.VMEM((rows, width), BF), sems(4)],
    )(mask, *arrived)

    rest = 2 * inner - cut
    side = call(
        middle_step, "svv", [shape(128, rest, dtype=F32)] + [shape(128, rest)] * 3
    )(at, side_keep, swap_w(side_send))
    side = [side[0]] + [shift(side[j], "y", j) for j in (1, 2, 3)]
    gate_keep, gate_send, _ = call(
        gate_sum,
        "sa",
        [shape(128, cut, dtype=F32), shape(128, cut), MARK],
        [pltpu.VMEM((4, 256, cut), BF), sems(4)],
        limit=12,
    )(at, gate)
    keep, send = sum_call(at, down, [tok_mark])
    side_grad, mark = call(ring_sum, "vvvva", [shape(128, rest), MARK])(*side, send)
    gate_up_grad = (gate_keep + swap_w(gate_send).astype(F32)).astype(BF)
    gate_up_grad = jnp.concatenate([gate_up_grad, side_grad], axis=1)
    down_grad = (keep + swap_w(send).astype(F32)).astype(BF).reshape(4, 24, part)
    cols = [
        shift(lax.dynamic_index_in_dim(down_grad, (y + j) % 4, 0, False), "y", j) for j in range(4)
    ]
    down_grad = call(join_step, "svvvva", [shape(24, width)])(at, *cols, mark)[0]

    return token_grad, gate_up_grad[None], down_grad[None]


def solution(mesh):
    fine = Mesh(mesh.devices.reshape(2, 4, 4, 2, 2), AXES)
    rows, expert, dp = P(AXES, None), ("v", "c"), ("w", "x", "y")
    in_specs = (rows, rows, rows, rows, P(expert, None, None), P(expert, None, None))
    out_specs = (rows, P(expert, dp, None), P(expert, dp, None))
    return jax.shard_map(
        shards, mesh=fine, in_specs=in_specs, out_specs=out_specs, check_vma=False
    )
```

```python
import jax
import jax.numpy as jnp
from jax import lax
from jax.experimental import pallas as pl
from jax.experimental.pallas import tpu as pltpu
from jax.sharding import Mesh, PartitionSpec as P

CAP = 48
BF = jnp.bfloat16
F32 = jnp.float32
MB = 1024 * 1024
AXES = ("w", "x", "y", "v", "c")
VMEM = pl.BlockSpec(memory_space=pltpu.VMEM)
SMEM = pl.BlockSpec(memory_space=pltpu.SMEM)
ANY = pl.BlockSpec(memory_space=pl.ANY)
HBM = pl.BlockSpec(memory_space=pltpu.HBM)
MARK = jax.ShapeDtypeStruct((8, 128), F32)


def swap_expert(a, k):
    return lax.ppermute(a, ("v", "c"), [(i, i ^ k) for i in range(4)])


def shift(a, axis, j):
    if j == 0:
        return a
    return lax.ppermute(a, axis, [(i, (i + j) % 4) for i in range(4)])


def swap_w(a):
    return lax.ppermute(a, "w", [(0, 1), (1, 0)])


def rows_dot(a, b):
    return lax.dot_general(a, b, (((0,), (0,)), ((), ())), preferred_element_type=F32)


def wide_dot(a, b):
    return lax.dot_general(a, b, (((1,), (1,)), ((), ())), preferred_element_type=F32)


def shape(*dims, dtype=BF):
    return jax.ShapeDtypeStruct(dims, dtype)


def aligned(i, size):
    return pl.ds(pl.multiple_of(i * size, size), size)


def call(body, ins, outs, scratch=(), flops=0, moved=0, limit=8, placed=()):
    specs = {"s": SMEM, "v": VMEM, "a": ANY}
    return pl.pallas_call(
        body,
        out_shape=[pltpu.HBM(o.shape, o.dtype) if i in placed else o for i, o in enumerate(outs)],
        in_specs=[specs[i] for i in ins],
        out_specs=[HBM if o in placed else VMEM for o in range(len(outs))],
        scratch_shapes=list(scratch),
        compiler_params=pltpu.CompilerParams(vmem_limit_bytes=limit * MB),
        cost_estimate=pl.CostEstimate(flops=flops, bytes_accessed=moved, transcendentals=0),
    )


def fetch(pairs, sems):
    copies = [pltpu.make_async_copy(s, d, sems.at[i]) for i, (s, d) in enumerate(pairs)]
    for copy in copies:
        copy.start()
    return copies


def land(pairs, sems):
    for copy in fetch(pairs, sems):
        copy.wait()


def sems(n):
    return pltpu.SemaphoreType.DMA((n,))


def pack_x(at, x0, x1, x2, x3, *outs):
    whole = outs[4]
    for k, piece in enumerate((x0, x1, x2, x3)):
        rows = slice(k * CAP, k * CAP + CAP)
        whole[rows, :] = piece[...]
        for j in range(4):
            for b in range(2):
                cols = aligned(b * 4 + lax.rem(at[1] + j, 4), 512)
                outs[j][rows, b * 512 : b * 512 + 512] = piece[:, cols]


def pack_g(g0, g1, g2, g3, hidden, *rest):
    out, mark, sem = rest[-3:]
    part, inner = g0.shape[1] // 4, hidden.shape[1]
    mark[...] = jnp.zeros_like(mark)
    pairs = []
    for i in range(4):
        for k, piece in enumerate((g0, g1, g2, g3)):
            to = out.at[i, pl.ds(k * CAP, CAP), pl.ds(0, part)]
            pairs.append((piece.at[:, pl.ds(i * part, part)], to))
        pairs.append((hidden, out.at[i, :, pl.ds(part, inner)]))
    land(pairs, sem)


def act_step(x, weights, hidden, slope, silu, buf, sem):
    inner, step = hidden.shape[1], buf.shape[2]
    n = inner // step
    cuts = [(i, h) for i in range(n) for h in range(2)]
    copies = fetch(
        [
            (weights.at[:, pl.ds(h * inner + i * step, step)], buf.at[2 * i + h])
            for i, h in cuts
        ],
        sem,
    )
    for i in range(n):
        cols = slice(i * step, i * step + step)
        copies[2 * i].wait()
        gpart = jnp.dot(x[...], buf[2 * i], preferred_element_type=F32)
        copies[2 * i + 1].wait()
        upart = jnp.dot(x[...], buf[2 * i + 1], preferred_element_type=F32)
        sig = jax.nn.sigmoid(gpart)
        soft = gpart * sig
        hidden[:, cols] = (soft * upart).astype(BF)
        slope[:, cols] = upart * (sig * (1.0 + gpart * (1.0 - sig)))
        silu[:, cols] = soft


def dh_step(g0, g1, g2, g3, slope, silu, weights, *rest):
    dact, mark, whole, factors, buf, sem, gsem = rest[-7:]
    mark[...] = jnp.zeros_like(mark)
    n, step = buf.shape[:2]
    copies = fetch([(weights.at[pl.ds(i * step, step), :], buf.at[i]) for i in range(n)], sem)
    pieces = [(g, whole.at[pl.ds(k * CAP, CAP), :]) for k, g in enumerate((g0, g1, g2, g3))]
    land(pieces + [(slope, factors.at[0]), (silu, factors.at[1])], gsem)
    for i in range(n):
        cols = slice(i * step, i * step + step)
        copies[i].wait()
        dh = wide_dot(whole[...], buf[i])
        dact[0, :, cols] = (dh * factors[0, :, cols]).astype(BF)
        dact[1, :, cols] = (dh * factors[1, :, cols]).astype(BF)


def back_step(dact, weights, *rest):
    outs, mark, buf, sem = rest[-7:-3], *rest[-3:]
    n, step, inner = buf.shape[0], buf.shape[1], dact.shape[2]
    copies = fetch([(weights.at[pl.ds(i * step, step), :], buf.at[i]) for i in range(n)], sem)
    mark[...] = jnp.zeros_like(mark)
    for i in range(n):
        copies[i].wait()
        got = wide_dot(dact[0], buf[i, :, :inner]) + wide_dot(dact[1], buf[i, :, inner:])
        for k in range(4):
            outs[k][:, i * step : i * step + step] = got[k * CAP : k * CAP + CAP].astype(BF)


def tok_step(mask, a0, a1, a2, a3, out, mark, whole, sem):
    mark[...] = jnp.zeros_like(mark)
    pieces = (a0, a1, a2, a3)
    land([(a, whole.at[pl.ds(k * CAP, CAP), :]) for k, a in enumerate(pieces)], sem)
    out[...] = jnp.dot(mask[...], whole[...], preferred_element_type=F32).astype(BF)


def tile_step(at, *refs):
    xs, ds = refs[:4], refs[4:8]
    own, next0, next1, prev0, prev1, far0, far1, mark, xall, dall, sem = refs[-11:]
    rows, inner = xs[0].shape[0], ds[0].shape[2]
    part = [pl.ds(p * rows, rows) for p in range(4)]
    land(
        [(xs[p], xall.at[part[p], :]) for p in range(4)]
        + [
            (ds[p].at[h], dall.at[part[p], pl.ds(h * inner, inner)])
            for p in range(4)
            for h in range(2)
        ],
        sem,
    )
    mark[...] = jnp.zeros_like(mark)
    for j, out in ((2, (far0, far1)), (1, (next0, next1)), (3, (prev0, prev1)), (0, None)):
        other = lax.rem(at[2] + j, 4)
        for b in range(2):
            got = rows_dot(xall[:, aligned(b * 4 + other, 128)], dall[...])
            if out is None:
                own[b * 128 : b * 128 + 128, :] = got
            else:
                out[b][...] = got.astype(out[b].dtype)


def tile_call(at, xs, ds, after):
    rows, part = xs[0].shape
    wide = 2 * ds[0].shape[2]
    half, full = shape(128, wide), shape(128, wide, dtype=F32)
    return call(
        tile_step,
        "s" + "a" * (8 + len(after)),
        [shape(256, wide, dtype=F32), full, half, half, full, half, half, MARK],
        [pltpu.VMEM((4 * rows, part), BF), pltpu.VMEM((4 * rows, wide), BF), sems(12)],
        flops=8 * rows * part * wide,
        moved=8 * rows * (part + wide),
        limit=16,
    )(at, *xs, *ds, *after)


def middle_step(next0, next1, prev0, prev1, from_prev, from_next, after, to_next, to_prev):
    to_next[:128, :] = (next0[...] + from_prev[...].astype(F32)).astype(BF)
    to_next[128:, :] = next1[...]
    to_prev[:128, :] = prev0[...]
    to_prev[128:, :] = (prev1[...] + from_next[...].astype(F32)).astype(BF)


def down_step(at, both, *rest):
    outs, mark, gall, hall, total, sem = rest[-9:-5], *rest[-5:]
    rows, part, inner = both.shape[1], gall.shape[1], hall.shape[1]
    pairs = []
    for i in range(4):
        pairs.append((both.at[i, :, pl.ds(0, part)], gall.at[pl.ds(i * rows, rows), :]))
        pairs.append((both.at[i, :, pl.ds(part, inner)], hall.at[pl.ds(i * rows, rows), :]))
    land(pairs, sem)
    mark[...] = jnp.zeros_like(mark)
    for b in range(2):
        cols = slice(b * inner // 2, (b + 1) * inner // 2)
        total[cols, :] = rows_dot(hall[:, cols], gall[...])
    for j in (1, 2, 3, 0):
        other = lax.rem(at[1] + j, 4)
        for b in range(2):
            outs[j][b * 96 : b * 96 + 96, :] = total[aligned(b * 4 + other, 96), :].astype(
                outs[j].dtype
            )


def gate_sum(at, own, r1, r2, keep, send, mark):
    half = keep.shape[0]
    mark[...] = jnp.zeros_like(mark)

    def part(i):
        rows = aligned(i, half)
        return own[rows, :] + r1[rows, :].astype(F32) + r2[rows, :].astype(F32)

    send[...] = part(1 - at[0]).astype(BF)
    keep[...] = part(at[0])


def sum_step(at, own, r1, r2, r3, *rest):
    keep, send, f, g, sem = rest[-5:]
    half = keep.shape[0]
    land([(own, f), (r1, g.at[0]), (r2, g.at[1]), (r3, g.at[2])], sem)

    def part(i):
        rows = aligned(i, half)
        return f[rows, :] + sum(g[p, rows, :].astype(F32) for p in range(3))

    send[...] = part(1 - at[0]).astype(BF)
    keep[...] = part(at[0])


def sum_call(at, parts, after):
    rows, cols = parts[0].shape
    return call(
        sum_step,
        "saaaa" + "a" * len(after),
        [shape(rows // 2, cols, dtype=F32), shape(rows // 2, cols)],
        [pltpu.VMEM((rows, cols), F32), pltpu.VMEM((3, rows, cols), BF), sems(4)],
        limit=12,
    )(at, *parts, *after)


def join_step(at, c0, c1, c2, c3, mark, out):
    for j, piece in enumerate((c0, c1, c2, c3)):
        out[:, aligned(lax.rem(at[2] + 4 - j, 4), piece.shape[1])] = piece[...]


def shards(tokens, cotangent, routes, gates, gate_up, down_proj):
    gate_up = pltpu.with_memory_space_constraint(gate_up[0], pltpu.HBM)
    down_proj = pltpu.with_memory_space_constraint(down_proj[0], pltpu.HBM)
    w, x, y = lax.axis_index("w"), lax.axis_index("x"), lax.axis_index("y")
    me = lax.axis_index(("v", "c"))
    at = jnp.stack([w, x, y, me]).astype(jnp.int32)
    toks, width = tokens.shape
    inner = down_proj.shape[0]
    rows, part = 4 * CAP, width // 4
    experts = jnp.bitwise_xor(me, jnp.arange(4, dtype=jnp.int32))
    matches = routes[:, :, None] == experts[None, None, :]
    member = jnp.any(matches, axis=1)
    weight = jnp.sum(jnp.where(matches, gates[:, :, None], F32(0.0)), axis=1)
    position = jnp.cumsum(member.astype(jnp.int32), axis=0) - 1
    select = member[:, :, None] & (
        position[:, :, None] == jnp.arange(CAP, dtype=jnp.int32)[None, None, :]
    )
    mask = select.astype(BF).reshape(toks, rows)
    slot_gate = jnp.sum(jnp.where(select, weight[:, :, None], F32(0.0)), axis=0).reshape(rows, 1)
    send_x = rows_dot(mask, tokens).astype(BF).reshape(4, CAP, width)
    send_g = (rows_dot(mask, cotangent) * slot_gate).astype(BF).reshape(4, CAP, width)
    xs = [send_x[0]] + [swap_expert(send_x[k], k) for k in (1, 2, 3)]
    gs = [send_g[0]] + [swap_expert(send_g[k], k) for k in (1, 2, 3)]

    packed = call(
        pack_x, "svvvv", [shape(rows, part)] * 4 + [shape(rows, width)], moved=4 * rows * width
    )(at, *xs)
    xa = [shift(packed[j], "x", j) for j in range(4)]
    n = 2 * inner // 256
    hidden, slope, silu = call(
        act_step,
        "va",
        [shape(rows, inner), shape(rows, inner, dtype=F32), shape(rows, inner, dtype=F32)],
        [pltpu.VMEM((n, width, 256), BF), sems(n)],
        flops=4 * rows * width * inner,
        moved=4 * width * inner,
        limit=18,
    )(packed[4], gate_up)
    n = inner // 256
    dact, mark = call(
        dh_step,
        "aaaaaaa",
        [shape(2, rows, inner), MARK],
        [
            pltpu.VMEM((rows, width), BF),
            pltpu.VMEM((2, rows, inner), F32),
            pltpu.VMEM((n, 256, width), BF),
            sems(n),
            sems(6),
        ],
        flops=2 * rows * width * inner,
        moved=2 * width * inner,
        limit=14,
    )(*gs, slope, silu, down_proj)
    da = [shift(dact, "x", j) for j in range(4)]
    sent, sent_mark = call(
        pack_g,
        "aaaaaaaaa",
        [shape(4, rows, part + inner), MARK],
        [sems(20)],
        moved=4 * rows * width,
        placed=(0,),
    )(*gs, hidden, *xa[1:], mark)
    both = lax.all_to_all(sent, "y", split_axis=0, concat_axis=0, tiled=True)
    n = width // 512
    *back, back_mark = call(
        back_step,
        "vaa",
        [shape(CAP, width)] * 4 + [MARK],
        [pltpu.VMEM((n, 512, 2 * inner), BF), sems(n)],
        flops=4 * rows * width * inner,
        moved=4 * width * inner,
        limit=18,
    )(dact, gate_up, sent_mark)
    arrived = [back[0]] + [swap_expert(back[k], k) for k in (1, 2, 3)]
    own, next0, next1, prev0, prev1, far0, far1, mark = tile_call(at, xa, da, [arrived[2]])
    *parts, mark = call(
        down_step,
        "saa",
        [shape(192, part, dtype=F32)] + [shape(192, part)] * 3 + [MARK],
        [
            pltpu.VMEM((4 * rows, part), BF),
            pltpu.VMEM((4 * rows, inner), BF),
            pltpu.VMEM((inner, part), F32),
            sems(8),
        ],
        flops=8 * rows * part * inner,
        moved=8 * rows * (part + inner),
        limit=16,
    )(at, both, mark)
    to_next, to_prev = call(middle_step, "vvvvvva", [shape(256, 2 * inner)] * 2)(
        next0, next1, prev0, prev1, shift(far0, "y", 1), shift(far1, "y", 3), mark
    )
    gate = [own, shift(to_next, "y", 1), shift(to_prev, "y", 3)]
    down = [parts[0]] + [shift(parts[j], "x", j) for j in (1, 2, 3)]
    token_grad, tok_mark = call(
        tok_step,
        "vaaaa",
        [shape(toks, width), MARK],
        [pltpu.VMEM((rows, width), BF), sems(4)],
    )(mask, *arrived)

    gate_keep, gate_send, mark = call(
        gate_sum,
        "svvv",
        [shape(128, 2 * inner, dtype=F32), shape(128, 2 * inner), MARK],
    )(at, *gate)
    gate_up_grad = (gate_keep + swap_w(gate_send).astype(F32)).astype(BF)
    keep, send = sum_call(at, down, [tok_mark])
    down_grad = (keep + swap_w(send).astype(F32)).astype(BF).reshape(4, 24, part)
    cols = [
        shift(lax.dynamic_index_in_dim(down_grad, (y + j) % 4, 0, False), "y", j) for j in range(4)
    ]
    down_grad = call(join_step, "svvvva", [shape(24, width)])(at, *cols, mark)[0]

    return token_grad, gate_up_grad[None], down_grad[None]


def solution(mesh):
    fine = Mesh(mesh.devices.reshape(2, 4, 4, 2, 2), AXES)
    rows, expert, dp = P(AXES, None), ("v", "c"), ("w", "x", "y")
    in_specs = (rows, rows, rows, rows, P(expert, None, None), P(expert, None, None))
    out_specs = (rows, P(expert, dp, None), P(expert, dp, None))
    return jax.shard_map(
        shards, mesh=fine, in_specs=in_specs, out_specs=out_specs, check_vma=False
    )
```

```python
import jax
import jax.numpy as jnp
from jax import lax
from jax.experimental import pallas as pl
from jax.experimental.pallas import tpu as pltpu
from jax.sharding import Mesh, PartitionSpec as P

CAP = 48
BF = jnp.bfloat16
F32 = jnp.float32
MB = 1024 * 1024
AXES = ("w", "x", "y", "v", "c")
VMEM = pl.BlockSpec(memory_space=pltpu.VMEM)
SMEM = pl.BlockSpec(memory_space=pltpu.SMEM)
ANY = pl.BlockSpec(memory_space=pl.ANY)
HBM = pl.BlockSpec(memory_space=pltpu.HBM)
MARK = jax.ShapeDtypeStruct((8, 128), F32)


def swap_expert(a, k):
    return lax.ppermute(a, ("v", "c"), [(i, i ^ k) for i in range(4)])


def shift(a, axis, j):
    if j == 0:
        return a
    return lax.ppermute(a, axis, [(i, (i + j) % 4) for i in range(4)])


def swap_w(a):
    return lax.ppermute(a, "w", [(0, 1), (1, 0)])


def rows_dot(a, b):
    return lax.dot_general(a, b, (((0,), (0,)), ((), ())), preferred_element_type=F32)


def wide_dot(a, b):
    return lax.dot_general(a, b, (((1,), (1,)), ((), ())), preferred_element_type=F32)


def shape(*dims, dtype=BF):
    return jax.ShapeDtypeStruct(dims, dtype)


def aligned(i, size):
    return pl.ds(pl.multiple_of(i * size, size), size)


def call(body, ins, outs, scratch=(), flops=0, moved=0, limit=8, placed=()):
    specs = {"s": SMEM, "v": VMEM, "a": ANY}
    return pl.pallas_call(
        body,
        out_shape=[pltpu.HBM(o.shape, o.dtype) if i in placed else o for i, o in enumerate(outs)],
        in_specs=[specs[i] for i in ins],
        out_specs=[HBM if o in placed else VMEM for o in range(len(outs))],
        scratch_shapes=list(scratch),
        compiler_params=pltpu.CompilerParams(vmem_limit_bytes=limit * MB),
        cost_estimate=pl.CostEstimate(flops=flops, bytes_accessed=moved, transcendentals=0),
    )


def fetch(pairs, sems):
    copies = [pltpu.make_async_copy(s, d, sems.at[i]) for i, (s, d) in enumerate(pairs)]
    for copy in copies:
        copy.start()
    return copies


def land(pairs, sems):
    for copy in fetch(pairs, sems):
        copy.wait()


def sems(n):
    return pltpu.SemaphoreType.DMA((n,))


def pack_x(at, x0, x1, x2, x3, *outs):
    whole = outs[4]
    for k, piece in enumerate((x0, x1, x2, x3)):
        rows = slice(k * CAP, k * CAP + CAP)
        whole[rows, :] = piece[...]
        for j in range(4):
            for b in range(2):
                cols = aligned(b * 4 + lax.rem(at[1] + j, 4), 512)
                outs[j][rows, b * 512 : b * 512 + 512] = piece[:, cols]


def pack_g(g0, g1, g2, g3, hidden, *rest):
    out, mark, sem = rest[-3:]
    part, inner = g0.shape[1] // 4, hidden.shape[1]
    mark[...] = jnp.zeros_like(mark)
    pairs = []
    for i in range(4):
        for k, piece in enumerate((g0, g1, g2, g3)):
            to = out.at[i, pl.ds(k * CAP, CAP), pl.ds(0, part)]
            pairs.append((piece.at[:, pl.ds(i * part, part)], to))
        pairs.append((hidden, out.at[i, :, pl.ds(part, inner)]))
    land(pairs, sem)


def act_step(x, weights, hidden, slope, silu, buf, sem):
    inner, step = hidden.shape[1], buf.shape[2]
    n = inner // step
    cuts = [(i, h) for i in range(n) for h in range(2)]
    copies = fetch(
        [
            (weights.at[:, pl.ds(h * inner + i * step, step)], buf.at[2 * i + h])
            for i, h in cuts
        ],
        sem,
    )
    for i in range(n):
        cols = slice(i * step, i * step + step)
        copies[2 * i].wait()
        gpart = jnp.dot(x[...], buf[2 * i], preferred_element_type=F32)
        copies[2 * i + 1].wait()
        upart = jnp.dot(x[...], buf[2 * i + 1], preferred_element_type=F32)
        sig = jax.nn.sigmoid(gpart)
        soft = gpart * sig
        hidden[:, cols] = (soft * upart).astype(BF)
        slope[:, cols] = upart * (sig * (1.0 + gpart * (1.0 - sig)))
        silu[:, cols] = soft


def dh_step(g0, g1, g2, g3, slope, silu, weights, *rest):
    dact, mark, whole, factors, buf, sem, gsem = rest[-7:]
    mark[...] = jnp.zeros_like(mark)
    n, step = buf.shape[:2]
    copies = fetch([(weights.at[pl.ds(i * step, step), :], buf.at[i]) for i in range(n)], sem)
    pieces = [(g, whole.at[pl.ds(k * CAP, CAP), :]) for k, g in enumerate((g0, g1, g2, g3))]
    land(pieces + [(slope, factors.at[0]), (silu, factors.at[1])], gsem)
    for i in range(n):
        cols = slice(i * step, i * step + step)
        copies[i].wait()
        dh = wide_dot(whole[...], buf[i])
        dact[0, :, cols] = (dh * factors[0, :, cols]).astype(BF)
        dact[1, :, cols] = (dh * factors[1, :, cols]).astype(BF)


def back_step(dact, weights, *rest):
    outs, mark, buf, sem = rest[-7:-3], *rest[-3:]
    n, step, inner = buf.shape[0], buf.shape[1], dact.shape[2]
    copies = fetch([(weights.at[pl.ds(i * step, step), :], buf.at[i]) for i in range(n)], sem)
    mark[...] = jnp.zeros_like(mark)
    for i in range(n):
        copies[i].wait()
        got = wide_dot(dact[0], buf[i, :, :inner]) + wide_dot(dact[1], buf[i, :, inner:])
        for k in range(4):
            outs[k][:, i * step : i * step + step] = got[k * CAP : k * CAP + CAP].astype(BF)


def tok_step(mask, a0, a1, a2, a3, out, mark, whole, sem):
    mark[...] = jnp.zeros_like(mark)
    pieces = (a0, a1, a2, a3)
    land([(a, whole.at[pl.ds(k * CAP, CAP), :]) for k, a in enumerate(pieces)], sem)
    out[...] = jnp.dot(mask[...], whole[...], preferred_element_type=F32).astype(BF)


def tile_step(*refs):
    xs, ds = refs[:4], refs[4:8]
    out, mark, xall, dall, buf, sem, osem = refs[-7:]
    rows = xs[0].shape[0]
    part = [pl.ds(p * rows, rows) for p in range(4)]
    inner = ds[0].shape[2]
    land(
        [(xs[p], xall.at[part[p], :]) for p in range(4)]
        + [
            (ds[p].at[h], dall.at[part[p], pl.ds(h * inner, inner)])
            for p in range(4)
            for h in range(2)
        ],
        sem,
    )
    mark[...] = jnp.zeros_like(mark)
    copies = []
    for b in range(2):
        got = rows_dot(xall[:, b * 512 : b * 512 + 512], dall[...])
        for j in range(4):
            buf[j, b * 128 : b * 128 + 128, :] = got[j * 128 : j * 128 + 128].astype(BF)
            if b == 1:
                copies.append(pltpu.make_async_copy(buf.at[j], out.at[j], osem.at[j]))
                copies[-1].start()
    for copy in copies:
        copy.wait()


def tile_call(xs, ds, after):
    rows, part = xs[0].shape
    wide = 2 * ds[0].shape[2]
    return call(
        tile_step,
        "a" * (8 + len(after)),
        [shape(4, 256, wide), MARK],
        [
            pltpu.VMEM((4 * rows, part), BF),
            pltpu.VMEM((4 * rows, wide), BF),
            pltpu.VMEM((4, 256, wide), BF),
            sems(12),
            sems(4),
        ],
        flops=8 * rows * part * wide,
        moved=8 * rows * (part + wide),
        limit=24,
        placed=(0,),
    )(*xs, *ds, *after)


def down_step(at, both, *rest):
    outs, mark, gall, hall, total, sem = rest[-9:-5], *rest[-5:]
    rows, part, inner = both.shape[1], gall.shape[1], hall.shape[1]
    pairs = []
    for i in range(4):
        pairs.append((both.at[i, :, pl.ds(0, part)], gall.at[pl.ds(i * rows, rows), :]))
        pairs.append((both.at[i, :, pl.ds(part, inner)], hall.at[pl.ds(i * rows, rows), :]))
    land(pairs, sem)
    mark[...] = jnp.zeros_like(mark)
    for b in range(2):
        cols = slice(b * inner // 2, (b + 1) * inner // 2)
        total[cols, :] = rows_dot(hall[:, cols], gall[...])
    for j in (1, 2, 3, 0):
        other = lax.rem(at[1] + j, 4)
        for b in range(2):
            outs[j][b * 96 : b * 96 + 96, :] = total[aligned(b * 4 + other, 96), :].astype(
                outs[j].dtype
            )


def gate_sum(at, parts, keep, send, mark, g, sem):
    mark[...] = jnp.zeros_like(mark)
    half = keep.shape[0]
    copies = fetch([(parts.at[i], g.at[i]) for i in range(4)], sem)
    for copy in copies:
        copy.wait()

    def part(i):
        return sum(g[p, aligned(i, half), :].astype(F32) for p in range(4))

    send[...] = part(1 - at[0]).astype(BF)
    keep[...] = part(at[0])


def sum_step(at, own, r1, r2, r3, *rest):
    keep, send, f, g, sem = rest[-5:]
    half = keep.shape[0]
    land([(own, f), (r1, g.at[0]), (r2, g.at[1]), (r3, g.at[2])], sem)

    def part(i):
        rows = aligned(i, half)
        return f[rows, :] + sum(g[p, rows, :].astype(F32) for p in range(3))

    send[...] = part(1 - at[0]).astype(BF)
    keep[...] = part(at[0])


def sum_call(at, parts, after):
    rows, cols = parts[0].shape
    return call(
        sum_step,
        "saaaa" + "a" * len(after),
        [shape(rows // 2, cols, dtype=F32), shape(rows // 2, cols)],
        [pltpu.VMEM((rows, cols), F32), pltpu.VMEM((3, rows, cols), BF), sems(4)],
        limit=12,
    )(at, *parts, *after)


def join_step(at, c0, c1, c2, c3, mark, out):
    for j, piece in enumerate((c0, c1, c2, c3)):
        out[:, aligned(lax.rem(at[2] + 4 - j, 4), piece.shape[1])] = piece[...]


def shards(tokens, cotangent, routes, gates, gate_up, down_proj):
    gate_up = pltpu.with_memory_space_constraint(gate_up[0], pltpu.HBM)
    down_proj = pltpu.with_memory_space_constraint(down_proj[0], pltpu.HBM)
    w, x, y = lax.axis_index("w"), lax.axis_index("x"), lax.axis_index("y")
    me = lax.axis_index(("v", "c"))
    at = jnp.stack([w, x, y, me]).astype(jnp.int32)
    toks, width = tokens.shape
    inner = down_proj.shape[0]
    rows, part = 4 * CAP, width // 4
    experts = jnp.bitwise_xor(me, jnp.arange(4, dtype=jnp.int32))
    matches = routes[:, :, None] == experts[None, None, :]
    member = jnp.any(matches, axis=1)
    weight = jnp.sum(jnp.where(matches, gates[:, :, None], F32(0.0)), axis=1)
    position = jnp.cumsum(member.astype(jnp.int32), axis=0) - 1
    select = member[:, :, None] & (
        position[:, :, None] == jnp.arange(CAP, dtype=jnp.int32)[None, None, :]
    )
    mask = select.astype(BF).reshape(toks, rows)
    slot_gate = jnp.sum(jnp.where(select, weight[:, :, None], F32(0.0)), axis=0).reshape(rows, 1)
    send_x = rows_dot(mask, tokens).astype(BF).reshape(4, CAP, width)
    send_g = (rows_dot(mask, cotangent) * slot_gate).astype(BF).reshape(4, CAP, width)
    xs = [send_x[0]] + [swap_expert(send_x[k], k) for k in (1, 2, 3)]
    gs = [send_g[0]] + [swap_expert(send_g[k], k) for k in (1, 2, 3)]

    packed = call(
        pack_x, "svvvv", [shape(rows, part)] * 4 + [shape(rows, width)], moved=4 * rows * width
    )(at, *xs)
    xa = [shift(packed[j], "x", j) for j in range(4)]
    n = 2 * inner // 256
    hidden, slope, silu = call(
        act_step,
        "va",
        [shape(rows, inner), shape(rows, inner, dtype=F32), shape(rows, inner, dtype=F32)],
        [pltpu.VMEM((n, width, 256), BF), sems(n)],
        flops=4 * rows * width * inner,
        moved=4 * width * inner,
        limit=18,
    )(packed[4], gate_up)
    n = inner // 256
    dact, mark = call(
        dh_step,
        "aaaaaaa",
        [shape(2, rows, inner), MARK],
        [
            pltpu.VMEM((rows, width), BF),
            pltpu.VMEM((2, rows, inner), F32),
            pltpu.VMEM((n, 256, width), BF),
            sems(n),
            sems(6),
        ],
        flops=2 * rows * width * inner,
        moved=2 * width * inner,
        limit=14,
    )(*gs, slope, silu, down_proj)
    da = [shift(dact, "x", j) for j in range(4)]
    sent, sent_mark = call(
        pack_g,
        "aaaaaaaaa",
        [shape(4, rows, part + inner), MARK],
        [sems(20)],
        moved=4 * rows * width,
        placed=(0,),
    )(*gs, hidden, *xa[1:], mark)
    both = lax.all_to_all(sent, "y", split_axis=0, concat_axis=0, tiled=True)
    n = width // 512
    *back, back_mark = call(
        back_step,
        "vaa",
        [shape(CAP, width)] * 4 + [MARK],
        [pltpu.VMEM((n, 512, 2 * inner), BF), sems(n)],
        flops=4 * rows * width * inner,
        moved=4 * width * inner,
        limit=18,
    )(dact, gate_up, sent_mark)
    arrived = [back[0]] + [swap_expert(back[k], k) for k in (1, 2, 3)]
    parts, mark = tile_call(xa, da, [arrived[2]])
    gate = lax.all_to_all(parts, "y", split_axis=0, concat_axis=0, tiled=True)
    *parts, _ = call(
        down_step,
        "saa",
        [shape(192, part, dtype=F32)] + [shape(192, part)] * 3 + [MARK],
        [
            pltpu.VMEM((4 * rows, part), BF),
            pltpu.VMEM((4 * rows, inner), BF),
            pltpu.VMEM((inner, part), F32),
            sems(8),
        ],
        flops=8 * rows * part * inner,
        moved=8 * rows * (part + inner),
        limit=16,
    )(at, both, mark)
    down = [parts[0]] + [shift(parts[j], "x", j) for j in (1, 2, 3)]
    token_grad, tok_mark = call(
        tok_step,
        "vaaaa",
        [shape(toks, width), MARK],
        [pltpu.VMEM((rows, width), BF), sems(4)],
    )(mask, *arrived)

    gate_keep, gate_send, mark = call(
        gate_sum,
        "sa",
        [shape(128, 2 * inner, dtype=F32), shape(128, 2 * inner), MARK],
        [pltpu.VMEM((4, 256, 2 * inner), BF), sems(4)],
        limit=12,
    )(at, gate)
    gate_up_grad = (gate_keep + swap_w(gate_send).astype(F32)).astype(BF)
    keep, send = sum_call(at, down, [tok_mark])
    down_grad = (keep + swap_w(send).astype(F32)).astype(BF).reshape(4, 24, part)
    cols = [
        shift(lax.dynamic_index_in_dim(down_grad, (y + j) % 4, 0, False), "y", j) for j in range(4)
    ]
    down_grad = call(join_step, "svvvva", [shape(24, width)])(at, *cols, mark)[0]

    return token_grad, gate_up_grad[None], down_grad[None]


def solution(mesh):
    fine = Mesh(mesh.devices.reshape(2, 4, 4, 2, 2), AXES)
    rows, expert, dp = P(AXES, None), ("v", "c"), ("w", "x", "y")
    in_specs = (rows, rows, rows, rows, P(expert, None, None), P(expert, None, None))
    out_specs = (rows, P(expert, dp, None), P(expert, dp, None))
    return jax.shard_map(
        shards, mesh=fine, in_specs=in_specs, out_specs=out_specs, check_vma=False
    )
```
